32 devices in a mesh: pb: 4 (over y, x), db: 8 (over z, core).
Axes of the slice: x: 2, y: 2, z: 4, core: 2. Of those that a mesh axis runs over, the one named last changes fastest.
Arguments:
- database: bfloat16 [2048, 768], P('db')
- neighbours: int32 [2048, 16], P('db'), may hold values from 0 to 2047, as said below
- valid_count: int32 [2048], P('db'), may hold values from 9 to 16, as said below
- queries: bfloat16 [65536, 768], P('pb'), may hold values from -6 to 6
Outputs:
- augmented: bfloat16 [2048, 768], P('db')
- best_score: float32 [65536], P('pb')
The draws below stay inside these ranges and needn't reach their ends.
Inputs may be any that keep to these rules, and one draw needn't show every extreme that they name: `neighbours`: every entry is a row number of the whole database, also in slots at or past valid_count (those carry no weight). The owner of row r is r // 256. In each aligned block of 64 rows, at most 256 of its 1024 entries name rows of one owner, and in every block some owner is named by exactly 256 entries. `valid_count`: every aligned block of 64 rows holds a row with 16 valid slots.
All inputs are finite; a program needn't handle non-finite values.
Results may differ from the reference program's by a relative error of at most 0.0028.
Values may be sent and summed in bfloat16 or wider, within the bound.
No kernel may reach another device: no remote copies, remote signals or barrier semaphores. Data moves between devices by JAX's collectives and lax.ppermute only.
A program may use at most 128 MiB of HBM per device.

```python
import math
import jax
import jax.numpy as jnp
from jax import lax

D = 768
K = 16
ROW_DEV = 256
QROWS = 64
OWNERS = 8
CAP = 256
ROWS = 2048
QUERIES = 65536


def draw_database(key, part):
    key = jax.random.fold_in(key, 1)
    key_main, key_rows, key_cols = jax.random.split(key, 3)
    row_scale = jnp.exp(jax.random.uniform(key_rows, (ROWS, 1), jnp.float32, 0.0, math.log(10.0)))
    col_scale = jnp.exp(jax.random.uniform(key_cols, (1, D), jnp.float32, 0.0, math.log(10.0)))
    values = jax.random.normal(key_main, (ROWS, D), jnp.float32) * row_scale * col_scale / 3.0
    return values.astype(jnp.bfloat16)


def owner_block(block_key):
    key_rank, key_spread, key_order, key_local = jax.random.split(block_key, 4)
    total = K * QROWS
    base_count = (total - CAP) // (OWNERS - 1)
    extra_count = total - CAP - base_count * (OWNERS - 1)
    positions = jnp.arange(OWNERS, dtype=jnp.int32)
    rank_of = jax.random.permutation(key_rank, OWNERS).astype(jnp.int32)
    spread = jax.random.randint(key_spread, (OWNERS,), 0, base_count // 2 + 1, dtype=jnp.int32)
    next_rank = jnp.where(positions < OWNERS - 1, positions + 1, 1)
    change = spread[rank_of] - spread[next_rank[rank_of]]
    drawn = base_count + (rank_of <= extra_count).astype(jnp.int32) + change
    counts = jnp.where(rank_of == 0, CAP, drawn)
    ends = jnp.cumsum(counts)
    slots = jnp.arange(total, dtype=jnp.int32)
    owner_of = jnp.sum((slots[:, None] >= ends[None, :]).astype(jnp.int32), axis=1)
    order = jax.random.permutation(key_order, total)
    owner_of = owner_of[order]
    local_row = jax.random.randint(key_local, (total,), 0, ROW_DEV, dtype=jnp.int32)
    return (owner_of * ROW_DEV + local_row).reshape(QROWS, K)


def draw_neighbours(key, part):
    key = jax.random.fold_in(key, 2)
    block_keys = jax.random.split(key, ROWS // QROWS)
    return jax.vmap(owner_block)(block_keys).reshape(ROWS, K)


def draw_valid_count(key, part):
    key = jax.random.fold_in(key, 3)
    key_counts, key_place = jax.random.split(key, 2)
    counts = jax.random.randint(key_counts, (ROWS // QROWS, QROWS), K // 2 + 1, K + 1, dtype=jnp.int32)
    place = jax.random.randint(key_place, (ROWS // QROWS, 1), 0, QROWS, dtype=jnp.int32)
    counts = jnp.where(jnp.arange(QROWS, dtype=jnp.int32)[None, :] == place, K, counts)
    return counts.reshape(ROWS)


def steps_of(stream_key, shape, shards, smallest, high):
    gain, own = 1.0, jax.random.fold_in(stream_key, 6)
    for axis_at, shards_of in shards:
        steps = jnp.exp(jax.random.uniform(jax.random.fold_in(own, axis_at), (shards_of,), jnp.float32, smallest / len(shards), high / len(shards)))
        gain = gain * jnp.repeat(steps, shape[axis_at] // shards_of).reshape([-1 if axis == axis_at else 1 for axis in range(len(shape))])
    return gain


def normal_values(own_key, dims, scale, reach, cuts=(), kind=jnp.bfloat16):
    result = scale * jax.random.normal(own_key, dims, jnp.float32)
    if cuts:
        result = result * steps_of(own_key, dims, cuts, -0.22, 0.18)
    return jnp.clip(result, -reach, reach).astype(kind)


def setup_inputs(seed: int = 0) -> dict:
    arg_keys = jax.random.split(jax.random.key(seed), 5)
    database = draw_database(jax.random.fold_in(arg_keys[4], 71), 0)
    neighbours = draw_neighbours(jax.random.fold_in(arg_keys[4], 71), 0)
    valid_count = draw_valid_count(jax.random.fold_in(arg_keys[4], 71), 0)
    queries = normal_values(arg_keys[3], (QUERIES, D), 1.0, 6.0, ((0, 4),))
    return {"database": database, "neighbours": neighbours, "valid_count": valid_count, "queries": queries}


epsilon = 1e-06

def inverse_norms(values):
    squares = lax.optimization_barrier(jnp.sum(values * values, axis=-1))
    return lax.rsqrt(squares + epsilon)

def augment_rows(own_rows, fetched, valid_here):
    own_float = own_rows.astype(jnp.float32)
    fetched_float = fetched.astype(jnp.float32)
    own_inverse = inverse_norms(own_float)
    far_inverse = inverse_norms(fetched_float)
    cosine = jnp.einsum('rd,rkd->rk', own_float, fetched_float) * own_inverse[:, None] * far_inverse
    halfway = (1.0 + cosine) * 0.5
    mask_on = jnp.arange(fetched.shape[1], dtype=jnp.int32)[None, :] < valid_here[:, None]
    weight = jnp.where(mask_on, halfway * halfway * halfway, jnp.zeros_like(halfway))
    coefficient = (weight * far_inverse).astype(jnp.bfloat16)
    summed = own_float * own_inverse[:, None] + jnp.einsum('rk,rkd->rd', coefficient.astype(jnp.float32), fetched_float)
    return (summed * inverse_norms(summed)[:, None]).astype(jnp.bfloat16)

def reference(database, neighbours, valid_count, queries):

    def one_shard(shard_index):
        first_row = shard_index * ROW_DEV
        own_rows = lax.dynamic_slice_in_dim(database, first_row, ROW_DEV, 0)
        wanted_ids = lax.dynamic_slice_in_dim(neighbours, first_row, ROW_DEV, 0)
        valid_here = lax.dynamic_slice_in_dim(valid_count, first_row, ROW_DEV, 0)
        fetched = database[wanted_ids]
        return augment_rows(own_rows, fetched, valid_here)
    shard_list = jnp.arange(OWNERS, dtype=jnp.int32)
    augmented = lax.map(one_shard, shard_list).reshape(ROWS, D)

    def best_of(shard_index):
        block_rows = lax.dynamic_slice_in_dim(augmented, shard_index * ROW_DEV, ROW_DEV, 0)
        scores = jnp.dot(queries, block_rows.T, preferred_element_type=jnp.float32)
        return lax.optimization_barrier(jnp.max(scores, axis=1))
    best_score = lax.optimization_barrier(jnp.max(lax.map(best_of, shard_list), axis=0))
    return (augmented, best_score)
```

```python
import functools

import jax
import jax.numpy as jnp
from jax import lax
from jax.experimental import pallas as pl
from jax.experimental.pallas import tpu as pltpu
from jax.sharding import PartitionSpec as P

epsilon = 1e-06
MIB = 1 << 20


def column_inverse(values):
    squares = jnp.sum(values * values, axis=-1, keepdims=True)
    return lax.rsqrt(squares + epsilon)


def as_row(column):
    wide = jnp.broadcast_to(column, (column.shape[0], 128))
    return wide.T[0:1, :]


def count_kernel(ids_ref, wanted_a_ref, wanted_b_ref, count_a_ref, count_b_ref):
    fanout = wanted_a_ref.shape[1]
    rows, pool = count_a_ref.shape
    width = min(pool, 512)
    step = 16
    for wanted_ref, count_ref in ((wanted_a_ref, count_a_ref), (wanted_b_ref, count_b_ref)):

        @pl.loop(0, rows // step)
        def _(at):
            lines = pl.ds(pl.multiple_of(at * step, step), step)
            wanted = wanted_ref[lines, :]
            columns = [jnp.broadcast_to(wanted[:, k : k + 1], (step, 128)) for k in range(fanout)]
            for first in range(0, pool, 128):
                ids = jnp.broadcast_to(ids_ref[:, first : first + 128], (step, 128))
                total = jnp.zeros((step, 128), jnp.float32)
                for column in columns:
                    total = total + jnp.where(column == ids, 1.0, 0.0)
                count_ref[lines, first : first + 128] = total.astype(jnp.bfloat16)


def partial_kernel(groups, dest_ref, count_ref, *rest):
    out_ref = rest[-1]
    chunks = rest[:-1]
    dest = dest_ref[...]
    dest_inverse = column_inverse(dest.astype(jnp.float32))
    at = 0
    first = 0
    total = None
    for parts in groups:
        block = [chunks[at + i][...] for i in range(parts)]
        at += parts
        block = block[0] if parts == 1 else jnp.concatenate(block, axis=0)
        height = block.shape[0]
        far = as_row(column_inverse(block.astype(jnp.float32)))
        products = lax.dot_general(
            dest, block, (((1,), (1,)), ((), ())), preferred_element_type=jnp.float32
        )
        cosine = products * dest_inverse * far
        halfway = (1.0 + cosine) * 0.5
        weight = halfway * halfway * halfway
        coefficient = (weight * far).astype(jnp.bfloat16).astype(jnp.float32)
        spread = coefficient * count_ref[:, first : first + height].astype(jnp.float32)
        first += height
        high = spread.astype(jnp.bfloat16)
        low = (spread - high.astype(jnp.float32)).astype(jnp.bfloat16)
        term = jnp.dot(high, block, preferred_element_type=jnp.float32)
        term = term + jnp.dot(low, block, preferred_element_type=jnp.float32)
        total = term if total is None else total + term
    out_ref[...] = total


def score_kernel(own_ref, here_ref, there_ref, queries_ref, augmented_ref, best_ref):
    @pl.when(pl.program_id(0) == 0)
    def _():
        own = own_ref[...].astype(jnp.float32)
        summed = own * column_inverse(own) + (here_ref[...] + there_ref[...])
        augmented_ref[...] = (summed * column_inverse(summed)).astype(jnp.bfloat16)

    scores = lax.dot_general(
        augmented_ref[...],
        queries_ref[...],
        (((1,), (1,)), ((), ())),
        preferred_element_type=jnp.float32,
    )
    best = jnp.max(scores, axis=0, keepdims=True)
    for line in range(best_ref.shape[0]):
        best_ref[line : line + 1, :] = best[:, line * 128 : (line + 1) * 128]


def local(database, neighbours, valid_count, queries):
    rows, features = database.shape
    fanout = neighbours.shape[1]
    count = queries.shape[0]
    owners = lax.axis_size("db")
    panels = lax.axis_size("pb")
    assert panels == 4 and owners % 2 == 0
    planes = owners // 2
    quarter = rows // panels
    me = lax.axis_index("pb")
    owner = lax.axis_index("db")
    plane, core = owner // 2, owner % 2

    def shift(value, steps):
        pairs = [(i, (i + 2 * steps) % owners) for i in range(owners)]
        return lax.ppermute(value, "db", pairs)

    def swap(value):
        return lax.ppermute(value, "db", [(i, i ^ 1) for i in range(owners)])

    def cross(value, bits):
        return lax.ppermute(value, "pb", [(i, i ^ bits) for i in range(panels)])

    mine = lax.dynamic_slice_in_dim(database, me * quarter, quarter, 0)
    other = lax.dynamic_slice_in_dim(database, (me ^ 3) * quarter, quarter, 0)
    near = [shift(mine, s) for s in range(1, planes)]
    far = [shift(other, s) for s in range(1, planes)]
    beside = [cross(piece, 1) for piece in near]
    behind = [cross(piece, 2) for piece in near]

    slots = jnp.arange(fanout, dtype=jnp.int32)[None, :]
    wanted = jnp.where(slots < valid_count[:, None], neighbours, -1)
    twin_wanted = swap(wanted)
    twin = swap(database)

    order = jnp.stack([me, me ^ 3, me ^ 1, me ^ 2])
    inner = (order[:, None] * quarter + jnp.arange(quarter, dtype=jnp.int32)[None, :]).reshape(-1)
    ids = [owner * rows + jnp.arange(rows, dtype=jnp.int32)]
    for s in range(1, planes):
        source = ((plane - s + planes) % planes) * 2 + core
        ids.append(source * rows + inner)
    ids = jnp.concatenate(ids).reshape(1, -1)
    pool = planes * rows

    vmem = pl.BlockSpec(memory_space=pltpu.VMEM)
    twin_count, own_count = pl.pallas_call(
        count_kernel,
        out_shape=[jax.ShapeDtypeStruct((rows, pool), jnp.bfloat16)] * 2,
        in_specs=[vmem] * 3,
        out_specs=[vmem] * 2,
        compiler_params=pltpu.CompilerParams(vmem_limit_bytes=16 * MIB),
        name="counts",
    )(ids, twin_wanted, wanted)

    pieces = [database]
    groups = (1,)
    for s in range(planes - 1):
        pieces += [near[s], far[s], beside[s], behind[s]]
        groups += (4,)

    def partial(dest, counts):
        return pl.pallas_call(
            functools.partial(partial_kernel, groups),
            out_shape=jax.ShapeDtypeStruct((rows, features), jnp.float32),
            in_specs=[vmem] * (2 + len(pieces)),
            out_specs=vmem,
            compiler_params=pltpu.CompilerParams(vmem_limit_bytes=32 * MIB),
            cost_estimate=pl.CostEstimate(
                flops=6 * rows * pool * features, bytes_accessed=2 * pool * features, transcendentals=0
            ),
            name="partial_sums",
        )(dest, counts, *pieces)

    there = swap(partial(twin, twin_count))
    here = partial(database, own_count)

    tile = min(1024, count)
    whole = lambda shape: pl.BlockSpec(shape, lambda i: (0, 0))
    augmented, best = pl.pallas_call(
        score_kernel,
        grid=(count // tile,),
        out_shape=[
            jax.ShapeDtypeStruct((rows, features), jnp.bfloat16),
            jax.ShapeDtypeStruct((count // 128, 128), jnp.float32),
        ],
        in_specs=[
            whole((rows, features)),
            whole((rows, features)),
            whole((rows, features)),
            pl.BlockSpec((tile, features), lambda i: (i, 0)),
        ],
        out_specs=[whole((rows, features)), pl.BlockSpec((tile // 128, 128), lambda i: (i, 0))],
        compiler_params=pltpu.CompilerParams(vmem_limit_bytes=32 * MIB),
        cost_estimate=pl.CostEstimate(
            flops=2 * count * rows * features, bytes_accessed=2 * count * features, transcendentals=0
        ),
        name="scores",
    )(database, here, there, queries)

    best = jnp.maximum(best, swap(best))
    received = [shift(best, s) for s in range(1, planes)]
    for value in received:
        best = jnp.maximum(best, value)
    return augmented, best.reshape(count)


def solution(mesh):
    return jax.shard_map(
        local,
        mesh=mesh,
        in_specs=(P("db", None), P("db", None), P("db"), P("pb", None)),
        out_specs=(P("db", None), P("pb")),
        check_vma=False,
    )
```

```python
import functools

import jax
import jax.numpy as jnp
from jax import lax
from jax.experimental import pallas as pl
from jax.experimental.pallas import tpu as pltpu
from jax.sharding import PartitionSpec as P

epsilon = 1e-06
MIB = 1 << 20


def column_inverse(values):
    squares = jnp.sum(values * values, axis=-1, keepdims=True)
    return lax.rsqrt(squares + epsilon)


def as_row(column):
    wide = jnp.broadcast_to(column, (column.shape[0], 128))
    return wide.T[0:1, :]


def count_kernel(rows, early_ids_ref, late_ids_ref, twin_ref, own_ref, early_ref, late_ref):
    fanout = own_ref.shape[1]
    step = 16
    for number, wanted_ref in enumerate((twin_ref, own_ref)):

        @pl.loop(0, rows // step)
        def _(at):
            start = pl.multiple_of(at * step, step)
            wanted = wanted_ref[pl.ds(start, step), :]
            columns = [jnp.broadcast_to(wanted[:, k : k + 1], (step, 128)) for k in range(fanout)]
            for ids_ref, count_ref in ((early_ids_ref, early_ref), (late_ids_ref, late_ref)):
                pool = count_ref.shape[1]
                for first in range(0, pool, 128):
                    width = min(128, pool - first)
                    ids = jnp.broadcast_to(ids_ref[:, first : first + width], (step, width))
                    total = jnp.zeros((step, width), jnp.float32)
                    for column in columns:
                        total = total + jnp.where(column[:, :width] == ids, 1.0, 0.0)
                    count_ref[pl.ds(number * rows + start, step), first : first + width] = total.astype(
                        jnp.bfloat16
                    )


def spread_terms(dest, dest_inverse, block, far, counts):
    products = lax.dot_general(
        dest, block, (((1,), (1,)), ((), ())), preferred_element_type=jnp.float32
    )
    cosine = products * dest_inverse * far
    halfway = (1.0 + cosine) * 0.5
    weight = halfway * halfway * halfway
    coefficient = (weight * far).astype(jnp.bfloat16).astype(jnp.float32)
    spread = coefficient * counts.astype(jnp.float32)
    high = spread.astype(jnp.bfloat16)
    low = (spread - high.astype(jnp.float32)).astype(jnp.bfloat16)
    return jnp.dot(high, block, preferred_element_type=jnp.float32) + jnp.dot(
        low, block, preferred_element_type=jnp.float32
    )


def early_kernel(twin_ref, own_ref, near_ref, counts_ref, out_ref):
    rows = own_ref.shape[0]
    block = jnp.concatenate([own_ref[...], near_ref[...]], axis=0)
    far = as_row(column_inverse(block.astype(jnp.float32)))
    for number, dest_ref in enumerate((twin_ref, own_ref)):
        lines = slice(number * rows, (number + 1) * rows)
        dest = dest_ref[...]
        dest_inverse = column_inverse(dest.astype(jnp.float32))
        out_ref[lines, :] = spread_terms(dest, dest_inverse, block, far, counts_ref[lines, :])


def late_kernel(number, dest_ref, early_ref, counts_ref, *rest):
    out_ref = rest[-1]
    rows = dest_ref.shape[0]
    lines = slice(number * rows, (number + 1) * rows)
    block = jnp.concatenate([ref[...] for ref in rest[:-1]], axis=0)
    far = as_row(column_inverse(block.astype(jnp.float32)))
    dest = dest_ref[...]
    dest_inverse = column_inverse(dest.astype(jnp.float32))
    terms = spread_terms(dest, dest_inverse, block, far, counts_ref[lines, :])
    out_ref[...] = early_ref[lines, :] + terms


def score_kernel(own_ref, here_ref, there_ref, queries_ref, augmented_ref, best_ref, turned_ref):
    @pl.when(pl.program_id(0) == 0)
    def _():
        own = own_ref[...].astype(jnp.float32)
        summed = own * column_inverse(own) + (here_ref[...] + there_ref[...])
        augmented = (summed * column_inverse(summed)).astype(jnp.bfloat16)
        augmented_ref[...] = augmented
        turned_ref[...] = augmented.T

    tile = queries_ref.shape[0]
    step = 512
    turned = turned_ref[...]
    for first in range(0, tile, step):
        scores = jnp.dot(
            queries_ref[first : first + step, :], turned, preferred_element_type=jnp.float32
        )
        widest = scores[:, :128]
        for at in range(128, scores.shape[1], 128):
            widest = jnp.maximum(widest, scores[:, at : at + 128])
        for at in range(0, step, 128):
            best = jnp.max(widest[at : at + 128, :].T, axis=0, keepdims=True)
            line = (first + at) // 128
            best_ref[line : line + 1, :] = best


def local(database, neighbours, valid_count, queries):
    rows, features = database.shape
    fanout = neighbours.shape[1]
    count = queries.shape[0]
    owners = lax.axis_size("db")
    panels = lax.axis_size("pb")
    assert panels == 4 and owners % 2 == 0
    planes = owners // 2
    quarter = rows // panels
    me = lax.axis_index("pb")
    owner = lax.axis_index("db")
    plane, core = owner // 2, owner % 2

    def shift(value, steps):
        pairs = [(i, (i + 2 * steps) % owners) for i in range(owners)]
        return lax.ppermute(value, "db", pairs)

    def swap(value):
        return lax.ppermute(value, "db", [(i, i ^ 1) for i in range(owners)])

    def cross(value, bits):
        pairs = []
        for panel in range(panels):
            for i in range(owners):
                pairs.append((panel * owners + i, (panel ^ bits[i % 2]) * owners + i))
        return lax.ppermute(value, ("pb", "db"), pairs)

    mine = lax.dynamic_slice_in_dim(database, me * quarter, quarter, 0)
    other = lax.dynamic_slice_in_dim(database, (me ^ 3) * quarter, quarter, 0)
    steps = range(1, planes)
    near = jnp.concatenate([shift(mine, s) for s in steps], axis=0)
    across = [shift(other, s) for s in steps]
    beside = cross(near, (1, 2))
    behind = cross(near, (2, 1))

    slots = jnp.arange(fanout, dtype=jnp.int32)[None, :]
    wanted = jnp.where(slots < valid_count[:, None], neighbours, -1)
    twin_wanted = swap(wanted)
    twin = swap(database)

    inner = jnp.arange(quarter, dtype=jnp.int32)[None, :]
    sources = jnp.stack([(((plane - s + planes) % planes) * 2 + core) * rows for s in steps])
    ids_of = lambda panel: (sources[:, None] + panel * quarter + inner).reshape(1, -1)
    own_ids = (owner * rows + jnp.arange(rows, dtype=jnp.int32)).reshape(1, -1)
    early_ids = jnp.concatenate([own_ids, ids_of(me)], axis=1)
    late_ids = jnp.concatenate([ids_of(me ^ 3), ids_of(me ^ (1 + core)), ids_of(me ^ (2 - core))], axis=1)

    vmem = pl.BlockSpec(memory_space=pltpu.VMEM)
    early_counts, late_counts = pl.pallas_call(
        functools.partial(count_kernel, rows),
        out_shape=[
            jax.ShapeDtypeStruct((2 * rows, early_ids.shape[1]), jnp.bfloat16),
            jax.ShapeDtypeStruct((2 * rows, late_ids.shape[1]), jnp.bfloat16),
        ],
        in_specs=[vmem] * 4,
        out_specs=[vmem] * 2,
        compiler_params=pltpu.CompilerParams(vmem_limit_bytes=16 * MIB),
        name="counts",
    )(early_ids, late_ids, twin_wanted, wanted)

    early = pl.pallas_call(
        early_kernel,
        out_shape=jax.ShapeDtypeStruct((2 * rows, features), jnp.float32),
        in_specs=[vmem] * 4,
        out_specs=vmem,
        compiler_params=pltpu.CompilerParams(vmem_limit_bytes=32 * MIB),
        name="early_sums",
    )(twin, database, near, early_counts)

    def late(number, dest):
        return pl.pallas_call(
            functools.partial(late_kernel, number),
            out_shape=jax.ShapeDtypeStruct((rows, features), jnp.float32),
            in_specs=[vmem] * (5 + len(across)),
            out_specs=vmem,
            compiler_params=pltpu.CompilerParams(vmem_limit_bytes=40 * MIB),
            name="late_sums",
        )(dest, early, late_counts, *across, beside, behind)

    there = swap(late(0, twin))
    here = late(1, database)

    tile = min(2048, count)
    whole = lambda shape: pl.BlockSpec(shape, lambda i: (0, 0))
    augmented, best = pl.pallas_call(
        score_kernel,
        grid=(count // tile,),
        out_shape=[
            jax.ShapeDtypeStruct((rows, features), jnp.bfloat16),
            jax.ShapeDtypeStruct((count // 128, 128), jnp.float32),
        ],
        in_specs=[
            whole((rows, features)),
            whole((rows, features)),
            whole((rows, features)),
            pl.BlockSpec((tile, features), lambda i: (i, 0)),
        ],
        out_specs=[whole((rows, features)), pl.BlockSpec((tile // 128, 128), lambda i: (i, 0))],
        scratch_shapes=[pltpu.VMEM((features, rows), jnp.bfloat16)],
        compiler_params=pltpu.CompilerParams(vmem_limit_bytes=32 * MIB),
        cost_estimate=pl.CostEstimate(
            flops=2 * count * rows * features, bytes_accessed=2 * count * features, transcendentals=0
        ),
        name="scores",
    )(database, here, there, queries)

    best = jnp.maximum(best, swap(best))
    received = [shift(best, s) for s in steps]
    for value in received:
        best = jnp.maximum(best, value)
    return augmented, best.reshape(count)


def solution(mesh):
    return jax.shard_map(
        local,
        mesh=mesh,
        in_specs=(P("db", None), P("db", None), P("db"), P("pb", None)),
        out_specs=(P("db", None), P("pb")),
        check_vma=False,
    )
```

```python
import functools

import jax
import jax.numpy as jnp
from jax import lax
from jax.experimental import pallas as pl
from jax.experimental.pallas import tpu as pltpu
from jax.sharding import PartitionSpec as P

epsilon = 1e-06
MIB = 1 << 20


def column_inverse(values):
    squares = jnp.sum(values * values, axis=-1, keepdims=True)
    return lax.rsqrt(squares + epsilon)


def as_row(column):
    wide = jnp.broadcast_to(column, (column.shape[0], 128))
    return wide.T[0:1, :]


def count_kernel(planes, place_ref, twin_ref, own_ref, database_ref, early_ref, late_ref, copy_ref, tiles_ref, lows_ref, sem):
    rows = copy_ref.shape[0]
    fanout = own_ref.shape[0] * 128 // rows
    quarter = rows // 4
    span = (planes - 1) * quarter
    early_tiles = early_ref.shape[1] // 128
    late_tiles = late_ref.shape[1] // 128
    copy = pltpu.make_async_copy(database_ref, copy_ref, sem)
    copy.start()
    me, plane, core = place_ref[0], place_ref[1], place_ref[2]
    bits = rows.bit_length() - 1
    lines = own_ref.shape[0]
    for number, wanted_ref in enumerate((twin_ref, own_ref)):
        wanted = wanted_ref[...]
        owner = wanted >> bits
        row = wanted & (rows - 1)
        cross = (row >> (bits - 2)) ^ me
        inner = row & (quarter - 1)
        away = plane - (owner >> 1)
        away = jnp.where(away < 0, away + planes, away)
        behind = (away - 1) * quarter + inner
        section = jnp.where(cross == 3, 0, jnp.where(cross == 1 + core, span, 2 * span))
        position = jnp.where(cross == 0, rows + behind, early_tiles * 128 + section + behind)
        position = jnp.where(away == 0, row, position)
        position = jnp.where((wanted >= 0) & ((owner & 1) == core), position, -1)
        tiles_ref[number * lines : (number + 1) * lines, :] = position >> 7
        lows_ref[number * lines : (number + 1) * lines, :] = (position & 127).astype(jnp.float32)

    group = 16
    height = (early_tiles + late_tiles) * group
    width = group * fanout
    at_row = lax.broadcasted_iota(jnp.int32, (height, width), 0)
    at_lane = lax.broadcasted_iota(jnp.int32, (height, width), 1)
    target = jnp.where(at_lane // fanout == at_row % group, at_row // group, -2)
    lane = lax.broadcasted_iota(jnp.int32, (128, 128), 1).astype(jnp.float32)
    each = width // 128

    def body(at, carry):
        tile = [tiles_ref[pl.ds(at * each + i, 1), :] for i in range(each)]
        tile = jnp.concatenate(tile, axis=1)
        left = jnp.where(jnp.broadcast_to(tile, (height, width)) == target, 1.0, 0.0).astype(jnp.bfloat16)
        right = []
        for i in range(each):
            low = jnp.broadcast_to(lows_ref[pl.ds(at * each + i, 1), :], (128, 128)).T
            right.append(jnp.where(low == lane, 1.0, 0.0).astype(jnp.bfloat16))
        right = jnp.concatenate(right, axis=0)
        counts = jnp.dot(left, right, preferred_element_type=jnp.float32).astype(jnp.bfloat16)
        start = pl.ds(pl.multiple_of(at * group, group), group)
        for t in range(early_tiles):
            early_ref[start, t * 128 : (t + 1) * 128] = counts[t * group : (t + 1) * group, :]
        for t in range(late_tiles):
            first = (early_tiles + t) * group
            late_ref[start, t * 128 : (t + 1) * 128] = counts[first : first + group, :]
        return carry

    lax.fori_loop(0, 2 * rows // group, body, 0, unroll=4)
    copy.wait()


def spread_terms(dest, dest_inverse, block, far, counts):
    products = lax.dot_general(
        dest, block, (((1,), (1,)), ((), ())), preferred_element_type=jnp.float32
    )
    cosine = products * dest_inverse * far
    halfway = (1.0 + cosine) * 0.5
    weight = halfway * halfway * halfway
    coefficient = (weight * far).astype(jnp.bfloat16).astype(jnp.float32)
    spread = coefficient * counts.astype(jnp.float32)
    high = spread.astype(jnp.bfloat16)
    low = (spread - high.astype(jnp.float32)).astype(jnp.bfloat16)
    return jnp.dot(high, block, preferred_element_type=jnp.float32) + jnp.dot(
        low, block, preferred_element_type=jnp.float32
    )


def early_kernel(twin_ref, own_ref, near_ref, counts_ref, out_ref):
    rows = own_ref.shape[0]
    block = jnp.concatenate([own_ref[...], near_ref[...]], axis=0)
    far = as_row(column_inverse(block.astype(jnp.float32)))
    for number, dest_ref in enumerate((twin_ref, own_ref)):
        lines = slice(number * rows, (number + 1) * rows)
        dest = dest_ref[...]
        dest_inverse = column_inverse(dest.astype(jnp.float32))
        out_ref[lines, :] = spread_terms(dest, dest_inverse, block, far, counts_ref[lines, : block.shape[0]])


def late_kernel(number, dest_ref, early_ref, counts_ref, *rest):
    out_ref = rest[-1]
    rows = dest_ref.shape[0]
    lines = slice(number * rows, (number + 1) * rows)
    block = jnp.concatenate([ref[...] for ref in rest[:-1]], axis=0)
    far = as_row(column_inverse(block.astype(jnp.float32)))
    dest = dest_ref[...]
    dest_inverse = column_inverse(dest.astype(jnp.float32))
    terms = spread_terms(dest, dest_inverse, block, far, counts_ref[lines, : block.shape[0]])
    out_ref[...] = early_ref[lines, :] + terms


def score_kernel(place_ref, own_ref, own_a_ref, own_b_ref, twin_ref, twin_a_ref, twin_b_ref, queries_ref, augmented_ref, best_ref, turned_ref):
    rows = own_ref.shape[0]

    @pl.when(pl.program_id(0) == 0)
    def _():
        parts = ((own_ref, own_a_ref, own_b_ref), (twin_ref, twin_a_ref, twin_b_ref))
        for number, (row_ref, a_ref, b_ref) in enumerate(parts):
            values = row_ref[...].astype(jnp.float32)
            summed = values * column_inverse(values) + (a_ref[...] + b_ref[...])
            augmented = (summed * column_inverse(summed)).astype(jnp.bfloat16)
            if number == 0:
                augmented_ref[...] = augmented
            turned_ref[:, number * rows : (number + 1) * rows] = augmented.T

    tile = queries_ref.shape[0]
    step = min(256, tile)
    turned = turned_ref[...]
    lane = lax.broadcasted_iota(jnp.int32, (step // 128, 16, 8, 128), 3)
    query = lax.broadcasted_iota(jnp.int32, (step // 128, 16, 8, 128), 1) * 8
    query = query + lax.broadcasted_iota(jnp.int32, (step // 128, 16, 8, 128), 2)
    for first in range(0, tile, step):
        scores = jnp.dot(
            queries_ref[first : first + step, :], turned, preferred_element_type=jnp.float32
        )
        widest = scores[:, :128]
        for at in range(128, scores.shape[1], 128):
            widest = jnp.maximum(widest, scores[:, at : at + 128])
        best = jnp.broadcast_to(jnp.max(widest, axis=1, keepdims=True), widest.shape)
        best = jnp.where(lane == query, best.reshape(lane.shape), -jnp.inf)
        best = jnp.max(jnp.max(best, axis=1), axis=1)
        best_ref[first // 128 : (first + step) // 128, :] = best


def local(database, neighbours, valid_count, queries):
    rows, features = database.shape
    fanout = neighbours.shape[1]
    count = queries.shape[0]
    owners = lax.axis_size("db")
    panels = lax.axis_size("pb")
    assert panels == 4 and owners % 2 == 0
    planes = owners // 2
    quarter = rows // panels
    me = lax.axis_index("pb")
    owner = lax.axis_index("db")
    plane, core = owner // 2, owner % 2

    def shift(value, steps):
        pairs = [(i, (i + 2 * steps) % owners) for i in range(owners)]
        return lax.ppermute(value, "db", pairs)

    def swap(value):
        return lax.ppermute(value, "db", [(i, i ^ 1) for i in range(owners)])

    def cross(value, bits):
        pairs = []
        for panel in range(panels):
            for i in range(owners):
                pairs.append((panel * owners + i, (panel ^ bits[i % 2]) * owners + i))
        return lax.ppermute(value, ("pb", "db"), pairs)

    mine = lax.dynamic_slice_in_dim(database, me * quarter, quarter, 0)
    other = lax.dynamic_slice_in_dim(database, (me ^ 3) * quarter, quarter, 0)
    steps = range(1, planes)
    near = jnp.concatenate([shift(mine, s) for s in steps], axis=0)
    across = [shift(other, s) for s in steps]
    beside = cross(near, (1, 2))
    behind = cross(near, (2, 1))

    slots = jnp.arange(fanout, dtype=jnp.int32)[None, :]
    wanted = jnp.where(slots < valid_count[:, None], neighbours, -1).reshape(-1, 128)
    twin_wanted = swap(wanted)
    place = jnp.stack([me, plane, core]).astype(jnp.int32)

    padded = lambda size: (size + 127) // 128 * 128
    span = (planes - 1) * quarter
    vmem = pl.BlockSpec(memory_space=pltpu.VMEM)
    smem = pl.BlockSpec(memory_space=pltpu.SMEM)
    early_counts, late_counts, own = pl.pallas_call(
        functools.partial(count_kernel, planes),
        out_shape=[
            jax.ShapeDtypeStruct((2 * rows, padded(rows + span)), jnp.bfloat16),
            jax.ShapeDtypeStruct((2 * rows, padded(3 * span)), jnp.bfloat16),
            jax.ShapeDtypeStruct((rows, features), jnp.bfloat16),
        ],
        in_specs=[smem, vmem, vmem, pl.BlockSpec(memory_space=pl.ANY)],
        out_specs=[vmem] * 3,
        scratch_shapes=[
            pltpu.VMEM((2 * wanted.shape[0], 128), jnp.int32),
            pltpu.VMEM((2 * wanted.shape[0], 128), jnp.float32),
            pltpu.SemaphoreType.DMA(()),
        ],
        compiler_params=pltpu.CompilerParams(vmem_limit_bytes=24 * MIB),
        name="counts",
    )(place, twin_wanted, wanted, database)
    twin = swap(own)

    early = pl.pallas_call(
        early_kernel,
        out_shape=jax.ShapeDtypeStruct((2 * rows, features), jnp.float32),
        in_specs=[vmem] * 4,
        out_specs=vmem,
        compiler_params=pltpu.CompilerParams(vmem_limit_bytes=32 * MIB),
        name="early_sums",
    )(twin, own, near, early_counts)

    def late(number, dest):
        return pl.pallas_call(
            functools.partial(late_kernel, number),
            out_shape=jax.ShapeDtypeStruct((rows, features), jnp.float32),
            in_specs=[vmem] * (5 + len(across)),
            out_specs=vmem,
            compiler_params=pltpu.CompilerParams(vmem_limit_bytes=40 * MIB),
            name="late_sums",
        )(dest, early, late_counts, *across, beside, behind)

    twin_a = late(0, twin)
    own_b = swap(twin_a)
    own_a = late(1, own)
    twin_b = swap(own_a)

    half = count // 2
    tile = min(1024, half)
    whole = lambda shape: pl.BlockSpec(shape, lambda i, place: (0, 0))
    augmented, best = pl.pallas_call(
        score_kernel,
        grid_spec=pltpu.PrefetchScalarGridSpec(
            num_scalar_prefetch=1,
            grid=(half // tile,),
            in_specs=[whole((rows, features))] * 6
            + [pl.BlockSpec((tile, features), lambda i, place: (place[2] * (half // tile) + i, 0))],
            out_specs=[
                whole((rows, features)),
                pl.BlockSpec((tile // 128, 128), lambda i, place: (i, 0)),
            ],
            scratch_shapes=[pltpu.VMEM((features, 2 * rows), jnp.bfloat16)],
        ),
        out_shape=[
            jax.ShapeDtypeStruct((rows, features), jnp.bfloat16),
            jax.ShapeDtypeStruct((half // 128, 128), jnp.float32),
        ],
        compiler_params=pltpu.CompilerParams(vmem_limit_bytes=32 * MIB),
        cost_estimate=pl.CostEstimate(
            flops=2 * count * rows * features, bytes_accessed=count * features, transcendentals=0
        ),
        name="scores",
    )(place, own, own_a, own_b, twin, twin_a, twin_b, queries)

    received = [shift(best, s) for s in steps]
    for value in received:
        best = jnp.maximum(best, value)
    other_half = swap(best)
    first = jnp.where(core == 0, best, other_half)
    second = jnp.where(core == 0, other_half, best)
    return augmented, jnp.concatenate([first, second], axis=0).reshape(count)


def solution(mesh):
    return jax.shard_map(
        local,
        mesh=mesh,
        in_specs=(P("db", None), P("db", None), P("db"), P("pb", None)),
        out_specs=(P("db", None), P("pb")),
        check_vma=False,
    )
```

```python
import functools

import jax
import jax.numpy as jnp
from jax import lax
from jax.experimental import pallas as pl
from jax.experimental.pallas import tpu as pltpu
from jax.sharding import PartitionSpec as P

epsilon = 1e-06
MIB = 1 << 20


def column_inverse(values):
    squares = jnp.sum(values * values, axis=-1, keepdims=True)
    return lax.rsqrt(squares + epsilon)


def as_row(column):
    wide = jnp.broadcast_to(column, (column.shape[0], 128))
    return wide.T[0:1, :]


def count_kernel(planes, place_ref, twin_ref, own_ref, database_ref, near_ref, early_ref, late_ref, copy_ref, tiles_ref, lows_ref, sem):
    rows = copy_ref.shape[0]
    fanout = own_ref.shape[0] * 128 // rows
    quarter = rows // 4
    span = (planes - 1) * quarter
    early_tiles = early_ref.shape[1] // 128
    late_tiles = late_ref.shape[1] // 128
    copy = pltpu.make_async_copy(database_ref, copy_ref, sem)
    copy.start()
    me, plane, core = place_ref[0], place_ref[1], place_ref[2]
    bits = rows.bit_length() - 1
    lines = own_ref.shape[0]
    for number, wanted_ref in enumerate((twin_ref, own_ref)):
        wanted = wanted_ref[...]
        owner = wanted >> bits
        side = owner & 1
        row = wanted & (rows - 1)
        cross = (row >> (bits - 2)) ^ me
        inner = row & (quarter - 1)
        away = (owner >> 1) ^ plane
        alone = (away == 0) | (away == planes - 1)
        held = jnp.where(alone, side, (away - 1) & 1) == core
        behind = ((away - 1) >> 1) * (2 * quarter) + side * quarter
        behind = inner + jnp.where(away == planes - 1, (planes - 2) * quarter, behind)
        section = jnp.where(cross == 0, 0, jnp.where(cross == 3, span, jnp.where(cross == 1 + core, 2 * span, 3 * span)))
        position = jnp.where(away == 0, row, rows + section + behind)
        position = jnp.where((wanted >= 0) & held, position, -1)
        tiles_ref[number * lines : (number + 1) * lines, :] = position >> 7
        lows_ref[number * lines : (number + 1) * lines, :] = position & 127

    group = 16
    height = (early_tiles + late_tiles) * group
    width = group * fanout
    at_row = lax.broadcasted_iota(jnp.int32, (height, width), 0)
    at_lane = lax.broadcasted_iota(jnp.int32, (height, width), 1)
    target = jnp.where(at_lane // fanout == at_row % group, at_row // group, -2)
    low_of = lax.broadcasted_iota(jnp.int32, (128, width), 0)
    each = width // 128

    def flat(ref, at):
        return jnp.concatenate([ref[pl.ds(at * each + i, 1), :] for i in range(each)], axis=1)

    def body(at, carry):
        tile = jnp.broadcast_to(flat(tiles_ref, at), (height, width))
        low = jnp.broadcast_to(flat(lows_ref, at), (128, width))
        left = jnp.where(tile == target, 1.0, 0.0).astype(jnp.bfloat16)
        right = jnp.where(low == low_of, 1.0, 0.0).astype(jnp.bfloat16)
        counts = lax.dot_general(
            left, right, (((1,), (1,)), ((), ())), preferred_element_type=jnp.float32
        ).astype(jnp.bfloat16)
        start = pl.ds(pl.multiple_of(at * group, group), group)
        for t in range(early_tiles):
            early_ref[start, t * 128 : (t + 1) * 128] = counts[t * group : (t + 1) * group, :]
        for t in range(late_tiles):
            first = (early_tiles + t) * group
            late_ref[start, t * 128 : (t + 1) * 128] = counts[first : first + group, :]
        return carry

    lax.fori_loop(0, 2 * rows // group, body, 0, unroll=4)
    copy.wait()


def pack_kernel(place_ref, twin_ref, near_ref, across_ref, near_both_ref, across_both_ref, alone_ref):
    quarter = near_ref.shape[0]
    me, core = place_ref[0], place_ref[2]
    mine = pl.ds(pl.multiple_of(core * quarter, quarter), quarter)
    others = pl.ds(pl.multiple_of((1 - core) * quarter, quarter), quarter)
    near_both_ref[mine, :] = near_ref[...]
    near_both_ref[others, :] = twin_ref[pl.ds(pl.multiple_of(me * quarter, quarter), quarter), :]
    across_both_ref[mine, :] = across_ref[...]
    alone_ref[...] = across_ref[...]
    across_both_ref[others, :] = twin_ref[pl.ds(pl.multiple_of((me ^ 3) * quarter, quarter), quarter), :]


def spread_terms(dest, dest_inverse, block, far, counts):
    products = lax.dot_general(
        dest, block, (((1,), (1,)), ((), ())), preferred_element_type=jnp.float32
    )
    cosine = products * dest_inverse * far
    halfway = (1.0 + cosine) * 0.5
    weight = halfway * halfway * halfway
    coefficient = (weight * far).astype(jnp.bfloat16).astype(jnp.float32)
    spread = coefficient * counts.astype(jnp.float32)
    high = spread.astype(jnp.bfloat16)
    low = (spread - high.astype(jnp.float32)).astype(jnp.bfloat16)
    return jnp.dot(high, block, preferred_element_type=jnp.float32) + jnp.dot(
        low, block, preferred_element_type=jnp.float32
    )


def early_kernel(twin_ref, own_ref, counts_ref, *rest):
    out_ref = rest[-1]
    rows = own_ref.shape[0]
    block = jnp.concatenate([own_ref[...]] + [ref[...] for ref in rest[:-1]], axis=0)
    far = as_row(column_inverse(block.astype(jnp.float32)))
    for number, dest_ref in enumerate((twin_ref, own_ref)):
        lines = slice(number * rows, (number + 1) * rows)
        dest = dest_ref[...]
        dest_inverse = column_inverse(dest.astype(jnp.float32))
        out_ref[lines, :] = spread_terms(dest, dest_inverse, block, far, counts_ref[lines, :])


def late_kernel(number, dest_ref, early_ref, counts_ref, *rest):
    out_ref = rest[-1]
    rows = dest_ref.shape[0]
    lines = slice(number * rows, (number + 1) * rows)
    block = jnp.concatenate([ref[...] for ref in rest[:-1]], axis=0)
    far = as_row(column_inverse(block.astype(jnp.float32)))
    dest = dest_ref[...]
    dest_inverse = column_inverse(dest.astype(jnp.float32))
    terms = spread_terms(dest, dest_inverse, block, far, counts_ref[lines, :])
    out_ref[...] = early_ref[lines, :] + terms


def score_kernel(place_ref, own_ref, own_a_ref, own_b_ref, twin_ref, twin_a_ref, twin_b_ref, queries_ref, augmented_ref, best_ref, turned_ref, held_ref, sems):
    rows = own_ref.shape[0]
    half = held_ref.shape[0]
    chunks = sems.shape[0]
    tile = half // chunks
    core = place_ref[2]

    def fetch(i):
        at = pl.multiple_of(i * tile, tile)
        return pltpu.make_async_copy(
            queries_ref.at[pl.ds(pl.multiple_of(core * half + at, tile), tile), :],
            held_ref.at[pl.ds(at, tile), :],
            sems.at[i],
        )

    for i in range(chunks):
        fetch(i).start()
    parts = ((own_ref, own_a_ref, own_b_ref), (twin_ref, twin_a_ref, twin_b_ref))
    for number, (row_ref, a_ref, b_ref) in enumerate(parts):
        values = row_ref[...].astype(jnp.float32)
        summed = values * column_inverse(values) + (a_ref[...] + b_ref[...])
        augmented = (summed * column_inverse(summed)).astype(jnp.bfloat16)
        if number == 0:
            augmented_ref[...] = augmented
        turned_ref[:, number * rows : (number + 1) * rows] = augmented.T

    step = min(256, tile)
    lines = step // 128
    shape = (lines, 16, 8, 128)
    lane = lax.broadcasted_iota(jnp.int32, shape, 3)
    query = lax.broadcasted_iota(jnp.int32, shape, 1) * 8 + lax.broadcasted_iota(jnp.int32, shape, 2)
    diagonal = lane == query

    @pl.loop(0, chunks)
    def _(i):
        fetch(i).wait()
        at = pl.multiple_of(i * tile, tile)
        line = pl.multiple_of(i * (tile // 128), tile // 128)
        found = []
        for first in range(0, tile, step):
            block = held_ref[pl.ds(at + first, step), :]
            widest = None
            for column in range(0, 2 * rows, 256):
                scores = jnp.dot(
                    block, turned_ref[:, column : column + 256], preferred_element_type=jnp.float32
                )
                scores = jnp.maximum(scores[:, :128], scores[:, 128:])
                widest = scores if widest is None else jnp.maximum(widest, scores)
            best = jnp.broadcast_to(jnp.max(widest, axis=1, keepdims=True), widest.shape)
            best = jnp.where(diagonal, best.reshape(shape), -jnp.inf)
            found.append(jnp.max(jnp.max(best, axis=1), axis=1))
        best_ref[pl.ds(line, tile // 128), :] = jnp.concatenate(found, axis=0)


def local(database, neighbours, valid_count, queries):
    rows, features = database.shape
    fanout = neighbours.shape[1]
    count = queries.shape[0]
    owners = lax.axis_size("db")
    panels = lax.axis_size("pb")
    assert panels == 4 and owners % 4 == 0 and owners & (owners - 1) == 0
    planes = owners // 2
    quarter = rows // panels
    me = lax.axis_index("pb")
    owner = lax.axis_index("db")
    plane, core = owner // 2, owner % 2

    def along(value, even, odd):
        apart = (even, odd)
        pairs = [(i, ((i // 2) ^ apart[i % 2]) * 2 + i % 2) for i in range(owners)]
        return lax.ppermute(value, "db", pairs)

    def swap(value):
        return lax.ppermute(value, "db", [(i, i ^ 1) for i in range(owners)])

    def cross(value, bits):
        pairs = []
        for panel in range(panels):
            for i in range(owners):
                pairs.append((panel * owners + i, (panel ^ bits[i % 2]) * owners + i))
        return lax.ppermute(value, ("pb", "db"), pairs)

    mine = lax.dynamic_slice_in_dim(database, me * quarter, quarter, 0)
    other = lax.dynamic_slice_in_dim(database, (me ^ 3) * quarter, quarter, 0)
    twin = swap(database)
    place = jnp.stack([me, plane, core]).astype(jnp.int32)
    vmem = pl.BlockSpec(memory_space=pltpu.VMEM)
    smem = pl.BlockSpec(memory_space=pltpu.SMEM)
    last = planes - 1
    near_last = along(mine, last, last)
    mine_both, other_both, other_alone = pl.pallas_call(
        pack_kernel,
        out_shape=[jax.ShapeDtypeStruct((2 * quarter, features), jnp.bfloat16)] * 2
        + [jax.ShapeDtypeStruct((quarter, features), jnp.bfloat16)],
        in_specs=[smem] + [vmem] * 3,
        out_specs=[vmem] * 3,
        name="pack",
    )(place, twin, mine, other)
    pairs = [(j, j + 1) for j in range(1, last, 2)]
    near = jnp.concatenate([along(mine_both, *pair) for pair in pairs] + [near_last], axis=0)
    across = [along(other_both, *pair) for pair in pairs] + [along(other_alone, last, last)]
    beside = cross(near, (1, 2))
    behind = cross(near, (2, 1))

    slots = jnp.arange(fanout, dtype=jnp.int32)[None, :]
    wanted = jnp.where(slots < valid_count[:, None], neighbours, -1).reshape(-1, 128)
    twin_wanted = swap(wanted)
    span = (planes - 1) * quarter
    early_counts, late_counts, own = pl.pallas_call(
        functools.partial(count_kernel, planes),
        out_shape=[
            jax.ShapeDtypeStruct((2 * rows, rows + 2 * span), jnp.bfloat16),
            jax.ShapeDtypeStruct((2 * rows, 2 * span), jnp.bfloat16),
            jax.ShapeDtypeStruct((rows, features), jnp.bfloat16),
        ],
        in_specs=[smem, vmem, vmem] + [pl.BlockSpec(memory_space=pl.ANY)] * 2,
        out_specs=[vmem] * 3,
        scratch_shapes=[
            pltpu.VMEM((2 * wanted.shape[0], 128), jnp.int32),
            pltpu.VMEM((2 * wanted.shape[0], 128), jnp.int32),
            pltpu.SemaphoreType.DMA(()),
        ],
        compiler_params=pltpu.CompilerParams(vmem_limit_bytes=24 * MIB),
        cost_estimate=pl.CostEstimate(flops=1 << 33, bytes_accessed=4 * rows * rows, transcendentals=0),
        name="counts",
    )(place, twin_wanted, wanted, database, near)

    early = pl.pallas_call(
        early_kernel,
        out_shape=jax.ShapeDtypeStruct((2 * rows, features), jnp.float32),
        in_specs=[vmem] * (4 + len(across)),
        out_specs=vmem,
        compiler_params=pltpu.CompilerParams(vmem_limit_bytes=40 * MIB),
        name="early_sums",
    )(twin, own, early_counts, near, *across)

    def late(number, dest):
        return pl.pallas_call(
            functools.partial(late_kernel, number),
            out_shape=jax.ShapeDtypeStruct((rows, features), jnp.float32),
            in_specs=[vmem] * 5,
            out_specs=vmem,
            compiler_params=pltpu.CompilerParams(vmem_limit_bytes=40 * MIB),
            name="late_sums",
        )(dest, early, late_counts, beside, behind)

    twin_a = late(0, twin)
    own_b = swap(twin_a)
    own_a = late(1, own)
    twin_b = swap(own_a)

    half = count // 2
    chunks = 4
    augmented, best = pl.pallas_call(
        score_kernel,
        out_shape=[
            jax.ShapeDtypeStruct((rows, features), jnp.bfloat16),
            jax.ShapeDtypeStruct((half // 128, 128), jnp.float32),
        ],
        in_specs=[smem] + [vmem] * 6 + [pl.BlockSpec(memory_space=pl.ANY)],
        out_specs=[vmem, vmem],
        scratch_shapes=[
            pltpu.VMEM((features, 2 * rows), jnp.bfloat16),
            pltpu.VMEM((half, features), jnp.bfloat16),
            pltpu.SemaphoreType.DMA((chunks,)),
        ],
        compiler_params=pltpu.CompilerParams(vmem_limit_bytes=40 * MIB),
        cost_estimate=pl.CostEstimate(
            flops=2 * count * rows * features, bytes_accessed=count * features, transcendentals=0
        ),
        name="scores",
    )(place, own, own_a, own_b, twin, twin_a, twin_b, queries)

    received = [along(best, apart, apart) for apart in range(1, planes)]
    for value in received:
        best = jnp.maximum(best, value)
    other_half = swap(best)
    first = jnp.where(core == 0, best, other_half)
    second = jnp.where(core == 0, other_half, best)
    return augmented, jnp.concatenate([first, second], axis=0).reshape(count)


def solution(mesh):
    return jax.shard_map(
        local,
        mesh=mesh,
        in_specs=(P("db", None), P("db", None), P("db"), P("pb", None)),
        out_specs=(P("db", None), P("pb")),
        check_vma=False,
    )
```

```python
import functools

import jax
import jax.numpy as jnp
from jax import lax
from jax.experimental import pallas as pl
from jax.experimental.pallas import tpu as pltpu
from jax.sharding import PartitionSpec as P

epsilon = 1e-06
MIB = 1 << 20


def column_inverse(values):
    squares = jnp.sum(values * values, axis=-1, keepdims=True)
    return lax.rsqrt(squares + epsilon)


def as_row(column):
    wide = jnp.broadcast_to(column, (column.shape[0], 128))
    return wide.T[0:1, :]


def position_of():
    owner = lax.axis_index("db")
    return lax.axis_index("pb"), owner // 2, owner % 2


def count_kernel(planes, twin_ref, own_ref, database_ref, near_ref, early_ref, late_ref, copy_ref, tiles_ref, lows_ref, sem):
    rows = copy_ref.shape[0]
    fanout = own_ref.shape[0] * 128 // rows
    quarter = rows // 4
    span = (planes - 1) * quarter
    early_tiles = early_ref.shape[1] // 128
    late_tiles = late_ref.shape[1] // 128
    copy = pltpu.make_async_copy(database_ref, copy_ref, sem)
    copy.start()
    me, plane, core = position_of()
    bits = rows.bit_length() - 1
    lines = own_ref.shape[0]
    for number, wanted_ref in enumerate((twin_ref, own_ref)):
        wanted = wanted_ref[...]
        owner = wanted >> bits
        side = owner & 1
        row = wanted & (rows - 1)
        cross = (row >> (bits - 2)) ^ me
        inner = row & (quarter - 1)
        away = (owner >> 1) ^ plane
        paired = (cross == 3) & (away > 0) & (away < planes - 1)
        held = jnp.where(paired, (away - 1) & 1, side) == core
        behind = inner + jnp.where(
            paired, ((away - 1) >> 1) * (2 * quarter) + (side ^ core) * quarter, (away - 1) * quarter
        )
        section = jnp.where(cross == 0, 0, jnp.where(cross == 3, span, jnp.where(cross == 1 + core, 2 * span, 3 * span)))
        position = jnp.where(away == 0, row, rows + section + behind)
        position = jnp.where((wanted >= 0) & held, position, -1)
        tiles_ref[number * lines : (number + 1) * lines, :] = position >> 7
        lows_ref[number * lines : (number + 1) * lines, :] = position & 127

    group = 16
    height = (early_tiles + late_tiles) * group
    width = group * fanout
    at_row = lax.broadcasted_iota(jnp.int32, (height, width), 0)
    at_lane = lax.broadcasted_iota(jnp.int32, (height, width), 1)
    target = jnp.where(at_lane // fanout == at_row % group, at_row // group, -2)
    low_of = lax.broadcasted_iota(jnp.int32, (128, width), 0)
    each = width // 128

    def flat(ref, at):
        return jnp.concatenate([ref[pl.ds(at * each + i, 1), :] for i in range(each)], axis=1)

    def body(at, carry):
        tile = jnp.broadcast_to(flat(tiles_ref, at), (height, width))
        low = jnp.broadcast_to(flat(lows_ref, at), (128, width))
        left = jnp.where(tile == target, 1.0, 0.0).astype(jnp.bfloat16)
        right = jnp.where(low == low_of, 1.0, 0.0).astype(jnp.bfloat16)
        counts = lax.dot_general(
            left, right, (((1,), (1,)), ((), ())), preferred_element_type=jnp.float32
        ).astype(jnp.bfloat16)
        start = pl.ds(pl.multiple_of(at * group, group), group)
        for t in range(early_tiles):
            early_ref[start, t * 128 : (t + 1) * 128] = counts[t * group : (t + 1) * group, :]
        for t in range(late_tiles):
            first = (early_tiles + t) * group
            late_ref[start, t * 128 : (t + 1) * 128] = counts[first : first + group, :]
        return carry

    lax.fori_loop(0, 2 * rows // group, body, 0, unroll=4)
    copy.wait()


def spread_terms(dest, dest_inverse, block, far, counts):
    products = lax.dot_general(
        dest, block, (((1,), (1,)), ((), ())), preferred_element_type=jnp.float32
    )
    cosine = products * dest_inverse * far
    halfway = (1.0 + cosine) * 0.5
    weight = halfway * halfway * halfway
    coefficient = (weight * far).astype(jnp.bfloat16).astype(jnp.float32)
    spread = coefficient * counts.astype(jnp.float32)
    high = spread.astype(jnp.bfloat16)
    low = (spread - high.astype(jnp.float32)).astype(jnp.bfloat16)
    return jnp.dot(high, block, preferred_element_type=jnp.float32) + jnp.dot(
        low, block, preferred_element_type=jnp.float32
    )


def early_kernel(twin_ref, own_ref, counts_ref, *rest):
    out_ref = rest[-1]
    rows = own_ref.shape[0]
    block = jnp.concatenate([own_ref[...]] + [ref[...] for ref in rest[:-1]], axis=0)
    far = as_row(column_inverse(block.astype(jnp.float32)))
    for number, dest_ref in enumerate((twin_ref, own_ref)):
        lines = slice(number * rows, (number + 1) * rows)
        dest = dest_ref[...]
        dest_inverse = column_inverse(dest.astype(jnp.float32))
        out_ref[lines, :] = spread_terms(dest, dest_inverse, block, far, counts_ref[lines, :])


def late_kernel(number, dest_ref, early_ref, counts_ref, *rest):
    out_ref = rest[-1]
    rows = dest_ref.shape[0]
    lines = slice(number * rows, (number + 1) * rows)
    block = jnp.concatenate([ref[...] for ref in rest[:-1]], axis=0)
    far = as_row(column_inverse(block.astype(jnp.float32)))
    dest = dest_ref[...]
    dest_inverse = column_inverse(dest.astype(jnp.float32))
    terms = spread_terms(dest, dest_inverse, block, far, counts_ref[lines, :])
    out_ref[...] = early_ref[lines, :] + terms


def score_kernel(own_ref, own_a_ref, own_b_ref, twin_ref, twin_a_ref, twin_b_ref, queries_ref, augmented_ref, best_ref, turned_ref, held_ref, sems):
    rows = own_ref.shape[0]
    half = held_ref.shape[0]
    chunks = sems.shape[0]
    tile = half // chunks
    core = position_of()[2]

    def fetch(i):
        at = pl.multiple_of(i * tile, tile)
        return pltpu.make_async_copy(
            queries_ref.at[pl.ds(pl.multiple_of(core * half + at, tile), tile), :],
            held_ref.at[pl.ds(at, tile), :],
            sems.at[i],
        )

    for i in range(chunks):
        fetch(i).start()
    parts = ((own_ref, own_a_ref, own_b_ref), (twin_ref, twin_a_ref, twin_b_ref))
    for number, (row_ref, a_ref, b_ref) in enumerate(parts):
        values = row_ref[...].astype(jnp.float32)
        summed = values * column_inverse(values) + (a_ref[...] + b_ref[...])
        augmented = (summed * column_inverse(summed)).astype(jnp.bfloat16)
        if number == 0:
            augmented_ref[...] = augmented
        turned_ref[:, number * rows : (number + 1) * rows] = augmented.T

    step = min(1024, tile)
    lines = step // 128
    shape = (lines, 16, 8, 128)
    lane = lax.broadcasted_iota(jnp.int32, shape, 3)
    query = lax.broadcasted_iota(jnp.int32, shape, 1) * 8 + lax.broadcasted_iota(jnp.int32, shape, 2)
    diagonal = lane == query

    @pl.loop(0, chunks)
    def _(i):
        fetch(i).wait()
        at = pl.multiple_of(i * tile, tile)
        line = pl.multiple_of(i * (tile // 128), tile // 128)
        found = []
        for first in range(0, tile, step):
            block = held_ref[pl.ds(at + first, step), :]
            widest = None
            for column in range(0, 2 * rows, 256):
                scores = jnp.dot(
                    block, turned_ref[:, column : column + 256], preferred_element_type=jnp.float32
                )
                scores = jnp.maximum(scores[:, :128], scores[:, 128:])
                widest = scores if widest is None else jnp.maximum(widest, scores)
            best = jnp.broadcast_to(jnp.max(widest, axis=1, keepdims=True), widest.shape)
            best = jnp.where(diagonal, best.reshape(shape), -jnp.inf)
            found.append(jnp.max(jnp.max(best, axis=1), axis=1))
        best_ref[pl.ds(line, tile // 128), :] = jnp.concatenate(found, axis=0)


def local(database, neighbours, valid_count, queries):
    rows, features = database.shape
    fanout = neighbours.shape[1]
    count = queries.shape[0]
    owners = lax.axis_size("db")
    panels = lax.axis_size("pb")
    assert panels == 4 and owners % 4 == 0 and owners & (owners - 1) == 0
    planes = owners // 2
    quarter = rows // panels
    me = lax.axis_index("pb")
    core = lax.axis_index("db") % 2

    def along(value, even, odd):
        apart = (even, odd)
        pairs = [(i, ((i // 2) ^ apart[i % 2]) * 2 + i % 2) for i in range(owners)]
        return lax.ppermute(value, "db", pairs)

    def swap(value):
        return lax.ppermute(value, "db", [(i, i ^ 1) for i in range(owners)])

    def cross(value, bits):
        pairs = []
        for panel in range(panels):
            for i in range(owners):
                pairs.append((panel * owners + i, (panel ^ bits[i % 2]) * owners + i))
        return lax.ppermute(value, ("pb", "db"), pairs)

    mine = lax.dynamic_slice_in_dim(database, me * quarter, quarter, 0)
    other = lax.dynamic_slice_in_dim(database, (me ^ 3) * quarter, quarter, 0)
    twin = swap(database)
    after_twin = twin[0, 0] * 0
    near = [along(mine, apart, apart) for apart in range(1, planes)]
    near = jnp.concatenate([near[0] + after_twin] + near[1:], axis=0)
    twin_other = lax.dynamic_slice_in_dim(twin, (me ^ 3) * quarter, quarter, 0)
    both = jnp.concatenate([other, twin_other], axis=0)
    last = planes - 1
    across = [along(both, apart, apart + 1) for apart in range(1, last, 2)] + [along(other, last, last)]
    vmem = pl.BlockSpec(memory_space=pltpu.VMEM)
    beside = cross(near, (1, 2))
    behind = cross(near, (2, 1))

    slots = jnp.arange(fanout, dtype=jnp.int32)[None, :]
    wanted = jnp.where(slots < valid_count[:, None], neighbours, -1).reshape(-1, 128)
    twin_wanted = swap(wanted)
    span = (planes - 1) * quarter
    early_counts, late_counts, own = pl.pallas_call(
        functools.partial(count_kernel, planes),
        out_shape=[
            jax.ShapeDtypeStruct((2 * rows, rows + 2 * span), jnp.bfloat16),
            jax.ShapeDtypeStruct((2 * rows, 2 * span), jnp.bfloat16),
            jax.ShapeDtypeStruct((rows, features), jnp.bfloat16),
        ],
        in_specs=[vmem, vmem, pl.BlockSpec(memory_space=pltpu.HBM), vmem],
        out_specs=[vmem] * 3,
        scratch_shapes=[
            pltpu.VMEM((2 * wanted.shape[0], 128), jnp.int32),
            pltpu.VMEM((2 * wanted.shape[0], 128), jnp.int32),
            pltpu.SemaphoreType.DMA(()),
        ],
        compiler_params=pltpu.CompilerParams(vmem_limit_bytes=24 * MIB),
        cost_estimate=pl.CostEstimate(flops=1 << 33, bytes_accessed=4 * rows * rows, transcendentals=0),
        name="counts",
    )(twin_wanted, wanted, database, near)

    early = pl.pallas_call(
        early_kernel,
        out_shape=jax.ShapeDtypeStruct((2 * rows, features), jnp.float32),
        in_specs=[vmem] * (4 + len(across)),
        out_specs=vmem,
        compiler_params=pltpu.CompilerParams(vmem_limit_bytes=40 * MIB),
        name="early_sums",
    )(twin, own, early_counts, near, *across)

    def late(number, dest):
        return pl.pallas_call(
            functools.partial(late_kernel, number),
            out_shape=jax.ShapeDtypeStruct((rows, features), jnp.float32),
            in_specs=[vmem] * 5,
            out_specs=vmem,
            compiler_params=pltpu.CompilerParams(vmem_limit_bytes=40 * MIB),
            name="late_sums",
        )(dest, early, late_counts, beside, behind)

    twin_a = late(0, twin)
    own_b = swap(twin_a)
    own_a = late(1, own)
    twin_b = swap(own_a)

    half = count // 2
    chunks = 4
    augmented, best = pl.pallas_call(
        score_kernel,
        out_shape=[
            jax.ShapeDtypeStruct((rows, features), jnp.bfloat16),
            jax.ShapeDtypeStruct((half // 128, 128), jnp.float32),
        ],
        in_specs=[vmem] * 6 + [pl.BlockSpec(memory_space=pltpu.HBM)],
        out_specs=[vmem, vmem],
        scratch_shapes=[
            pltpu.VMEM((features, 2 * rows), jnp.bfloat16),
            pltpu.VMEM((half, features), jnp.bfloat16),
            pltpu.SemaphoreType.DMA((chunks,)),
        ],
        compiler_params=pltpu.CompilerParams(vmem_limit_bytes=40 * MIB),
        cost_estimate=pl.CostEstimate(
            flops=2 * count * rows * features, bytes_accessed=count * features, transcendentals=0
        ),
        name="scores",
    )(own, own_a, own_b, twin, twin_a, twin_b, queries)

    received = [along(best, apart, apart) for apart in range(1, planes)]
    for value in received:
        best = jnp.maximum(best, value)
    other_half = swap(best)
    first = jnp.where(core == 0, best, other_half)
    second = jnp.where(core == 0, other_half, best)
    return augmented, jnp.concatenate([first, second], axis=0).reshape(count)


def solution(mesh):
    return jax.shard_map(
        local,
        mesh=mesh,
        in_specs=(P("db", None), P("db", None), P("db"), P("pb", None)),
        out_specs=(P("db", None), P("pb")),
        check_vma=False,
    )
```

```python
import functools

import jax
import jax.numpy as jnp
from jax import lax
from jax.experimental import pallas as pl
from jax.experimental.pallas import tpu as pltpu
from jax.sharding import PartitionSpec as P

epsilon = 1e-06
MIB = 1 << 20


def column_inverse(values):
    squares = jnp.sum(values * values, axis=-1, keepdims=True)
    return lax.rsqrt(squares + epsilon)


def as_row(column):
    wide = jnp.broadcast_to(column, (column.shape[0], 128))
    return wide.T[0:1, :]


def position_of():
    owner = lax.axis_index("db")
    return lax.axis_index("pb"), owner // 2, owner % 2


def count_kernel(planes, twin_ref, own_ref, database_ref, adjacent_ref, early_ref, late_ref, copy_ref, tiles_ref, lows_ref, sem):
    rows = copy_ref.shape[0]
    fanout = own_ref.shape[0] * 128 // rows
    quarter = rows // 4
    span = (planes - 1) * quarter
    early_tiles = early_ref.shape[1] // 128
    late_tiles = late_ref.shape[1] // 128
    copy = pltpu.make_async_copy(database_ref, copy_ref, sem)
    copy.start()
    me, plane, core = position_of()
    bits = rows.bit_length() - 1
    lines = own_ref.shape[0]
    for number, wanted_ref in enumerate((twin_ref, own_ref)):
        wanted = wanted_ref[...]
        owner = wanted >> bits
        side = owner & 1
        row = wanted & (rows - 1)
        cross = (row >> (bits - 2)) ^ me
        inner = row & (quarter - 1)
        away = (owner >> 1) ^ plane
        paired = (cross == 3) & (away > 1)
        held = jnp.where(paired, away & 1, side) == core
        straight = (away - 1) * quarter
        crossed = ((away >> 1) * 2 - 1 + (side ^ core)) * quarter
        late = early_tiles * 128 + jnp.where(cross == 3, 0, jnp.where(cross == 1 + core, span, 2 * span))
        position = jnp.where(cross == 0, rows, late) + jnp.where(paired, crossed, straight) + inner
        position = jnp.where(away == 0, row, position)
        position = jnp.where((wanted >= 0) & held, position, -1)
        tiles_ref[number * lines : (number + 1) * lines, :] = position >> 7
        lows_ref[number * lines : (number + 1) * lines, :] = position & 127

    group = 16
    height = (early_tiles + late_tiles) * group
    width = group * fanout
    at_row = lax.broadcasted_iota(jnp.int32, (height, width), 0)
    at_lane = lax.broadcasted_iota(jnp.int32, (height, width), 1)
    target = jnp.where(at_lane // fanout == at_row % group, at_row // group, -2)
    low_of = lax.broadcasted_iota(jnp.int32, (128, width), 0)
    each = width // 128

    def flat(ref, at):
        return jnp.concatenate([ref[pl.ds(at * each + i, 1), :] for i in range(each)], axis=1)

    def body(at, carry):
        tile = jnp.broadcast_to(flat(tiles_ref, at), (height, width))
        low = jnp.broadcast_to(flat(lows_ref, at), (128, width))
        left = jnp.where(tile == target, 1.0, 0.0).astype(jnp.bfloat16)
        right = jnp.where(low == low_of, 1.0, 0.0).astype(jnp.bfloat16)
        counts = lax.dot_general(
            left, right, (((1,), (1,)), ((), ())), preferred_element_type=jnp.float32
        ).astype(jnp.bfloat16)
        start = pl.ds(pl.multiple_of(at * group, group), group)
        for t in range(early_tiles):
            early_ref[start, t * 128 : (t + 1) * 128] = counts[t * group : (t + 1) * group, :]
        for t in range(late_tiles):
            first = (early_tiles + t) * group
            late_ref[start, t * 128 : (t + 1) * 128] = counts[first : first + group, :]
        return carry

    lax.fori_loop(0, 2 * rows // group, body, 0, unroll=4)
    copy.wait()


def spread_terms(dest, dest_inverse, block, far, counts):
    products = lax.dot_general(
        dest, block, (((1,), (1,)), ((), ())), preferred_element_type=jnp.float32
    )
    cosine = products * dest_inverse * far
    halfway = (1.0 + cosine) * 0.5
    weight = halfway * halfway * halfway
    coefficient = (weight * far).astype(jnp.bfloat16).astype(jnp.float32)
    spread = coefficient * counts.astype(jnp.float32)
    high = spread.astype(jnp.bfloat16)
    low = (spread - high.astype(jnp.float32)).astype(jnp.bfloat16)
    return jnp.dot(high, block, preferred_element_type=jnp.float32) + jnp.dot(
        low, block, preferred_element_type=jnp.float32
    )


def early_kernel(twin_ref, own_ref, counts_ref, *rest):
    out_ref = rest[-1]
    rows = own_ref.shape[0]
    block = jnp.concatenate([own_ref[...]] + [ref[...] for ref in rest[:-1]], axis=0)
    far = as_row(column_inverse(block.astype(jnp.float32)))
    for number, dest_ref in enumerate((twin_ref, own_ref)):
        lines = slice(number * rows, (number + 1) * rows)
        dest = dest_ref[...]
        dest_inverse = column_inverse(dest.astype(jnp.float32))
        out_ref[lines, :] = spread_terms(dest, dest_inverse, block, far, counts_ref[lines, : block.shape[0]])


def late_kernel(number, dest_ref, early_ref, counts_ref, *rest):
    out_ref = rest[-1]
    rows = dest_ref.shape[0]
    lines = slice(number * rows, (number + 1) * rows)
    adjacent_ref = rest[0]
    halfway = adjacent_ref.shape[0] // 2
    block = jnp.concatenate([adjacent_ref[halfway:, :]] + [ref[...] for ref in rest[1:-1]], axis=0)
    far = as_row(column_inverse(block.astype(jnp.float32)))
    dest = dest_ref[...]
    dest_inverse = column_inverse(dest.astype(jnp.float32))
    terms = spread_terms(dest, dest_inverse, block, far, counts_ref[lines, : block.shape[0]])
    out_ref[...] = early_ref[lines, :] + terms


def score_kernel(own_ref, own_a_ref, own_b_ref, twin_ref, twin_a_ref, twin_b_ref, queries_ref, augmented_ref, best_ref, rows_ref, held_ref, sems):
    rows = own_ref.shape[0]
    half = held_ref.shape[0]
    chunks = sems.shape[0]
    tile = half // chunks
    core = position_of()[2]

    def fetch(i):
        at = pl.multiple_of(i * tile, tile)
        return pltpu.make_async_copy(
            queries_ref.at[pl.ds(pl.multiple_of(core * half + at, tile), tile), :],
            held_ref.at[pl.ds(at, tile), :],
            sems.at[i],
        )

    for i in range(chunks):
        fetch(i).start()
    parts = ((own_ref, own_a_ref, own_b_ref), (twin_ref, twin_a_ref, twin_b_ref))
    for number, (row_ref, a_ref, b_ref) in enumerate(parts):
        values = row_ref[...].astype(jnp.float32)
        summed = values * column_inverse(values) + (a_ref[...] + b_ref[...])
        augmented = (summed * column_inverse(summed)).astype(jnp.bfloat16)
        if number == 0:
            augmented_ref[...] = augmented
        rows_ref[number * rows : (number + 1) * rows, :] = augmented

    step = 256

    @pl.loop(0, chunks)
    def _(i):
        fetch(i).wait()
        at = pl.multiple_of(i * tile, tile)
        line = pl.multiple_of(i * (tile // 128), tile // 128)
        found = []
        for first in range(0, tile, step):
            scores = lax.dot_general(
                rows_ref[...],
                held_ref[pl.ds(at + first, step), :],
                (((1,), (1,)), ((), ())),
                preferred_element_type=jnp.float32,
            )
            best = jnp.max(scores, axis=0, keepdims=True)
            found += [best[:, part : part + 128] for part in range(0, step, 128)]
        best_ref[pl.ds(line, tile // 128), :] = jnp.concatenate(found, axis=0)


def local(database, neighbours, valid_count, queries):
    rows, features = database.shape
    fanout = neighbours.shape[1]
    count = queries.shape[0]
    owners = lax.axis_size("db")
    panels = lax.axis_size("pb")
    assert panels == 4 and owners % 4 == 0 and owners & (owners - 1) == 0
    planes = owners // 2
    quarter = rows // panels
    me = lax.axis_index("pb")
    core = lax.axis_index("db") % 2

    def along(value, even, odd):
        apart = (even, odd)
        pairs = [(i, ((i // 2) ^ apart[i % 2]) * 2 + i % 2) for i in range(owners)]
        return lax.ppermute(value, "db", pairs)

    def swap(value):
        return lax.ppermute(value, "db", [(i, i ^ 1) for i in range(owners)])

    def cross(value, bits):
        pairs = []
        for panel in range(panels):
            for i in range(owners):
                pairs.append((panel * owners + i, (panel ^ bits[i % 2]) * owners + i))
        return lax.ppermute(value, ("pb", "db"), pairs)

    mine = lax.dynamic_slice_in_dim(database, me * quarter, quarter, 0)
    other = lax.dynamic_slice_in_dim(database, (me ^ 3) * quarter, quarter, 0)
    adjacent = along(jnp.concatenate([mine, other], axis=0), 1, 1)
    farther = [along(mine, apart, apart) for apart in range(2, planes)]
    twin = swap(database)
    twin_other = lax.dynamic_slice_in_dim(twin, (me ^ 3) * quarter, quarter, 0)
    both = jnp.concatenate([other, twin_other], axis=0) + adjacent[0, 0] * 0
    across = [along(both, apart, apart + 1) for apart in range(2, planes, 2)]
    vmem = pl.BlockSpec(memory_space=pltpu.VMEM)
    slots = jnp.arange(fanout, dtype=jnp.int32)[None, :]
    after_tie = (twin[0, 0] * 0).astype(jnp.int32)
    wanted = jnp.where(slots < valid_count[:, None], neighbours, -1).reshape(-1, 128) + after_tie
    twin_wanted = swap(wanted)
    padded = lambda size: (size + 127) // 128 * 128
    span = (planes - 1) * quarter
    early_counts, late_counts, own = pl.pallas_call(
        functools.partial(count_kernel, planes),
        out_shape=[
            jax.ShapeDtypeStruct((2 * rows, padded(rows + span)), jnp.bfloat16),
            jax.ShapeDtypeStruct((2 * rows, padded(3 * span)), jnp.bfloat16),
            jax.ShapeDtypeStruct((rows, features), jnp.bfloat16),
        ],
        in_specs=[vmem, vmem, pl.BlockSpec(memory_space=pltpu.HBM), vmem],
        out_specs=[vmem] * 3,
        scratch_shapes=[
            pltpu.VMEM((2 * wanted.shape[0], 128), jnp.int32),
            pltpu.VMEM((2 * wanted.shape[0], 128), jnp.int32),
            pltpu.SemaphoreType.DMA(()),
        ],
        compiler_params=pltpu.CompilerParams(vmem_limit_bytes=24 * MIB),
        cost_estimate=pl.CostEstimate(flops=1 << 33, bytes_accessed=4 * rows * rows, transcendentals=0),
        name="counts",
    )(twin_wanted, wanted, database, adjacent)
    after_counts = early_counts[0, 0] * 0 + both[0, 0] * 0
    near = jnp.concatenate([adjacent[:quarter] + after_counts] + farther, axis=0)
    beside = cross(near, (1, 2))
    behind = cross(near, (2, 1))

    early = pl.pallas_call(
        early_kernel,
        out_shape=jax.ShapeDtypeStruct((2 * rows, features), jnp.float32),
        in_specs=[vmem] * 4,
        out_specs=vmem,
        compiler_params=pltpu.CompilerParams(vmem_limit_bytes=40 * MIB),
        cost_estimate=pl.CostEstimate(flops=1 << 33, bytes_accessed=4 * rows * rows, transcendentals=0),
        name="early_sums",
    )(twin, own, early_counts, near)

    def late(number, dest):
        return pl.pallas_call(
            functools.partial(late_kernel, number),
            out_shape=jax.ShapeDtypeStruct((rows, features), jnp.float32),
            in_specs=[vmem] * (6 + len(across)),
            out_specs=vmem,
            compiler_params=pltpu.CompilerParams(vmem_limit_bytes=40 * MIB),
            name="late_sums",
        )(dest, early, late_counts, adjacent, *across, beside, behind)

    twin_a = late(0, twin)
    own_b = swap(twin_a)
    own_a = late(1, own)
    twin_b = swap(own_a)

    half = count // 2
    chunks = 4
    augmented, best = pl.pallas_call(
        score_kernel,
        out_shape=[
            jax.ShapeDtypeStruct((rows, features), jnp.bfloat16),
            jax.ShapeDtypeStruct((half // 128, 128), jnp.float32),
        ],
        in_specs=[vmem] * 6 + [pl.BlockSpec(memory_space=pltpu.HBM)],
        out_specs=[vmem, vmem],
        scratch_shapes=[
            pltpu.VMEM((2 * rows, features), jnp.bfloat16),
            pltpu.VMEM((half, features), jnp.bfloat16),
            pltpu.SemaphoreType.DMA((chunks,)),
        ],
        compiler_params=pltpu.CompilerParams(vmem_limit_bytes=40 * MIB),
        cost_estimate=pl.CostEstimate(
            flops=2 * count * rows * features, bytes_accessed=count * features, transcendentals=0
        ),
        name="scores",
    )(own, own_a, own_b, twin, twin_a, twin_b, queries)

    received = [along(best, apart, apart) for apart in range(1, planes)]
    for value in received:
        best = jnp.maximum(best, value)
    other_half = swap(best)
    first = jnp.where(core == 0, best, other_half)
    second = jnp.where(core == 0, other_half, best)
    return augmented, jnp.concatenate([first, second], axis=0).reshape(count)


def solution(mesh):
    return jax.shard_map(
        local,
        mesh=mesh,
        in_specs=(P("db", None), P("db", None), P("db"), P("pb", None)),
        out_specs=(P("db", None), P("pb")),
        check_vma=False,
    )
```

```python
import functools

import jax
import jax.numpy as jnp
from jax import lax
from jax.experimental import pallas as pl
from jax.experimental.pallas import tpu as pltpu
from jax.sharding import PartitionSpec as P

epsilon = 1e-06
MIB = 1 << 20


def column_inverse(values):
    squares = jnp.sum(values * values, axis=-1, keepdims=True)
    return lax.rsqrt(squares + epsilon)


def as_row(column):
    wide = jnp.broadcast_to(column, (column.shape[0], 128))
    return wide.T[0:1, :]


def position_of():
    owner = lax.axis_index("db")
    return lax.axis_index("pb"), owner // 2, owner % 2


def quarter_of(panel):
    return ((panel ^ (panel >> 1)) & 1) * 2 + (panel >> 1)


def count_kernel(
    planes, twin_ref, own_ref, twin_rows_ref, database_ref, adjacent_ref, early_ref, late_ref, copy_ref,
    both_ref, near_ref, across_ref, tiles_ref, lows_ref, sem,
):
    rows = copy_ref.shape[0]
    fanout = own_ref.shape[0] * 128 // rows
    quarter = rows // 4
    span = (planes - 1) * quarter
    early_tiles = early_ref.shape[1] // 128
    late_tiles = late_ref.shape[1] // 128
    copy = pltpu.make_async_copy(database_ref, copy_ref, sem)
    copy.start()
    me, plane, core = position_of()
    bits = rows.bit_length() - 1
    lines = own_ref.shape[0]
    for number, wanted_ref in enumerate((twin_ref, own_ref)):
        wanted = wanted_ref[...]
        owner = wanted >> bits
        side = owner & 1
        row = wanted & (rows - 1)
        part = row >> (bits - 2)
        cross = ((part & 1) * 2 + ((part ^ (part >> 1)) & 1)) ^ me
        inner = row & (quarter - 1)
        away = (owner >> 1) ^ plane
        paired = (cross == 3) & (away > 1)
        held = jnp.where(paired, away & 1, side) == core
        straight = (away - 1) * quarter
        crossed = ((away >> 1) * 2 - 1 + (side ^ core)) * quarter
        late = early_tiles * 128 + jnp.where(cross == 3, 0, jnp.where(cross == 1 + core, span, 2 * span))
        position = jnp.where(cross == 0, rows, late) + jnp.where(paired, crossed, straight) + inner
        position = jnp.where(away == 0, row, position)
        position = jnp.where((wanted >= 0) & held, position, -1)
        tiles_ref[number * lines : (number + 1) * lines, :] = position >> 7
        lows_ref[number * lines : (number + 1) * lines, :] = position & 127

    group = 16
    height = (early_tiles + late_tiles) * group
    width = group * fanout
    at_row = lax.broadcasted_iota(jnp.int32, (height, width), 0)
    at_lane = lax.broadcasted_iota(jnp.int32, (height, width), 1)
    target = jnp.where(at_lane // fanout == at_row % group, at_row // group, -2)
    low_of = lax.broadcasted_iota(jnp.int32, (128, width), 0)
    each = width // 128

    def flat(ref, at):
        return jnp.concatenate([ref[pl.ds(at * each + i, 1), :] for i in range(each)], axis=1)

    def body(at, carry):
        tile = jnp.broadcast_to(flat(tiles_ref, at), (height, width))
        low = jnp.broadcast_to(flat(lows_ref, at), (128, width))
        left = jnp.where(tile == target, 1.0, 0.0).astype(jnp.bfloat16)
        right = jnp.where(low == low_of, 1.0, 0.0).astype(jnp.bfloat16)
        counts = lax.dot_general(
            left, right, (((1,), (1,)), ((), ())), preferred_element_type=jnp.float32
        ).astype(jnp.bfloat16)
        start = pl.ds(pl.multiple_of(at * group, group), group)
        for t in range(early_tiles):
            early_ref[start, t * 128 : (t + 1) * 128] = counts[t * group : (t + 1) * group, :]
        for t in range(late_tiles):
            first = (early_tiles + t) * group
            late_ref[start, t * 128 : (t + 1) * 128] = counts[first : first + group, :]
        return carry

    lax.fori_loop(0, 2 * rows // group, body, 0, unroll=4)
    copy.wait()
    at = pl.multiple_of(quarter_of(me ^ 3) * quarter, quarter)
    both_ref[:quarter, :] = copy_ref[pl.ds(at, quarter), :]
    both_ref[quarter:, :] = twin_rows_ref[pl.ds(at, quarter), :]
    at = pl.multiple_of((me >> 1) * quarter, quarter)
    near_ref[...] = adjacent_ref[pl.ds(at, quarter), :]
    across_ref[...] = adjacent_ref[pl.ds(quarter - at, quarter), :]


def spread_terms(dest, dest_inverse, block, far, counts):
    products = lax.dot_general(
        dest, block, (((1,), (1,)), ((), ())), preferred_element_type=jnp.float32
    )
    cosine = products * dest_inverse * far
    halfway = (1.0 + cosine) * 0.5
    weight = halfway * halfway * halfway
    coefficient = (weight * far).astype(jnp.bfloat16).astype(jnp.float32)
    spread = coefficient * counts.astype(jnp.float32)
    high = spread.astype(jnp.bfloat16)
    low = (spread - high.astype(jnp.float32)).astype(jnp.bfloat16)
    return jnp.dot(high, block, preferred_element_type=jnp.float32) + jnp.dot(
        low, block, preferred_element_type=jnp.float32
    )


def early_kernel(twin_ref, own_ref, counts_ref, *rest):
    out_ref = rest[-1]
    rows = own_ref.shape[0]
    block = jnp.concatenate([own_ref[...]] + [ref[...] for ref in rest[:-1]], axis=0)
    far = as_row(column_inverse(block.astype(jnp.float32)))
    for number, dest_ref in enumerate((twin_ref, own_ref)):
        lines = slice(number * rows, (number + 1) * rows)
        dest = dest_ref[...]
        dest_inverse = column_inverse(dest.astype(jnp.float32))
        out_ref[lines, :] = spread_terms(dest, dest_inverse, block, far, counts_ref[lines, : block.shape[0]])


def late_kernel(number, dest_ref, early_ref, counts_ref, *rest):
    out_ref = rest[-1]
    rows = dest_ref.shape[0]
    lines = slice(number * rows, (number + 1) * rows)
    block = jnp.concatenate([ref[...] for ref in rest[:-1]], axis=0)
    far = as_row(column_inverse(block.astype(jnp.float32)))
    dest = dest_ref[...]
    dest_inverse = column_inverse(dest.astype(jnp.float32))
    terms = spread_terms(dest, dest_inverse, block, far, counts_ref[lines, : block.shape[0]])
    out_ref[...] = early_ref[lines, :] + terms


def score_kernel(own_ref, own_a_ref, own_b_ref, twin_ref, twin_a_ref, twin_b_ref, queries_ref, augmented_ref, best_ref, rows_ref, held_ref, sems):
    rows = own_ref.shape[0]
    half = held_ref.shape[0]
    chunks = sems.shape[0]
    tile = half // chunks
    core = position_of()[2]

    def fetch(i):
        at = pl.multiple_of(i * tile, tile)
        return pltpu.make_async_copy(
            queries_ref.at[pl.ds(pl.multiple_of(core * half + at, tile), tile), :],
            held_ref.at[pl.ds(at, tile), :],
            sems.at[i],
        )

    for i in range(chunks):
        fetch(i).start()
    parts = ((own_ref, own_a_ref, own_b_ref), (twin_ref, twin_a_ref, twin_b_ref))
    for number, (row_ref, a_ref, b_ref) in enumerate(parts):
        values = row_ref[...].astype(jnp.float32)
        summed = values * column_inverse(values) + (a_ref[...] + b_ref[...])
        augmented = (summed * column_inverse(summed)).astype(jnp.bfloat16)
        if number == 0:
            augmented_ref[...] = augmented
        rows_ref[number * rows : (number + 1) * rows, :] = augmented

    step = 256

    @pl.loop(0, chunks)
    def _(i):
        fetch(i).wait()
        at = pl.multiple_of(i * tile, tile)
        line = pl.multiple_of(i * (tile // 128), tile // 128)
        found = []
        for first in range(0, tile, step):
            scores = lax.dot_general(
                rows_ref[...],
                held_ref[pl.ds(at + first, step), :],
                (((1,), (1,)), ((), ())),
                preferred_element_type=jnp.float32,
            )
            best = jnp.max(scores, axis=0, keepdims=True)
            found += [best[:, part : part + 128] for part in range(0, step, 128)]
        best_ref[pl.ds(line, tile // 128), :] = jnp.concatenate(found, axis=0)


def local(database, neighbours, valid_count, queries):
    rows, features = database.shape
    fanout = neighbours.shape[1]
    count = queries.shape[0]
    owners = lax.axis_size("db")
    panels = lax.axis_size("pb")
    assert panels == 4 and owners % 4 == 0 and owners & (owners - 1) == 0
    planes = owners // 2
    quarter = rows // panels
    me = lax.axis_index("pb")
    core = lax.axis_index("db") % 2

    def along(value, even, odd):
        apart = (even, odd)
        pairs = [(i, ((i // 2) ^ apart[i % 2]) * 2 + i % 2) for i in range(owners)]
        return lax.ppermute(value, "db", pairs)

    def swap(value):
        return lax.ppermute(value, "db", [(i, i ^ 1) for i in range(owners)])

    def cross(value, bits):
        pairs = []
        for panel in range(panels):
            for i in range(owners):
                pairs.append((panel * owners + i, (panel ^ bits[i % 2]) * owners + i))
        return lax.ppermute(value, ("pb", "db"), pairs)

    pair = lax.dynamic_slice_in_dim(database, (quarter_of(me) >> 1) * 2 * quarter, 2 * quarter, 0)
    mine = jnp.where(me >> 1 == 1, pair[quarter:], pair[:quarter])
    adjacent = along(pair, 1, 1)
    farther = [along(mine, apart, apart) for apart in range(2, planes)]
    twin = swap(database)
    vmem = pl.BlockSpec(memory_space=pltpu.VMEM)
    slots = jnp.arange(fanout, dtype=jnp.int32)[None, :]
    wanted = jnp.where(slots < valid_count[:, None], neighbours, -1).reshape(-1, 128)
    twin_wanted = swap(wanted)
    padded = lambda size: (size + 127) // 128 * 128
    span = (planes - 1) * quarter
    early_counts, late_counts, own, both, near, across = pl.pallas_call(
        functools.partial(count_kernel, planes),
        out_shape=[
            jax.ShapeDtypeStruct((2 * rows, padded(rows + span)), jnp.bfloat16),
            jax.ShapeDtypeStruct((2 * rows, padded(3 * span)), jnp.bfloat16),
            jax.ShapeDtypeStruct((rows, features), jnp.bfloat16),
            jax.ShapeDtypeStruct((2 * quarter, features), jnp.bfloat16),
            jax.ShapeDtypeStruct((quarter, features), jnp.bfloat16),
            jax.ShapeDtypeStruct((quarter, features), jnp.bfloat16),
        ],
        in_specs=[vmem, vmem, vmem, pl.BlockSpec(memory_space=pltpu.HBM), vmem],
        out_specs=[vmem] * 6,
        scratch_shapes=[
            pltpu.VMEM((2 * wanted.shape[0], 128), jnp.int32),
            pltpu.VMEM((2 * wanted.shape[0], 128), jnp.int32),
            pltpu.SemaphoreType.DMA(()),
        ],
        compiler_params=pltpu.CompilerParams(vmem_limit_bytes=24 * MIB),
        cost_estimate=pl.CostEstimate(flops=1 << 31, bytes_accessed=4 * rows * rows, transcendentals=0),
        name="counts",
    )(twin_wanted, wanted, twin, database, adjacent)
    across = [across] + [along(both, apart, apart + 1) for apart in range(2, planes, 2)]
    near = jnp.concatenate([near] + farther, axis=0)
    cut = span // 2
    near = [near[:cut], near[cut:]]
    beside = [cross(piece, (1, 2)) for piece in near]
    behind = [cross(piece, (2, 1)) for piece in near]

    early = pl.pallas_call(
        early_kernel,
        out_shape=jax.ShapeDtypeStruct((2 * rows, features), jnp.float32),
        in_specs=[vmem] * 5,
        out_specs=vmem,
        compiler_params=pltpu.CompilerParams(vmem_limit_bytes=40 * MIB),
        cost_estimate=pl.CostEstimate(flops=1 << 29, bytes_accessed=4 * rows * rows, transcendentals=0),
        name="early_sums",
    )(twin, own, early_counts, *near)

    def late(number, dest):
        return pl.pallas_call(
            functools.partial(late_kernel, number),
            out_shape=jax.ShapeDtypeStruct((rows, features), jnp.float32),
            in_specs=[vmem] * (7 + len(across)),
            out_specs=vmem,
            compiler_params=pltpu.CompilerParams(vmem_limit_bytes=40 * MIB),
            name="late_sums",
        )(dest, early, late_counts, *across, *beside, *behind)

    twin_a = late(0, twin)
    own_b = swap(twin_a)
    own_a = late(1, own)
    twin_b = swap(own_a)

    half = count // 2
    chunks = 4
    augmented, best = pl.pallas_call(
        score_kernel,
        out_shape=[
            jax.ShapeDtypeStruct((rows, features), jnp.bfloat16),
            jax.ShapeDtypeStruct((half // 128, 128), jnp.float32),
        ],
        in_specs=[vmem] * 6 + [pl.BlockSpec(memory_space=pltpu.HBM)],
        out_specs=[vmem, vmem],
        scratch_shapes=[
            pltpu.VMEM((2 * rows, features), jnp.bfloat16),
            pltpu.VMEM((half, features), jnp.bfloat16),
            pltpu.SemaphoreType.DMA((chunks,)),
        ],
        compiler_params=pltpu.CompilerParams(vmem_limit_bytes=40 * MIB),
        cost_estimate=pl.CostEstimate(
            flops=2 * count * rows * features, bytes_accessed=count * features, transcendentals=0
        ),
        name="scores",
    )(own, own_a, own_b, twin, twin_a, twin_b, queries)

    received = [along(best, apart, apart) for apart in range(1, planes)]
    for value in received:
        best = jnp.maximum(best, value)
    other_half = swap(best)
    first = jnp.where(core == 0, best, other_half)
    second = jnp.where(core == 0, other_half, best)
    return augmented, jnp.concatenate([first, second], axis=0).reshape(count)


def solution(mesh):
    return jax.shard_map(
        local,
        mesh=mesh,
        in_specs=(P("db", None), P("db", None), P("db"), P("pb", None)),
        out_specs=(P("db", None), P("pb")),
        check_vma=False,
    )
```

```python
import functools

import jax
import jax.numpy as jnp
from jax import lax
from jax.experimental import pallas as pl
from jax.experimental.pallas import tpu as pltpu
from jax.sharding import PartitionSpec as P

epsilon = 1e-06
MIB = 1 << 20


def column_inverse(values):
    squares = jnp.sum(values * values, axis=-1, keepdims=True)
    return lax.rsqrt(squares + epsilon)


def as_row(column):
    wide = jnp.broadcast_to(column, (column.shape[0], 128))
    return wide.T[0:1, :]


def position_of():
    owner = lax.axis_index("db")
    return lax.axis_index("pb"), owner // 2, owner % 2


def count_kernel(planes, twin_ref, own_ref, database_ref, early_ref, late_ref, copy_ref, tiles_ref, lows_ref, sem):
    rows = copy_ref.shape[0]
    fanout = own_ref.shape[0] * 128 // rows
    quarter = rows // 4
    span = (planes - 1) * quarter
    early_tiles = early_ref.shape[1] // 128
    late_tiles = late_ref.shape[1] // 128
    copy = pltpu.make_async_copy(database_ref, copy_ref, sem)
    copy.start()
    me, plane, core = position_of()
    bits = rows.bit_length() - 1
    lines = own_ref.shape[0]
    for number, wanted_ref in enumerate((twin_ref, own_ref)):
        wanted = wanted_ref[...]
        owner = wanted >> bits
        side = owner & 1
        row = wanted & (rows - 1)
        cross = (row >> (bits - 2)) ^ me
        inner = row & (quarter - 1)
        away = (owner >> 1) ^ plane
        paired = (cross == 3) & (away > 1)
        held = jnp.where(paired, away & 1, side) == core
        straight = (away - 1) * quarter
        crossed = ((away >> 1) * 2 - 1 + (side ^ core)) * quarter
        late = early_tiles * 128 + jnp.where(cross == 3, 0, jnp.where(cross == 1 + core, span, 2 * span))
        position = jnp.where(cross == 0, rows, late) + jnp.where(paired, crossed, straight) + inner
        position = jnp.where(away == 0, row, position)
        position = jnp.where((wanted >= 0) & held, position, -1)
        tiles_ref[number * lines : (number + 1) * lines, :] = position >> 7
        lows_ref[number * lines : (number + 1) * lines, :] = position & 127

    group = 16
    height = (early_tiles + late_tiles) * group
    width = group * fanout
    at_row = lax.broadcasted_iota(jnp.int32, (height, width), 0)
    at_lane = lax.broadcasted_iota(jnp.int32, (height, width), 1)
    target = jnp.where(at_lane // fanout == at_row % group, at_row // group, -2)
    low_of = lax.broadcasted_iota(jnp.int32, (128, width), 0)
    each = width // 128

    def flat(ref, at):
        return jnp.concatenate([ref[pl.ds(at * each + i, 1), :] for i in range(each)], axis=1)

    def body(at, carry):
        tile = jnp.broadcast_to(flat(tiles_ref, at), (height, width))
        low = jnp.broadcast_to(flat(lows_ref, at), (128, width))
        left = jnp.where(tile == target, 1.0, 0.0).astype(jnp.bfloat16)
        right = jnp.where(low == low_of, 1.0, 0.0).astype(jnp.bfloat16)
        counts = lax.dot_general(
            left, right, (((1,), (1,)), ((), ())), preferred_element_type=jnp.float32
        ).astype(jnp.bfloat16)
        start = pl.ds(pl.multiple_of(at * group, group), group)
        for t in range(early_tiles):
            early_ref[start, t * 128 : (t + 1) * 128] = counts[t * group : (t + 1) * group, :]
        for t in range(late_tiles):
            first = (early_tiles + t) * group
            late_ref[start, t * 128 : (t + 1) * 128] = counts[first : first + group, :]
        return carry

    lax.fori_loop(0, 2 * rows // group, body, 0, unroll=4)
    copy.wait()


def join_kernel(own_ref, twin_ref, adjacent_ref, *rest):
    both_ref, across_ref, first_ref, second_ref = rest[-4:]
    quarter = across_ref.shape[0]
    me = position_of()[0]
    at = pl.multiple_of((me ^ 3) * quarter, quarter)
    both_ref[:quarter, :] = own_ref[pl.ds(at, quarter), :]
    both_ref[quarter:, :] = twin_ref[pl.ds(at, quarter), :]
    across_ref[...] = adjacent_ref[quarter:, :]
    near = [adjacent_ref[:quarter, :]] + [ref[...] for ref in rest[:-4]]
    near = jnp.concatenate(near, axis=0)
    cut = first_ref.shape[0]
    first_ref[...] = near[:cut]
    second_ref[...] = near[cut:]


def spread_terms(dest, dest_inverse, block, far, counts):
    products = lax.dot_general(
        dest, block, (((1,), (1,)), ((), ())), preferred_element_type=jnp.float32
    )
    cosine = products * dest_inverse * far
    halfway = (1.0 + cosine) * 0.5
    weight = halfway * halfway * halfway
    coefficient = (weight * far).astype(jnp.bfloat16).astype(jnp.float32)
    spread = coefficient * counts.astype(jnp.float32)
    high = spread.astype(jnp.bfloat16)
    low = (spread - high.astype(jnp.float32)).astype(jnp.bfloat16)
    return jnp.dot(high, block, preferred_element_type=jnp.float32) + jnp.dot(
        low, block, preferred_element_type=jnp.float32
    )


def early_kernel(twin_ref, own_ref, counts_ref, *rest):
    out_ref = rest[-1]
    rows = own_ref.shape[0]
    block = jnp.concatenate([own_ref[...]] + [ref[...] for ref in rest[:-1]], axis=0)
    far = as_row(column_inverse(block.astype(jnp.float32)))
    for number, dest_ref in enumerate((twin_ref, own_ref)):
        lines = slice(number * rows, (number + 1) * rows)
        dest = dest_ref[...]
        dest_inverse = column_inverse(dest.astype(jnp.float32))
        out_ref[lines, :] = spread_terms(dest, dest_inverse, block, far, counts_ref[lines, : block.shape[0]])


def late_kernel(number, dest_ref, early_ref, counts_ref, *rest):
    out_ref = rest[-1]
    rows = dest_ref.shape[0]
    lines = slice(number * rows, (number + 1) * rows)
    block = jnp.concatenate([ref[...] for ref in rest[:-1]], axis=0)
    far = as_row(column_inverse(block.astype(jnp.float32)))
    dest = dest_ref[...]
    dest_inverse = column_inverse(dest.astype(jnp.float32))
    terms = spread_terms(dest, dest_inverse, block, far, counts_ref[lines, : block.shape[0]])
    out_ref[...] = early_ref[lines, :] + terms


def score_kernel(own_ref, own_a_ref, own_b_ref, twin_ref, twin_a_ref, twin_b_ref, queries_ref, augmented_ref, best_ref, rows_ref, held_ref, sems):
    rows = own_ref.shape[0]
    half = held_ref.shape[0]
    chunks = sems.shape[0]
    tile = half // chunks
    core = position_of()[2]

    def fetch(i):
        at = pl.multiple_of(i * tile, tile)
        return pltpu.make_async_copy(
            queries_ref.at[pl.ds(pl.multiple_of(core * half + at, tile), tile), :],
            held_ref.at[pl.ds(at, tile), :],
            sems.at[i],
        )

    for i in range(chunks):
        fetch(i).start()
    parts = ((own_ref, own_a_ref, own_b_ref), (twin_ref, twin_a_ref, twin_b_ref))
    for number, (row_ref, a_ref, b_ref) in enumerate(parts):
        values = row_ref[...].astype(jnp.float32)
        summed = values * column_inverse(values) + (a_ref[...] + b_ref[...])
        augmented = (summed * column_inverse(summed)).astype(jnp.bfloat16)
        if number == 0:
            augmented_ref[...] = augmented
        rows_ref[number * rows : (number + 1) * rows, :] = augmented

    step = 256

    @pl.loop(0, chunks)
    def _(i):
        fetch(i).wait()
        at = pl.multiple_of(i * tile, tile)
        line = pl.multiple_of(i * (tile // 128), tile // 128)
        found = []
        for first in range(0, tile, step):
            scores = lax.dot_general(
                rows_ref[...],
                held_ref[pl.ds(at + first, step), :],
                (((1,), (1,)), ((), ())),
                preferred_element_type=jnp.float32,
            )
            best = jnp.max(scores, axis=0, keepdims=True)
            found += [best[:, part : part + 128] for part in range(0, step, 128)]
        best_ref[pl.ds(line, tile // 128), :] = jnp.concatenate(found, axis=0)


def local(database, neighbours, valid_count, queries):
    rows, features = database.shape
    fanout = neighbours.shape[1]
    count = queries.shape[0]
    owners = lax.axis_size("db")
    panels = lax.axis_size("pb")
    assert panels == 4 and owners % 4 == 0 and owners & (owners - 1) == 0
    planes = owners // 2
    quarter = rows // panels
    me = lax.axis_index("pb")
    core = lax.axis_index("db") % 2

    def along(value, even, odd):
        apart = (even, odd)
        pairs = [(i, ((i // 2) ^ apart[i % 2]) * 2 + i % 2) for i in range(owners)]
        return lax.ppermute(value, "db", pairs)

    def swap(value):
        return lax.ppermute(value, "db", [(i, i ^ 1) for i in range(owners)])

    def cross(value, bits):
        pairs = []
        for panel in range(panels):
            for i in range(owners):
                pairs.append((panel * owners + i, (panel ^ bits[i % 2]) * owners + i))
        return lax.ppermute(value, ("pb", "db"), pairs)

    mine = lax.dynamic_slice_in_dim(database, me * quarter, quarter, 0)
    other = lax.dynamic_slice_in_dim(database, (me ^ 3) * quarter, quarter, 0)
    adjacent = along(jnp.concatenate([mine, other], axis=0), 1, 1)
    farther = [along(mine, apart, apart) for apart in range(2, planes)]
    twin = swap(database)
    vmem = pl.BlockSpec(memory_space=pltpu.VMEM)
    slots = jnp.arange(fanout, dtype=jnp.int32)[None, :]
    wanted = jnp.where(slots < valid_count[:, None], neighbours, -1).reshape(-1, 128)
    twin_wanted = swap(wanted)
    padded = lambda size: (size + 127) // 128 * 128
    span = (planes - 1) * quarter
    early_counts, late_counts, own = pl.pallas_call(
        functools.partial(count_kernel, planes),
        out_shape=[
            jax.ShapeDtypeStruct((2 * rows, padded(rows + span)), jnp.bfloat16),
            jax.ShapeDtypeStruct((2 * rows, padded(3 * span)), jnp.bfloat16),
            jax.ShapeDtypeStruct((rows, features), jnp.bfloat16),
        ],
        in_specs=[vmem, vmem, pl.BlockSpec(memory_space=pltpu.HBM)],
        out_specs=[vmem] * 3,
        scratch_shapes=[
            pltpu.VMEM((2 * wanted.shape[0], 128), jnp.int32),
            pltpu.VMEM((2 * wanted.shape[0], 128), jnp.int32),
            pltpu.SemaphoreType.DMA(()),
        ],
        compiler_params=pltpu.CompilerParams(vmem_limit_bytes=24 * MIB),
        cost_estimate=pl.CostEstimate(flops=1 << 26, bytes_accessed=4 * rows * rows, transcendentals=0),
        name="counts",
    )(twin_wanted, wanted, database)
    piece = lambda height: jax.ShapeDtypeStruct((height, features), jnp.bfloat16)
    both, across, *near = pl.pallas_call(
        join_kernel,
        out_shape=[piece(2 * quarter), piece(quarter), piece(span // 2), piece(span // 2)],
        in_specs=[vmem] * (3 + len(farther)),
        out_specs=[vmem] * 4,
        compiler_params=pltpu.CompilerParams(vmem_limit_bytes=8 * MIB),
        name="join",
    )(own, twin, adjacent, *farther)
    across = [across] + [along(both, apart, apart + 1) for apart in range(2, planes, 2)]
    beside = [cross(part, (1, 2)) for part in near]
    behind = [cross(part, (2, 1)) for part in near]

    early = pl.pallas_call(
        early_kernel,
        out_shape=jax.ShapeDtypeStruct((2 * rows, features), jnp.float32),
        in_specs=[vmem] * 5,
        out_specs=vmem,
        compiler_params=pltpu.CompilerParams(vmem_limit_bytes=40 * MIB),
        cost_estimate=pl.CostEstimate(flops=1 << 26, bytes_accessed=4 * rows * rows, transcendentals=0),
        name="early_sums",
    )(twin, own, early_counts, *near)

    def late(number, dest):
        return pl.pallas_call(
            functools.partial(late_kernel, number),
            out_shape=jax.ShapeDtypeStruct((rows, features), jnp.float32),
            in_specs=[vmem] * (7 + len(across)),
            out_specs=vmem,
            compiler_params=pltpu.CompilerParams(vmem_limit_bytes=40 * MIB),
            name="late_sums",
        )(dest, early, late_counts, *across, *beside, *behind)

    twin_a = late(0, twin)
    own_b = swap(twin_a)
    own_a = late(1, own)
    twin_b = swap(own_a)

    half = count // 2
    chunks = 4
    augmented, best = pl.pallas_call(
        score_kernel,
        out_shape=[
            jax.ShapeDtypeStruct((rows, features), jnp.bfloat16),
            jax.ShapeDtypeStruct((half // 128, 128), jnp.float32),
        ],
        in_specs=[vmem] * 6 + [pl.BlockSpec(memory_space=pltpu.HBM)],
        out_specs=[vmem, vmem],
        scratch_shapes=[
            pltpu.VMEM((2 * rows, features), jnp.bfloat16),
            pltpu.VMEM((half, features), jnp.bfloat16),
            pltpu.SemaphoreType.DMA((chunks,)),
        ],
        compiler_params=pltpu.CompilerParams(vmem_limit_bytes=40 * MIB),
        cost_estimate=pl.CostEstimate(
            flops=2 * count * rows * features, bytes_accessed=count * features, transcendentals=0
        ),
        name="scores",
    )(own, own_a, own_b, twin, twin_a, twin_b, queries)

    received = [along(best, apart, apart) for apart in range(1, planes)]
    for value in received:
        best = jnp.maximum(best, value)
    other_half = swap(best)
    first = jnp.where(core == 0, best, other_half)
    second = jnp.where(core == 0, other_half, best)
    return augmented, jnp.concatenate([first, second], axis=0).reshape(count)


def solution(mesh):
    return jax.shard_map(
        local,
        mesh=mesh,
        in_specs=(P("db", None), P("db", None), P("db"), P("pb", None)),
        out_specs=(P("db", None), P("pb")),
        check_vma=False,
    )
```

```python
import functools

import jax
import jax.numpy as jnp
from jax import lax
from jax.experimental import pallas as pl
from jax.experimental.pallas import tpu as pltpu
from jax.sharding import PartitionSpec as P

epsilon = 1e-06
MIB = 1 << 20


def column_inverse(values):
    squares = jnp.sum(values * values, axis=-1, keepdims=True)
    return lax.rsqrt(squares + epsilon)


def as_row(column):
    wide = jnp.broadcast_to(column, (column.shape[0], 128))
    return wide.T[0:1, :]


def position_of():
    owner = lax.axis_index("db")
    return lax.axis_index("pb"), owner // 2, owner % 2


def count_kernel(planes, twin_ref, own_ref, database_ref, early_ref, middle_ref, late_ref, copy_ref, tiles_ref, lows_ref, sem):
    rows = copy_ref.shape[0]
    fanout = own_ref.shape[0] * 128 // rows
    quarter = rows // 4
    span = (planes - 1) * quarter
    early_tiles = early_ref.shape[1] // 128
    middle_tiles = middle_ref.shape[1] // 128
    late_tiles = late_ref.shape[1] // 128
    cut = span // 2
    copy = pltpu.make_async_copy(database_ref, copy_ref, sem)
    copy.start()
    me, plane, core = position_of()
    bits = rows.bit_length() - 1
    lines = own_ref.shape[0]
    for number, wanted_ref in enumerate((twin_ref, own_ref)):
        wanted = wanted_ref[...]
        owner = wanted >> bits
        side = owner & 1
        row = wanted & (rows - 1)
        cross = (row >> (bits - 2)) ^ me
        inner = row & (quarter - 1)
        away = (owner >> 1) ^ plane
        paired = (cross == 3) & (away > 1)
        held = jnp.where(paired, away & 1, side) == core
        straight = (away - 1) * quarter
        crossed = ((away >> 1) * 2 - 1 + (side ^ core)) * quarter
        middle = early_tiles * 128
        late = middle + middle_tiles * 128
        straight = straight + inner
        crossed = crossed + inner
        second = jnp.where(cross == 1 + core, 0, cut)
        forwarded = straight + second + jnp.where(straight < cut, middle, late + span - cut)
        position = jnp.where(cross == 3, late + jnp.where(paired, crossed, straight), forwarded)
        position = jnp.where(cross == 0, rows + straight, position)
        position = jnp.where(away == 0, row, position)
        position = jnp.where((wanted >= 0) & held, position, -1)
        tiles_ref[number * lines : (number + 1) * lines, :] = position >> 7
        lows_ref[number * lines : (number + 1) * lines, :] = position & 127

    group = 16
    height = (early_tiles + middle_tiles + late_tiles) * group
    width = group * fanout
    at_row = lax.broadcasted_iota(jnp.int32, (height, width), 0)
    at_lane = lax.broadcasted_iota(jnp.int32, (height, width), 1)
    target = jnp.where(at_lane // fanout == at_row % group, at_row // group, -2)
    low_of = lax.broadcasted_iota(jnp.int32, (128, width), 0)
    each = width // 128

    def flat(ref, at):
        return jnp.concatenate([ref[pl.ds(at * each + i, 1), :] for i in range(each)], axis=1)

    def body(at, carry):
        tile = jnp.broadcast_to(flat(tiles_ref, at), (height, width))
        low = jnp.broadcast_to(flat(lows_ref, at), (128, width))
        left = jnp.where(tile == target, 1.0, 0.0).astype(jnp.bfloat16)
        right = jnp.where(low == low_of, 1.0, 0.0).astype(jnp.bfloat16)
        counts = lax.dot_general(
            left, right, (((1,), (1,)), ((), ())), preferred_element_type=jnp.float32
        ).astype(jnp.bfloat16)
        start = pl.ds(pl.multiple_of(at * group, group), group)
        tile = 0
        for count_ref in (early_ref, middle_ref, late_ref):
            for t in range(count_ref.shape[1] // 128):
                count_ref[start, t * 128 : (t + 1) * 128] = counts[tile * group : (tile + 1) * group, :]
                tile += 1
        return carry

    lax.fori_loop(0, 2 * rows // group, body, 0, unroll=4)
    copy.wait()


def join_kernel(own_ref, twin_ref, adjacent_ref, *rest):
    both_ref, across_ref, first_ref, second_ref = rest[-4:]
    quarter = across_ref.shape[0]
    me = position_of()[0]
    at = pl.multiple_of((me ^ 3) * quarter, quarter)
    both_ref[:quarter, :] = own_ref[pl.ds(at, quarter), :]
    both_ref[quarter:, :] = twin_ref[pl.ds(at, quarter), :]
    across_ref[...] = adjacent_ref[quarter:, :]
    near = [adjacent_ref[:quarter, :]] + [ref[...] for ref in rest[:-4]]
    near = jnp.concatenate(near, axis=0)
    cut = first_ref.shape[0]
    first_ref[...] = near[:cut]
    second_ref[...] = near[cut:]


def spread_terms(dest, dest_inverse, block, far, counts):
    products = lax.dot_general(
        dest, block, (((1,), (1,)), ((), ())), preferred_element_type=jnp.float32
    )
    cosine = products * dest_inverse * far
    halfway = (1.0 + cosine) * 0.5
    weight = halfway * halfway * halfway
    coefficient = (weight * far).astype(jnp.bfloat16).astype(jnp.float32)
    spread = coefficient * counts.astype(jnp.float32)
    high = spread.astype(jnp.bfloat16)
    low = (spread - high.astype(jnp.float32)).astype(jnp.bfloat16)
    return jnp.dot(high, block, preferred_element_type=jnp.float32) + jnp.dot(
        low, block, preferred_element_type=jnp.float32
    )


def early_kernel(twin_ref, own_ref, counts_ref, *rest):
    out_ref = rest[-1]
    rows = own_ref.shape[0]
    block = jnp.concatenate([own_ref[...]] + [ref[...] for ref in rest[:-1]], axis=0)
    far = as_row(column_inverse(block.astype(jnp.float32)))
    for number, dest_ref in enumerate((twin_ref, own_ref)):
        lines = slice(number * rows, (number + 1) * rows)
        dest = dest_ref[...]
        values = dest.astype(jnp.float32)
        dest_inverse = column_inverse(values)
        terms = spread_terms(dest, dest_inverse, block, far, counts_ref[lines, : block.shape[0]])
        if number == 1:
            terms = terms + values * dest_inverse
        out_ref[lines, :] = terms


def middle_kernel(twin_ref, own_ref, early_ref, counts_ref, beside_ref, behind_ref, out_ref):
    rows = own_ref.shape[0]
    block = jnp.concatenate([beside_ref[...], behind_ref[...]], axis=0)
    far = as_row(column_inverse(block.astype(jnp.float32)))
    for number, dest_ref in enumerate((twin_ref, own_ref)):
        lines = slice(number * rows, (number + 1) * rows)
        dest = dest_ref[...]
        dest_inverse = column_inverse(dest.astype(jnp.float32))
        terms = spread_terms(dest, dest_inverse, block, far, counts_ref[lines, : block.shape[0]])
        out_ref[lines, :] = early_ref[lines, :] + terms


def late_kernel(number, dest_ref, early_ref, counts_ref, *rest):
    out_ref = rest[-1]
    rows = dest_ref.shape[0]
    lines = slice(number * rows, (number + 1) * rows)
    block = jnp.concatenate([ref[...] for ref in rest[:-1]], axis=0)
    far = as_row(column_inverse(block.astype(jnp.float32)))
    dest = dest_ref[...]
    dest_inverse = column_inverse(dest.astype(jnp.float32))
    terms = spread_terms(dest, dest_inverse, block, far, counts_ref[lines, : block.shape[0]])
    out_ref[...] = early_ref[lines, :] + terms


def score_kernel(own_a_ref, own_b_ref, twin_a_ref, twin_b_ref, queries_ref, augmented_ref, best_ref, rows_ref, held_ref, sems):
    rows = own_a_ref.shape[0]
    half = held_ref.shape[0]
    chunks = sems.shape[0]
    tile = half // chunks
    core = position_of()[2]

    def fetch(i):
        at = pl.multiple_of(i * tile, tile)
        return pltpu.make_async_copy(
            queries_ref.at[pl.ds(pl.multiple_of(core * half + at, tile), tile), :],
            held_ref.at[pl.ds(at, tile), :],
            sems.at[i],
        )

    for i in range(chunks):
        fetch(i).start()
    for number, (a_ref, b_ref) in enumerate(((own_a_ref, own_b_ref), (twin_a_ref, twin_b_ref))):
        summed = a_ref[...] + b_ref[...]
        augmented = (summed * column_inverse(summed)).astype(jnp.bfloat16)
        if number == 0:
            augmented_ref[...] = augmented
        rows_ref[number * rows : (number + 1) * rows, :] = augmented

    step = min(1024, tile)

    @pl.loop(0, chunks)
    def _(i):
        fetch(i).wait()
        at = pl.multiple_of(i * tile, tile)
        line = pl.multiple_of(i * (tile // 128), tile // 128)
        found = []
        for first in range(0, tile, step):
            scores = lax.dot_general(
                rows_ref[...],
                held_ref[pl.ds(at + first, step), :],
                (((1,), (1,)), ((), ())),
                preferred_element_type=jnp.float32,
            )
            best = jnp.max(scores, axis=0, keepdims=True)
            found += [best[:, part : part + 128] for part in range(0, step, 128)]
        best_ref[pl.ds(line, tile // 128), :] = jnp.concatenate(found, axis=0)


def local(database, neighbours, valid_count, queries):
    rows, features = database.shape
    fanout = neighbours.shape[1]
    count = queries.shape[0]
    owners = lax.axis_size("db")
    panels = lax.axis_size("pb")
    assert panels == 4 and owners % 4 == 0 and owners & (owners - 1) == 0
    planes = owners // 2
    quarter = rows // panels
    me = lax.axis_index("pb")
    core = lax.axis_index("db") % 2

    def along(value, even, odd):
        apart = (even, odd)
        pairs = [(i, ((i // 2) ^ apart[i % 2]) * 2 + i % 2) for i in range(owners)]
        return lax.ppermute(value, "db", pairs)

    def swap(value):
        return lax.ppermute(value, "db", [(i, i ^ 1) for i in range(owners)])

    def cross(value, bits):
        pairs = []
        for panel in range(panels):
            for i in range(owners):
                pairs.append((panel * owners + i, (panel ^ bits[i % 2]) * owners + i))
        return lax.ppermute(value, ("pb", "db"), pairs)

    mine = lax.dynamic_slice_in_dim(database, me * quarter, quarter, 0)
    other = lax.dynamic_slice_in_dim(database, (me ^ 3) * quarter, quarter, 0)
    adjacent = along(jnp.concatenate([mine, other], axis=0), 1, 1)
    farther = [along(mine, apart, apart) for apart in range(2, planes)]
    twin = swap(database)
    vmem = pl.BlockSpec(memory_space=pltpu.VMEM)
    slots = jnp.arange(fanout, dtype=jnp.int32)[None, :]
    wanted = jnp.where(slots < valid_count[:, None], neighbours, -1).reshape(-1, 128)
    twin_wanted = swap(wanted)
    padded = lambda size: (size + 127) // 128 * 128
    span = (planes - 1) * quarter
    early_counts, middle_counts, late_counts, own = pl.pallas_call(
        functools.partial(count_kernel, planes),
        out_shape=[
            jax.ShapeDtypeStruct((2 * rows, padded(rows + span)), jnp.bfloat16),
            jax.ShapeDtypeStruct((2 * rows, padded(span)), jnp.bfloat16),
            jax.ShapeDtypeStruct((2 * rows, padded(2 * span)), jnp.bfloat16),
            jax.ShapeDtypeStruct((rows, features), jnp.bfloat16),
        ],
        in_specs=[vmem, vmem, pl.BlockSpec(memory_space=pltpu.HBM)],
        out_specs=[vmem] * 4,
        scratch_shapes=[
            pltpu.VMEM((2 * wanted.shape[0], 128), jnp.int32),
            pltpu.VMEM((2 * wanted.shape[0], 128), jnp.int32),
            pltpu.SemaphoreType.DMA(()),
        ],
        compiler_params=pltpu.CompilerParams(vmem_limit_bytes=24 * MIB),
        cost_estimate=pl.CostEstimate(flops=1 << 26, bytes_accessed=4 * rows * rows, transcendentals=0),
        name="counts",
    )(twin_wanted, wanted, database)
    piece = lambda height: jax.ShapeDtypeStruct((height, features), jnp.bfloat16)
    both, across, *near = pl.pallas_call(
        join_kernel,
        out_shape=[piece(2 * quarter), piece(quarter), piece(span // 2), piece(span // 2)],
        in_specs=[vmem] * (3 + len(farther)),
        out_specs=[vmem] * 4,
        compiler_params=pltpu.CompilerParams(vmem_limit_bytes=8 * MIB),
        name="join",
    )(own, twin, adjacent, *farther)
    across = [across] + [along(both, apart, apart + 1) for apart in range(2, planes, 2)]
    beside = [cross(part, (1, 2)) for part in near]
    behind = [cross(part, (2, 1)) for part in near]

    early = pl.pallas_call(
        early_kernel,
        out_shape=jax.ShapeDtypeStruct((2 * rows, features), jnp.float32),
        in_specs=[vmem] * 5,
        out_specs=vmem,
        compiler_params=pltpu.CompilerParams(vmem_limit_bytes=40 * MIB),
        cost_estimate=pl.CostEstimate(flops=1 << 26, bytes_accessed=4 * rows * rows, transcendentals=0),
        name="early_sums",
    )(twin, own, early_counts, *near)

    middle = pl.pallas_call(
        middle_kernel,
        out_shape=jax.ShapeDtypeStruct((2 * rows, features), jnp.float32),
        in_specs=[vmem] * 6,
        out_specs=vmem,
        compiler_params=pltpu.CompilerParams(vmem_limit_bytes=40 * MIB),
        cost_estimate=pl.CostEstimate(flops=1 << 26, bytes_accessed=4 * rows * rows, transcendentals=0),
        name="middle_sums",
    )(twin, own, early, middle_counts, beside[0], behind[0])

    def late(number, dest):
        return pl.pallas_call(
            functools.partial(late_kernel, number),
            out_shape=jax.ShapeDtypeStruct((rows, features), jnp.float32),
            in_specs=[vmem] * (5 + len(across)),
            out_specs=vmem,
            compiler_params=pltpu.CompilerParams(vmem_limit_bytes=40 * MIB),
            name="late_sums",
        )(dest, middle, late_counts, *across, beside[1], behind[1])

    twin_a = late(0, twin)
    own_b = swap(twin_a)
    own_a = late(1, own)
    twin_b = swap(own_a)

    half = count // 2
    chunks = 4
    augmented, best = pl.pallas_call(
        score_kernel,
        out_shape=[
            jax.ShapeDtypeStruct((rows, features), jnp.bfloat16),
            jax.ShapeDtypeStruct((half // 128, 128), jnp.float32),
        ],
        in_specs=[vmem] * 4 + [pl.BlockSpec(memory_space=pltpu.HBM)],
        out_specs=[vmem, vmem],
        scratch_shapes=[
            pltpu.VMEM((2 * rows, features), jnp.bfloat16),
            pltpu.VMEM((half, features), jnp.bfloat16),
            pltpu.SemaphoreType.DMA((chunks,)),
        ],
        compiler_params=pltpu.CompilerParams(vmem_limit_bytes=40 * MIB),
        cost_estimate=pl.CostEstimate(
            flops=2 * count * rows * features, bytes_accessed=count * features, transcendentals=0
        ),
        name="scores",
    )(own_a, own_b, twin_a, twin_b, queries)

    received = [along(best, apart, apart) for apart in range(1, planes)]
    for value in received:
        best = jnp.maximum(best, value)
    other_half = swap(best)
    first = jnp.where(core == 0, best, other_half)
    second = jnp.where(core == 0, other_half, best)
    return augmented, jnp.concatenate([first, second], axis=0).reshape(count)


def solution(mesh):
    return jax.shard_map(
        local,
        mesh=mesh,
        in_specs=(P("db", None), P("db", None), P("db"), P("pb", None)),
        out_specs=(P("db", None), P("pb")),
        check_vma=False,
    )
```

```python
import functools

import jax
import jax.numpy as jnp
from jax import lax
from jax.experimental import pallas as pl
from jax.experimental.pallas import tpu as pltpu
from jax.sharding import PartitionSpec as P

epsilon = 1e-06
MIB = 1 << 20


def column_inverse(values):
    squares = jnp.sum(values * values, axis=-1, keepdims=True)
    return lax.rsqrt(squares + epsilon)


def as_row(column):
    wide = jnp.broadcast_to(column, (column.shape[0], 128))
    return wide.T[0:1, :]


def position_of():
    owner = lax.axis_index("db")
    return lax.axis_index("pb"), owner // 2, owner % 2


def fetch_queries(queries_ref, held_ref, part, sem):
    rows = held_ref.shape[0]
    core = position_of()[2]
    start = pl.multiple_of((core * 2 + part) * rows, rows)
    return pltpu.make_async_copy(queries_ref.at[pl.ds(start, rows), :], held_ref, sem)


def count_kernel(
    planes, twin_ref, own_ref, database_ref, queries_ref, early_ref, middle_ref, late_ref, copy_ref, held_ref,
    tiles_ref, lows_ref, sem, queries_sem,
):
    rows = copy_ref.shape[0]
    fanout = own_ref.shape[0] * 128 // rows
    quarter = rows // 4
    span = (planes - 1) * quarter
    early_tiles = early_ref.shape[1] // 128
    middle_tiles = middle_ref.shape[1] // 128
    late_tiles = late_ref.shape[1] // 128
    cut = span // 2
    copy = pltpu.make_async_copy(database_ref, copy_ref, sem)
    copy.start()
    queries = fetch_queries(queries_ref, held_ref, 0, queries_sem)
    queries.start()
    me, plane, core = position_of()
    bits = rows.bit_length() - 1
    lines = own_ref.shape[0]
    for number, wanted_ref in enumerate((twin_ref, own_ref)):
        wanted = wanted_ref[...]
        owner = wanted >> bits
        side = owner & 1
        row = wanted & (rows - 1)
        cross = (row >> (bits - 2)) ^ me
        inner = row & (quarter - 1)
        away = (owner >> 1) ^ plane
        paired = (cross == 3) & (away > 1)
        held = jnp.where(paired, away & 1, side) == core
        straight = (away - 1) * quarter
        crossed = ((away >> 1) * 2 - 1 + (side ^ core)) * quarter
        middle = early_tiles * 128
        late = middle + middle_tiles * 128
        straight = straight + inner
        crossed = crossed + inner
        second = jnp.where(cross == 1 + core, 0, cut)
        forwarded = straight + second + jnp.where(straight < cut, middle, late + span - cut)
        position = jnp.where(cross == 3, late + jnp.where(paired, crossed, straight), forwarded)
        position = jnp.where(cross == 0, rows + straight, position)
        position = jnp.where(away == 0, row, position)
        position = jnp.where((wanted >= 0) & held, position, -1)
        tiles_ref[number * lines : (number + 1) * lines, :] = position >> 7
        lows_ref[number * lines : (number + 1) * lines, :] = position & 127

    group = 16
    height = (early_tiles + middle_tiles + late_tiles) * group
    width = group * fanout
    at_row = lax.broadcasted_iota(jnp.int32, (height, width), 0)
    at_lane = lax.broadcasted_iota(jnp.int32, (height, width), 1)
    target = jnp.where(at_lane // fanout == at_row % group, at_row // group, -2)
    low_of = lax.broadcasted_iota(jnp.int32, (128, width), 0)
    each = width // 128

    def flat(ref, at):
        return jnp.concatenate([ref[pl.ds(at * each + i, 1), :] for i in range(each)], axis=1)

    def body(at, carry):
        tile = jnp.broadcast_to(flat(tiles_ref, at), (height, width))
        low = jnp.broadcast_to(flat(lows_ref, at), (128, width))
        left = jnp.where(tile == target, 1.0, 0.0).astype(jnp.bfloat16)
        right = jnp.where(low == low_of, 1.0, 0.0).astype(jnp.bfloat16)
        counts = lax.dot_general(
            left, right, (((1,), (1,)), ((), ())), preferred_element_type=jnp.float32
        ).astype(jnp.bfloat16)
        start = pl.ds(pl.multiple_of(at * group, group), group)
        tile = 0
        for count_ref in (early_ref, middle_ref, late_ref):
            for t in range(count_ref.shape[1] // 128):
                count_ref[start, t * 128 : (t + 1) * 128] = counts[tile * group : (tile + 1) * group, :]
                tile += 1
        return carry

    lax.fori_loop(0, 2 * rows // group, body, 0, unroll=4)
    copy.wait()
    queries.wait()


def join_kernel(own_ref, twin_ref, adjacent_ref, *rest):
    both_ref, across_ref, first_ref, second_ref = rest[-4:]
    quarter = across_ref.shape[0]
    me = position_of()[0]
    at = pl.multiple_of((me ^ 3) * quarter, quarter)
    both_ref[:quarter, :] = own_ref[pl.ds(at, quarter), :]
    both_ref[quarter:, :] = twin_ref[pl.ds(at, quarter), :]
    across_ref[...] = adjacent_ref[quarter:, :]
    near = [adjacent_ref[:quarter, :]] + [ref[...] for ref in rest[:-4]]
    near = jnp.concatenate(near, axis=0)
    cut = first_ref.shape[0]
    first_ref[...] = near[:cut]
    second_ref[...] = near[cut:]


def spread_terms(dest, dest_inverse, block, far, counts):
    products = lax.dot_general(
        dest, block, (((1,), (1,)), ((), ())), preferred_element_type=jnp.float32
    )
    cosine = products * dest_inverse * far
    halfway = (1.0 + cosine) * 0.5
    weight = halfway * halfway * halfway
    coefficient = (weight * far).astype(jnp.bfloat16).astype(jnp.float32)
    spread = coefficient * counts.astype(jnp.float32)
    high = spread.astype(jnp.bfloat16)
    low = (spread - high.astype(jnp.float32)).astype(jnp.bfloat16)
    return jnp.dot(high, block, preferred_element_type=jnp.float32) + jnp.dot(
        low, block, preferred_element_type=jnp.float32
    )


def early_kernel(queries_ref, twin_ref, own_ref, counts_ref, *rest):
    out_ref, held_ref, sem = rest[-3:]
    queries = fetch_queries(queries_ref, held_ref, 1, sem)
    queries.start()
    rows = own_ref.shape[0]
    block = jnp.concatenate([own_ref[...]] + [ref[...] for ref in rest[:-3]], axis=0)
    far = as_row(column_inverse(block.astype(jnp.float32)))
    for number, dest_ref in enumerate((twin_ref, own_ref)):
        lines = slice(number * rows, (number + 1) * rows)
        dest = dest_ref[...]
        values = dest.astype(jnp.float32)
        dest_inverse = column_inverse(values)
        terms = spread_terms(dest, dest_inverse, block, far, counts_ref[lines, : block.shape[0]])
        if number == 1:
            terms = terms + values * dest_inverse
        out_ref[lines, :] = terms
    queries.wait()


def middle_kernel(twin_ref, own_ref, early_ref, counts_ref, beside_ref, behind_ref, out_ref):
    rows = own_ref.shape[0]
    block = jnp.concatenate([beside_ref[...], behind_ref[...]], axis=0)
    far = as_row(column_inverse(block.astype(jnp.float32)))
    for number, dest_ref in enumerate((twin_ref, own_ref)):
        lines = slice(number * rows, (number + 1) * rows)
        dest = dest_ref[...]
        dest_inverse = column_inverse(dest.astype(jnp.float32))
        terms = spread_terms(dest, dest_inverse, block, far, counts_ref[lines, : block.shape[0]])
        out_ref[lines, :] = early_ref[lines, :] + terms


def late_kernel(number, dest_ref, early_ref, counts_ref, *rest):
    out_ref = rest[-1]
    rows = dest_ref.shape[0]
    lines = slice(number * rows, (number + 1) * rows)
    block = jnp.concatenate([ref[...] for ref in rest[:-1]], axis=0)
    far = as_row(column_inverse(block.astype(jnp.float32)))
    dest = dest_ref[...]
    dest_inverse = column_inverse(dest.astype(jnp.float32))
    terms = spread_terms(dest, dest_inverse, block, far, counts_ref[lines, : block.shape[0]])
    out_ref[...] = early_ref[lines, :] + terms


def score_kernel(own_a_ref, own_b_ref, twin_a_ref, twin_b_ref, first_ref, second_ref, augmented_ref, best_ref, rows_ref):
    rows = own_a_ref.shape[0]
    for number, (a_ref, b_ref) in enumerate(((own_a_ref, own_b_ref), (twin_a_ref, twin_b_ref))):
        summed = a_ref[...] + b_ref[...]
        augmented = (summed * column_inverse(summed)).astype(jnp.bfloat16)
        if number == 0:
            augmented_ref[...] = augmented
        rows_ref[number * rows : (number + 1) * rows, :] = augmented

    height = first_ref.shape[0]
    step = min(1024, height)
    tile = min(2048, height)
    for number, held_ref in enumerate((first_ref, second_ref)):

        @pl.loop(0, height // tile)
        def _(i):
            at = pl.multiple_of(i * tile, tile)
            line = pl.multiple_of(number * (height // 128) + i * (tile // 128), tile // 128)
            found = []
            for first in range(0, tile, step):
                scores = lax.dot_general(
                    rows_ref[...],
                    held_ref[pl.ds(at + first, step), :],
                    (((1,), (1,)), ((), ())),
                    preferred_element_type=jnp.float32,
                )
                best = jnp.max(scores, axis=0, keepdims=True)
                found += [best[:, part : part + 128] for part in range(0, step, 128)]
            best_ref[pl.ds(line, tile // 128), :] = jnp.concatenate(found, axis=0)


def local(database, neighbours, valid_count, queries):
    rows, features = database.shape
    fanout = neighbours.shape[1]
    count = queries.shape[0]
    owners = lax.axis_size("db")
    panels = lax.axis_size("pb")
    assert panels == 4 and owners % 4 == 0 and owners & (owners - 1) == 0
    planes = owners // 2
    quarter = rows // panels
    me = lax.axis_index("pb")
    core = lax.axis_index("db") % 2

    def along(value, even, odd):
        apart = (even, odd)
        pairs = [(i, ((i // 2) ^ apart[i % 2]) * 2 + i % 2) for i in range(owners)]
        return lax.ppermute(value, "db", pairs)

    def swap(value):
        return lax.ppermute(value, "db", [(i, i ^ 1) for i in range(owners)])

    def cross(value, bits):
        pairs = []
        for panel in range(panels):
            for i in range(owners):
                pairs.append((panel * owners + i, (panel ^ bits[i % 2]) * owners + i))
        return lax.ppermute(value, ("pb", "db"), pairs)

    mine = lax.dynamic_slice_in_dim(database, me * quarter, quarter, 0)
    other = lax.dynamic_slice_in_dim(database, (me ^ 3) * quarter, quarter, 0)
    adjacent = along(jnp.concatenate([mine, other], axis=0), 1, 1)
    farther = [along(mine, apart, apart) for apart in range(2, planes)]
    twin = swap(database)
    vmem = pl.BlockSpec(memory_space=pltpu.VMEM)
    slots = jnp.arange(fanout, dtype=jnp.int32)[None, :]
    wanted = jnp.where(slots < valid_count[:, None], neighbours, -1).reshape(-1, 128)
    twin_wanted = swap(wanted)
    padded = lambda size: (size + 127) // 128 * 128
    span = (planes - 1) * quarter
    early_counts, middle_counts, late_counts, own, first_queries = pl.pallas_call(
        functools.partial(count_kernel, planes),
        out_shape=[
            jax.ShapeDtypeStruct((2 * rows, padded(rows + span)), jnp.bfloat16),
            jax.ShapeDtypeStruct((2 * rows, padded(span)), jnp.bfloat16),
            jax.ShapeDtypeStruct((2 * rows, padded(2 * span)), jnp.bfloat16),
            jax.ShapeDtypeStruct((rows, features), jnp.bfloat16),
            jax.ShapeDtypeStruct((count // 4, features), jnp.bfloat16),
        ],
        in_specs=[vmem, vmem] + [pl.BlockSpec(memory_space=pltpu.HBM)] * 2,
        out_specs=[vmem] * 5,
        scratch_shapes=[
            pltpu.VMEM((2 * wanted.shape[0], 128), jnp.int32),
            pltpu.VMEM((2 * wanted.shape[0], 128), jnp.int32),
            pltpu.SemaphoreType.DMA(()),
            pltpu.SemaphoreType.DMA(()),
        ],
        compiler_params=pltpu.CompilerParams(vmem_limit_bytes=30 * MIB),
        cost_estimate=pl.CostEstimate(flops=1 << 26, bytes_accessed=4 * rows * rows, transcendentals=0),
        name="counts",
    )(twin_wanted, wanted, database, queries)
    piece = lambda height: jax.ShapeDtypeStruct((height, features), jnp.bfloat16)
    both, across, *near = pl.pallas_call(
        join_kernel,
        out_shape=[piece(2 * quarter), piece(quarter), piece(span // 2), piece(span // 2)],
        in_specs=[vmem] * (3 + len(farther)),
        out_specs=[vmem] * 4,
        compiler_params=pltpu.CompilerParams(vmem_limit_bytes=8 * MIB),
        name="join",
    )(own, twin, adjacent, *farther)
    across = [across] + [along(both, apart, apart + 1) for apart in range(2, planes, 2)]
    beside = [cross(part, (1, 2)) for part in near]
    behind = [cross(part, (2, 1)) for part in near]

    early, second_queries = pl.pallas_call(
        early_kernel,
        out_shape=[
            jax.ShapeDtypeStruct((2 * rows, features), jnp.float32),
            jax.ShapeDtypeStruct((count // 4, features), jnp.bfloat16),
        ],
        in_specs=[pl.BlockSpec(memory_space=pltpu.HBM)] + [vmem] * 5,
        out_specs=[vmem] * 2,
        scratch_shapes=[pltpu.SemaphoreType.DMA(())],
        compiler_params=pltpu.CompilerParams(vmem_limit_bytes=30 * MIB),
        cost_estimate=pl.CostEstimate(flops=1 << 26, bytes_accessed=4 * rows * rows, transcendentals=0),
        name="early_sums",
    )(queries, twin, own, early_counts, *near)

    middle = pl.pallas_call(
        middle_kernel,
        out_shape=jax.ShapeDtypeStruct((2 * rows, features), jnp.float32),
        in_specs=[vmem] * 6,
        out_specs=vmem,
        compiler_params=pltpu.CompilerParams(vmem_limit_bytes=30 * MIB),
        cost_estimate=pl.CostEstimate(flops=1 << 26, bytes_accessed=4 * rows * rows, transcendentals=0),
        name="middle_sums",
    )(twin, own, early, middle_counts, beside[0], behind[0])

    def late(number, dest):
        return pl.pallas_call(
            functools.partial(late_kernel, number),
            out_shape=jax.ShapeDtypeStruct((rows, features), jnp.float32),
            in_specs=[vmem] * (5 + len(across)),
            out_specs=vmem,
            compiler_params=pltpu.CompilerParams(vmem_limit_bytes=30 * MIB),
            name="late_sums",
        )(dest, middle, late_counts, *across, beside[1], behind[1])

    twin_a = late(0, twin)
    own_b = swap(twin_a)
    own_a = late(1, own)
    twin_b = swap(own_a)

    half = count // 2
    augmented, best = pl.pallas_call(
        score_kernel,
        out_shape=[
            jax.ShapeDtypeStruct((rows, features), jnp.bfloat16),
            jax.ShapeDtypeStruct((half // 128, 128), jnp.float32),
        ],
        in_specs=[vmem] * 6,
        out_specs=[vmem, vmem],
        scratch_shapes=[pltpu.VMEM((2 * rows, features), jnp.bfloat16)],
        compiler_params=pltpu.CompilerParams(vmem_limit_bytes=30 * MIB),
        cost_estimate=pl.CostEstimate(
            flops=2 * count * rows * features, bytes_accessed=count * features, transcendentals=0
        ),
        name="scores",
    )(own_a, own_b, twin_a, twin_b, first_queries, second_queries)

    received = [along(best, apart, apart) for apart in range(1, planes)]
    for value in received:
        best = jnp.maximum(best, value)
    other_half = swap(best)
    first = jnp.where(core == 0, best, other_half)
    second = jnp.where(core == 0, other_half, best)
    return augmented, jnp.concatenate([first, second], axis=0).reshape(count)


def solution(mesh):
    return jax.shard_map(
        local,
        mesh=mesh,
        in_specs=(P("db", None), P("db", None), P("db"), P("pb", None)),
        out_specs=(P("db", None), P("pb")),
        check_vma=False,
    )
```

```python
import functools

import jax
import jax.numpy as jnp
from jax import lax
from jax.experimental import pallas as pl
from jax.experimental.pallas import tpu as pltpu
from jax.sharding import PartitionSpec as P

epsilon = 1e-06
MIB = 1 << 20


def column_inverse(values):
    squares = jnp.sum(values * values, axis=-1, keepdims=True)
    return lax.rsqrt(squares + epsilon)


def as_row(column):
    wide = jnp.broadcast_to(column, (column.shape[0], 128))
    return wide.T[0:1, :]


def position_of():
    owner = lax.axis_index("db")
    return lax.axis_index("pb"), owner // 2, owner % 2


def fetch_queries(queries_ref, held_ref, part, sem):
    rows = held_ref.shape[0]
    core = position_of()[2]
    start = pl.multiple_of((core * 2 + part) * rows, rows)
    return pltpu.make_async_copy(queries_ref.at[pl.ds(start, rows), :], held_ref, sem)


def count_kernel(
    planes, twin_ref, own_ref, database_ref, queries_ref, early_ref, middle_ref, late_ref, copy_ref, held_ref,
    tiles_ref, lows_ref, sem, queries_sem,
):
    rows = copy_ref.shape[0]
    fanout = own_ref.shape[0] * 128 // rows
    quarter = rows // 4
    span = (planes - 1) * quarter
    early_tiles = early_ref.shape[1] // 128
    middle_tiles = middle_ref.shape[1] // 128
    late_tiles = late_ref.shape[1] // 128
    cut = span // 2
    copy = pltpu.make_async_copy(database_ref, copy_ref, sem)
    copy.start()
    queries = fetch_queries(queries_ref, held_ref, 0, queries_sem)
    queries.start()
    me, plane, core = position_of()
    bits = rows.bit_length() - 1
    lines = own_ref.shape[0]
    for number, wanted_ref in enumerate((twin_ref, own_ref)):
        wanted = wanted_ref[...]
        owner = wanted >> bits
        side = owner & 1
        row = wanted & (rows - 1)
        cross = (row >> (bits - 2)) ^ me
        inner = row & (quarter - 1)
        away = (owner >> 1) ^ plane
        paired = (cross == 3) & (away > 1)
        held = jnp.where(paired, away & 1, side) == core
        straight = (away - 1) * quarter
        crossed = ((away >> 1) * 2 - 1 + (side ^ core)) * quarter
        middle = early_tiles * 128
        late = middle + middle_tiles * 128
        straight = straight + inner
        crossed = crossed + inner
        second = jnp.where(cross == 1 + core, 0, cut)
        forwarded = straight + second + jnp.where(straight < cut, middle, late + span - cut)
        position = jnp.where(cross == 3, late + jnp.where(paired, crossed, straight), forwarded)
        position = jnp.where(cross == 0, rows + straight, position)
        position = jnp.where(away == 0, row, position)
        position = jnp.where((wanted >= 0) & held, position, -1)
        tiles_ref[number * lines : (number + 1) * lines, :] = position >> 7
        lows_ref[number * lines : (number + 1) * lines, :] = position & 127

    group = 16
    height = (early_tiles + middle_tiles + late_tiles) * group
    width = group * fanout
    at_row = lax.broadcasted_iota(jnp.int32, (height, width), 0)
    at_lane = lax.broadcasted_iota(jnp.int32, (height, width), 1)
    target = jnp.where(at_lane // fanout == at_row % group, at_row // group, -2)
    low_of = lax.broadcasted_iota(jnp.int32, (128, width), 0)
    each = width // 128

    def flat(ref, at):
        return jnp.concatenate([ref[pl.ds(at * each + i, 1), :] for i in range(each)], axis=1)

    def body(at, carry):
        tile = jnp.broadcast_to(flat(tiles_ref, at), (height, width))
        low = jnp.broadcast_to(flat(lows_ref, at), (128, width))
        left = jnp.where(tile == target, 1.0, 0.0).astype(jnp.bfloat16)
        right = jnp.where(low == low_of, 1.0, 0.0).astype(jnp.bfloat16)
        counts = lax.dot_general(
            left, right, (((1,), (1,)), ((), ())), preferred_element_type=jnp.float32
        ).astype(jnp.bfloat16)
        start = pl.ds(pl.multiple_of(at * group, group), group)
        tile = 0
        for count_ref in (early_ref, middle_ref, late_ref):
            for t in range(count_ref.shape[1] // 128):
                count_ref[start, t * 128 : (t + 1) * 128] = counts[tile * group : (tile + 1) * group, :]
                tile += 1
        return carry

    lax.fori_loop(0, 2 * rows // group, body, 0, unroll=4)
    copy.wait()
    queries.wait()


def join_kernel(own_ref, twin_ref, *rest):
    both_ref, alone_ref, first_ref, second_ref = rest[-4:]
    quarter = alone_ref.shape[0]
    me = position_of()[0]
    at = pl.multiple_of((me ^ 3) * quarter, quarter)
    both_ref[:quarter, :] = own_ref[pl.ds(at, quarter), :]
    both_ref[quarter:, :] = twin_ref[pl.ds(at, quarter), :]
    alone_ref[...] = own_ref[pl.ds(at, quarter), :]
    near = jnp.concatenate([ref[...] for ref in rest[:-4]], axis=0)
    cut = first_ref.shape[0]
    first_ref[...] = near[:cut]
    second_ref[...] = near[cut:]


def spread_terms(dest, dest_inverse, block, far, counts):
    products = lax.dot_general(
        dest, block, (((1,), (1,)), ((), ())), preferred_element_type=jnp.float32
    )
    cosine = products * dest_inverse * far
    halfway = (1.0 + cosine) * 0.5
    weight = halfway * halfway * halfway
    coefficient = (weight * far).astype(jnp.bfloat16).astype(jnp.float32)
    spread = coefficient * counts.astype(jnp.float32)
    high = spread.astype(jnp.bfloat16)
    low = (spread - high.astype(jnp.float32)).astype(jnp.bfloat16)
    return jnp.dot(high, block, preferred_element_type=jnp.float32) + jnp.dot(
        low, block, preferred_element_type=jnp.float32
    )


def early_kernel(queries_ref, twin_ref, own_ref, counts_ref, *rest):
    out_ref, held_ref, sem = rest[-3:]
    queries = fetch_queries(queries_ref, held_ref, 1, sem)
    queries.start()
    rows = own_ref.shape[0]
    block = jnp.concatenate([own_ref[...]] + [ref[...] for ref in rest[:-3]], axis=0)
    far = as_row(column_inverse(block.astype(jnp.float32)))
    for number, dest_ref in enumerate((twin_ref, own_ref)):
        lines = slice(number * rows, (number + 1) * rows)
        dest = dest_ref[...]
        values = dest.astype(jnp.float32)
        dest_inverse = column_inverse(values)
        terms = spread_terms(dest, dest_inverse, block, far, counts_ref[lines, : block.shape[0]])
        if number == 1:
            terms = terms + values * dest_inverse
        out_ref[lines, :] = terms
    queries.wait()


def middle_kernel(twin_ref, own_ref, early_ref, counts_ref, beside_ref, behind_ref, out_ref):
    rows = own_ref.shape[0]
    block = jnp.concatenate([beside_ref[...], behind_ref[...]], axis=0)
    far = as_row(column_inverse(block.astype(jnp.float32)))
    for number, dest_ref in enumerate((twin_ref, own_ref)):
        lines = slice(number * rows, (number + 1) * rows)
        dest = dest_ref[...]
        dest_inverse = column_inverse(dest.astype(jnp.float32))
        terms = spread_terms(dest, dest_inverse, block, far, counts_ref[lines, : block.shape[0]])
        out_ref[lines, :] = early_ref[lines, :] + terms


def late_kernel(number, dest_ref, early_ref, counts_ref, *rest):
    out_ref = rest[-1]
    rows = dest_ref.shape[0]
    lines = slice(number * rows, (number + 1) * rows)
    block = jnp.concatenate([ref[...] for ref in rest[:-1]], axis=0)
    far = as_row(column_inverse(block.astype(jnp.float32)))
    dest = dest_ref[...]
    dest_inverse = column_inverse(dest.astype(jnp.float32))
    terms = spread_terms(dest, dest_inverse, block, far, counts_ref[lines, : block.shape[0]])
    out_ref[...] = early_ref[lines, :] + terms


def score_kernel(own_a_ref, own_b_ref, twin_a_ref, twin_b_ref, first_ref, second_ref, augmented_ref, best_ref, rows_ref):
    rows = own_a_ref.shape[0]
    for number, (a_ref, b_ref) in enumerate(((own_a_ref, own_b_ref), (twin_a_ref, twin_b_ref))):
        summed = a_ref[...] + b_ref[...]
        augmented = (summed * column_inverse(summed)).astype(jnp.bfloat16)
        if number == 0:
            augmented_ref[...] = augmented
        rows_ref[number * rows : (number + 1) * rows, :] = augmented

    height = first_ref.shape[0]
    step = min(1024, height)
    tile = min(2048, height)
    for number, held_ref in enumerate((first_ref, second_ref)):

        @pl.loop(0, height // tile)
        def _(i):
            at = pl.multiple_of(i * tile, tile)
            line = pl.multiple_of(number * (height // 128) + i * (tile // 128), tile // 128)
            found = []
            for first in range(0, tile, step):
                scores = lax.dot_general(
                    rows_ref[...],
                    held_ref[pl.ds(at + first, step), :],
                    (((1,), (1,)), ((), ())),
                    preferred_element_type=jnp.float32,
                )
                best = jnp.max(scores, axis=0, keepdims=True)
                found += [best[:, part : part + 128] for part in range(0, step, 128)]
            best_ref[pl.ds(line, tile // 128), :] = jnp.concatenate(found, axis=0)


def local(database, neighbours, valid_count, queries):
    rows, features = database.shape
    fanout = neighbours.shape[1]
    count = queries.shape[0]
    owners = lax.axis_size("db")
    panels = lax.axis_size("pb")
    assert panels == 4 and owners % 4 == 0 and owners & (owners - 1) == 0
    planes = owners // 2
    quarter = rows // panels
    me = lax.axis_index("pb")
    core = lax.axis_index("db") % 2

    def along(value, even, odd):
        apart = (even, odd)
        pairs = [(i, ((i // 2) ^ apart[i % 2]) * 2 + i % 2) for i in range(owners)]
        return lax.ppermute(value, "db", pairs)

    def swap(value):
        return lax.ppermute(value, "db", [(i, i ^ 1) for i in range(owners)])

    def cross(value, bits):
        pairs = []
        for panel in range(panels):
            for i in range(owners):
                pairs.append((panel * owners + i, (panel ^ bits[i % 2]) * owners + i))
        return lax.ppermute(value, ("pb", "db"), pairs)

    mine = lax.dynamic_slice_in_dim(database, me * quarter, quarter, 0)
    pieces = [along(mine, apart, apart) for apart in range(1, planes)]
    twin = swap(database)
    vmem = pl.BlockSpec(memory_space=pltpu.VMEM)
    slots = jnp.arange(fanout, dtype=jnp.int32)[None, :]
    wanted = jnp.where(slots < valid_count[:, None], neighbours, -1).reshape(-1, 128)
    twin_wanted = swap(wanted)
    padded = lambda size: (size + 127) // 128 * 128
    span = (planes - 1) * quarter
    early_counts, middle_counts, late_counts, own, first_queries = pl.pallas_call(
        functools.partial(count_kernel, planes),
        out_shape=[
            jax.ShapeDtypeStruct((2 * rows, padded(rows + span)), jnp.bfloat16),
            jax.ShapeDtypeStruct((2 * rows, padded(span)), jnp.bfloat16),
            jax.ShapeDtypeStruct((2 * rows, padded(2 * span)), jnp.bfloat16),
            jax.ShapeDtypeStruct((rows, features), jnp.bfloat16),
            jax.ShapeDtypeStruct((count // 4, features), jnp.bfloat16),
        ],
        in_specs=[vmem, vmem] + [pl.BlockSpec(memory_space=pltpu.HBM)] * 2,
        out_specs=[vmem] * 5,
        scratch_shapes=[
            pltpu.VMEM((2 * wanted.shape[0], 128), jnp.int32),
            pltpu.VMEM((2 * wanted.shape[0], 128), jnp.int32),
            pltpu.SemaphoreType.DMA(()),
            pltpu.SemaphoreType.DMA(()),
        ],
        compiler_params=pltpu.CompilerParams(vmem_limit_bytes=30 * MIB),
        cost_estimate=pl.CostEstimate(flops=1 << 26, bytes_accessed=4 * rows * rows, transcendentals=0),
        name="counts",
    )(twin_wanted, wanted, database, queries)
    piece = lambda height: jax.ShapeDtypeStruct((height, features), jnp.bfloat16)
    both, alone, *near = pl.pallas_call(
        join_kernel,
        out_shape=[piece(2 * quarter), piece(quarter), piece(span // 2), piece(span // 2)],
        in_specs=[vmem] * (2 + len(pieces)),
        out_specs=[vmem] * 4,
        compiler_params=pltpu.CompilerParams(vmem_limit_bytes=8 * MIB),
        name="join",
    )(own, twin, *pieces)
    across = [along(alone, 1, 1)] + [along(both, apart, apart + 1) for apart in range(2, planes, 2)]
    beside = [cross(part, (1, 2)) for part in near]
    behind = [cross(part, (2, 1)) for part in near]

    early, second_queries = pl.pallas_call(
        early_kernel,
        out_shape=[
            jax.ShapeDtypeStruct((2 * rows, features), jnp.float32),
            jax.ShapeDtypeStruct((count // 4, features), jnp.bfloat16),
        ],
        in_specs=[pl.BlockSpec(memory_space=pltpu.HBM)] + [vmem] * 5,
        out_specs=[vmem] * 2,
        scratch_shapes=[pltpu.SemaphoreType.DMA(())],
        compiler_params=pltpu.CompilerParams(vmem_limit_bytes=30 * MIB),
        cost_estimate=pl.CostEstimate(flops=1 << 26, bytes_accessed=4 * rows * rows, transcendentals=0),
        name="early_sums",
    )(queries, twin, own, early_counts, *near)

    middle = pl.pallas_call(
        middle_kernel,
        out_shape=jax.ShapeDtypeStruct((2 * rows, features), jnp.float32),
        in_specs=[vmem] * 6,
        out_specs=vmem,
        compiler_params=pltpu.CompilerParams(vmem_limit_bytes=30 * MIB),
        cost_estimate=pl.CostEstimate(flops=1 << 26, bytes_accessed=4 * rows * rows, transcendentals=0),
        name="middle_sums",
    )(twin, own, early, middle_counts, beside[0], behind[0])

    def late(number, dest):
        return pl.pallas_call(
            functools.partial(late_kernel, number),
            out_shape=jax.ShapeDtypeStruct((rows, features), jnp.float32),
            in_specs=[vmem] * (5 + len(across)),
            out_specs=vmem,
            compiler_params=pltpu.CompilerParams(vmem_limit_bytes=30 * MIB),
            name="late_sums",
        )(dest, middle, late_counts, *across, beside[1], behind[1])

    twin_a = late(0, twin)
    own_b = swap(twin_a)
    own_a = late(1, own)
    twin_b = swap(own_a)

    half = count // 2
    augmented, best = pl.pallas_call(
        score_kernel,
        out_shape=[
            jax.ShapeDtypeStruct((rows, features), jnp.bfloat16),
            jax.ShapeDtypeStruct((half // 128, 128), jnp.float32),
        ],
        in_specs=[vmem] * 6,
        out_specs=[vmem, vmem],
        scratch_shapes=[pltpu.VMEM((2 * rows, features), jnp.bfloat16)],
        compiler_params=pltpu.CompilerParams(vmem_limit_bytes=30 * MIB),
        cost_estimate=pl.CostEstimate(
            flops=2 * count * rows * features, bytes_accessed=count * features, transcendentals=0
        ),
        name="scores",
    )(own_a, own_b, twin_a, twin_b, first_queries, second_queries)

    apart = 1
    while apart < planes:
        best = jnp.maximum(best, along(best, apart, apart))
        apart *= 2
    other_half = swap(best)
    first = jnp.where(core == 0, best, other_half)
    second = jnp.where(core == 0, other_half, best)
    return augmented, jnp.concatenate([first, second], axis=0).reshape(count)


def solution(mesh):
    return jax.shard_map(
        local,
        mesh=mesh,
        in_specs=(P("db", None), P("db", None), P("db"), P("pb", None)),
        out_specs=(P("db", None), P("pb")),
        check_vma=False,
    )
```

```python
import functools
import math

import jax
import jax.numpy as jnp
from jax import lax
from jax.experimental import pallas as pl
from jax.experimental.pallas import tpu as pltpu
from jax.sharding import PartitionSpec as P

epsilon = 1e-06
MIB = 1 << 20


def column_inverse(values):
    squares = jnp.sum(values * values, axis=-1, keepdims=True)
    return lax.rsqrt(squares + epsilon)


def as_row(column):
    wide = jnp.broadcast_to(column, (column.shape[0], 128))
    return wide.T[0:1, :]


def position_of():
    owner = lax.axis_index("db")
    return lax.axis_index("pb"), owner // 2, owner % 2


def fetch_queries(queries_ref, held_ref, last, sem):
    rows = held_ref.shape[0]
    half = queries_ref.shape[0] // 2
    start = position_of()[2] * half + (half - rows if last else 0)
    start = pl.multiple_of(start, math.gcd(half, rows))
    return pltpu.make_async_copy(queries_ref.at[pl.ds(start, rows), :], held_ref, sem)


def count_kernel(
    planes, twin_ref, own_ref, database_ref, queries_ref, early_ref, middle_ref, late_ref, copy_ref, held_ref,
    tiles_ref, lows_ref, sem, queries_sem,
):
    rows = copy_ref.shape[0]
    fanout = own_ref.shape[0] * 128 // rows
    quarter = rows // 4
    span = (planes - 1) * quarter
    early_tiles = early_ref.shape[1] // 128
    middle_tiles = middle_ref.shape[1] // 128
    late_tiles = late_ref.shape[1] // 128
    cut = span // 2
    copy = pltpu.make_async_copy(database_ref, copy_ref, sem)
    copy.start()
    queries = fetch_queries(queries_ref, held_ref, False, queries_sem)
    queries.start()
    me, plane, core = position_of()
    bits = rows.bit_length() - 1
    lines = own_ref.shape[0]
    for number, wanted_ref in enumerate((twin_ref, own_ref)):
        wanted = wanted_ref[...]
        owner = wanted >> bits
        side = owner & 1
        row = wanted & (rows - 1)
        cross = (row >> (bits - 2)) ^ me
        inner = row & (quarter - 1)
        away = (owner >> 1) ^ plane
        paired = (cross == 3) & (away > 1)
        held = jnp.where(paired, away & 1, side) == core
        straight = (away - 1) * quarter
        crossed = ((away >> 1) * 2 - 1 + (side ^ core)) * quarter
        middle = early_tiles * 128
        late = middle + middle_tiles * 128
        straight = straight + inner
        crossed = crossed + inner
        second = jnp.where(cross == 1 + core, 0, cut)
        forwarded = straight + second + jnp.where(straight < cut, middle, late + span - cut)
        position = jnp.where(cross == 3, late + jnp.where(paired, crossed, straight), forwarded)
        position = jnp.where(cross == 0, rows + straight, position)
        position = jnp.where(away == 0, row, position)
        position = jnp.where((wanted >= 0) & held, position, -1)
        tiles_ref[number * lines : (number + 1) * lines, :] = position >> 7
        lows_ref[number * lines : (number + 1) * lines, :] = position & 127

    group = 16
    height = (early_tiles + middle_tiles + late_tiles) * group
    width = group * fanout
    at_row = lax.broadcasted_iota(jnp.int32, (height, width), 0)
    at_lane = lax.broadcasted_iota(jnp.int32, (height, width), 1)
    target = jnp.where(at_lane // fanout == at_row % group, at_row // group, -2)
    low_of = lax.broadcasted_iota(jnp.int32, (128, width), 0)
    each = width // 128

    def flat(ref, at):
        return jnp.concatenate([ref[pl.ds(at * each + i, 1), :] for i in range(each)], axis=1)

    def body(at, carry):
        tile = jnp.broadcast_to(flat(tiles_ref, at), (height, width))
        low = jnp.broadcast_to(flat(lows_ref, at), (128, width))
        left = jnp.where(tile == target, 1.0, 0.0).astype(jnp.bfloat16)
        right = jnp.where(low == low_of, 1.0, 0.0).astype(jnp.bfloat16)
        counts = lax.dot_general(
            left, right, (((1,), (1,)), ((), ())), preferred_element_type=jnp.float32
        ).astype(jnp.bfloat16)
        start = pl.ds(pl.multiple_of(at * group, group), group)
        tile = 0
        for count_ref in (early_ref, middle_ref, late_ref):
            for t in range(count_ref.shape[1] // 128):
                count_ref[start, t * 128 : (t + 1) * 128] = counts[tile * group : (tile + 1) * group, :]
                tile += 1
        return carry

    lax.fori_loop(0, 2 * rows // group, body, 0, unroll=4)
    copy.wait()
    queries.wait()


def join_kernel(own_ref, twin_ref, pieces_ref, both_ref, alone_ref, first_ref, second_ref):
    quarter = alone_ref.shape[0]
    me, plane, _ = position_of()
    at = pl.multiple_of((me ^ 3) * quarter, quarter)
    both_ref[:quarter, :] = own_ref[pl.ds(at, quarter), :]
    both_ref[quarter:, :] = twin_ref[pl.ds(at, quarter), :]
    alone_ref[...] = own_ref[pl.ds(at, quarter), :]
    planes = pieces_ref.shape[0]
    near = jnp.concatenate([pieces_ref[plane ^ apart] for apart in range(1, planes)], axis=0)
    cut = first_ref.shape[0]
    first_ref[...] = near[:cut]
    second_ref[...] = near[cut:]


def spread_terms(dest, dest_inverse, block, far, counts):
    products = lax.dot_general(
        dest, block, (((1,), (1,)), ((), ())), preferred_element_type=jnp.float32
    )
    cosine = products * dest_inverse * far
    halfway = (1.0 + cosine) * 0.5
    weight = halfway * halfway * halfway
    coefficient = (weight * far).astype(jnp.bfloat16).astype(jnp.float32)
    spread = coefficient * counts.astype(jnp.float32)
    high = spread.astype(jnp.bfloat16)
    low = (spread - high.astype(jnp.float32)).astype(jnp.bfloat16)
    return jnp.dot(high, block, preferred_element_type=jnp.float32) + jnp.dot(
        low, block, preferred_element_type=jnp.float32
    )


def early_kernel(queries_ref, twin_ref, own_ref, counts_ref, *rest):
    out_ref, held_ref, sem = rest[-3:]
    queries = fetch_queries(queries_ref, held_ref, True, sem)
    queries.start()
    rows = own_ref.shape[0]
    block = jnp.concatenate([own_ref[...]] + [ref[...] for ref in rest[:-3]], axis=0)
    far = as_row(column_inverse(block.astype(jnp.float32)))
    for number, dest_ref in enumerate((twin_ref, own_ref)):
        lines = slice(number * rows, (number + 1) * rows)
        dest = dest_ref[...]
        values = dest.astype(jnp.float32)
        dest_inverse = column_inverse(values)
        terms = spread_terms(dest, dest_inverse, block, far, counts_ref[lines, : block.shape[0]])
        if number == 1:
            terms = terms + values * dest_inverse
        out_ref[lines, :] = terms
    queries.wait()


def middle_kernel(twin_ref, own_ref, early_ref, counts_ref, beside_ref, behind_ref, out_ref):
    rows = own_ref.shape[0]
    block = jnp.concatenate([beside_ref[...], behind_ref[...]], axis=0)
    far = as_row(column_inverse(block.astype(jnp.float32)))
    for number, dest_ref in enumerate((twin_ref, own_ref)):
        lines = slice(number * rows, (number + 1) * rows)
        dest = dest_ref[...]
        dest_inverse = column_inverse(dest.astype(jnp.float32))
        terms = spread_terms(dest, dest_inverse, block, far, counts_ref[lines, : block.shape[0]])
        out_ref[lines, :] = early_ref[lines, :] + terms


def late_kernel(number, dest_ref, early_ref, counts_ref, *rest):
    out_ref = rest[-1]
    rows = dest_ref.shape[0]
    lines = slice(number * rows, (number + 1) * rows)
    block = jnp.concatenate([ref[...] for ref in rest[:-1]], axis=0)
    far = as_row(column_inverse(block.astype(jnp.float32)))
    dest = dest_ref[...]
    dest_inverse = column_inverse(dest.astype(jnp.float32))
    terms = spread_terms(dest, dest_inverse, block, far, counts_ref[lines, : block.shape[0]])
    out_ref[...] = early_ref[lines, :] + terms


def score_kernel(own_a_ref, own_b_ref, twin_a_ref, twin_b_ref, first_ref, second_ref, augmented_ref, best_ref, rows_ref):
    rows = own_a_ref.shape[0]
    for number, (a_ref, b_ref) in enumerate(((own_a_ref, own_b_ref), (twin_a_ref, twin_b_ref))):
        summed = a_ref[...] + b_ref[...]
        augmented = (summed * column_inverse(summed)).astype(jnp.bfloat16)
        if number == 0:
            augmented_ref[...] = augmented
        rows_ref[number * rows : (number + 1) * rows, :] = augmented

    line_of = 0
    for held_ref in (first_ref, second_ref):
        height = held_ref.shape[0]
        step = min(1024, height)
        tile = min(2048, height)
        before = line_of
        line_of += height // 128

        @pl.loop(0, height // tile)
        def _(i):
            at = pl.multiple_of(i * tile, tile)
            line = pl.multiple_of(before + i * (tile // 128), tile // 128)
            found = []
            for first in range(0, tile, step):
                scores = lax.dot_general(
                    rows_ref[...],
                    held_ref[pl.ds(at + first, step), :],
                    (((1,), (1,)), ((), ())),
                    preferred_element_type=jnp.float32,
                )
                best = jnp.max(scores, axis=0, keepdims=True)
                found += [best[:, part : part + 128] for part in range(0, step, 128)]
            found = jnp.concatenate(found, axis=0)
            for copy in range(best_ref.shape[0]):
                best_ref[copy, pl.ds(line, tile // 128), :] = found


def local(database, neighbours, valid_count, queries):
    rows, features = database.shape
    fanout = neighbours.shape[1]
    count = queries.shape[0]
    owners = lax.axis_size("db")
    panels = lax.axis_size("pb")
    assert panels == 4 and owners % 4 == 0 and owners & (owners - 1) == 0
    planes = owners // 2
    quarter = rows // panels
    me = lax.axis_index("pb")
    core = lax.axis_index("db") % 2

    def along(value, even, odd):
        apart = (even, odd)
        pairs = [(i, ((i // 2) ^ apart[i % 2]) * 2 + i % 2) for i in range(owners)]
        return lax.ppermute(value, "db", pairs)

    def among(value):
        groups = [[2 * z + c for z in range(planes)] for c in range(2)]
        return lax.all_to_all(value, "db", 0, 0, axis_index_groups=groups, tiled=True)

    def swap(value):
        return lax.ppermute(value, "db", [(i, i ^ 1) for i in range(owners)])

    def cross(value, bits):
        pairs = []
        for panel in range(panels):
            for i in range(owners):
                pairs.append((panel * owners + i, (panel ^ bits[i % 2]) * owners + i))
        return lax.ppermute(value, ("pb", "db"), pairs)

    mine = lax.dynamic_slice_in_dim(database, me * quarter, quarter, 0)
    pieces = among(jnp.broadcast_to(mine[None], (planes, quarter, features)))
    twin = swap(database)
    vmem = pl.BlockSpec(memory_space=pltpu.VMEM)
    slots = jnp.arange(fanout, dtype=jnp.int32)[None, :]
    wanted = jnp.where(slots < valid_count[:, None], neighbours, -1).reshape(-1, 128)
    twin_wanted = swap(wanted)
    padded = lambda size: (size + 127) // 128 * 128
    span = (planes - 1) * quarter
    early_counts, middle_counts, late_counts, own, first_queries = pl.pallas_call(
        functools.partial(count_kernel, planes),
        out_shape=[
            jax.ShapeDtypeStruct((2 * rows, padded(rows + span)), jnp.bfloat16),
            jax.ShapeDtypeStruct((2 * rows, padded(span)), jnp.bfloat16),
            jax.ShapeDtypeStruct((2 * rows, padded(2 * span)), jnp.bfloat16),
            jax.ShapeDtypeStruct((rows, features), jnp.bfloat16),
            jax.ShapeDtypeStruct((count // 8 * 3, features), jnp.bfloat16),
        ],
        in_specs=[vmem, vmem] + [pl.BlockSpec(memory_space=pltpu.HBM)] * 2,
        out_specs=[vmem] * 5,
        scratch_shapes=[
            pltpu.VMEM((2 * wanted.shape[0], 128), jnp.int32),
            pltpu.VMEM((2 * wanted.shape[0], 128), jnp.int32),
            pltpu.SemaphoreType.DMA(()),
            pltpu.SemaphoreType.DMA(()),
        ],
        compiler_params=pltpu.CompilerParams(vmem_limit_bytes=30 * MIB),
        cost_estimate=pl.CostEstimate(flops=1<<26, bytes_accessed=4*rows*rows, transcendentals=0),
        name="counts",
    )(twin_wanted, wanted, database, queries)
    piece = lambda height: jax.ShapeDtypeStruct((height, features), jnp.bfloat16)
    both, alone, *near = pl.pallas_call(
        join_kernel,
        out_shape=[piece(2 * quarter), piece(quarter), piece(span // 2), piece(span // 2)],
        in_specs=[vmem] * 3,
        out_specs=[vmem] * 4,
        compiler_params=pltpu.CompilerParams(vmem_limit_bytes=8 * MIB),
        name="join",
    )(own, twin, pieces)
    across = [along(alone, 1, 1)] + [along(both, apart, apart + 1) for apart in range(2, planes, 2)]
    beside = [cross(part, (1, 2)) for part in near]
    behind = [cross(part, (2, 1)) for part in near]

    early, second_queries = pl.pallas_call(
        early_kernel,
        out_shape=[
            jax.ShapeDtypeStruct((2 * rows, features), jnp.float32),
            jax.ShapeDtypeStruct((count // 8, features), jnp.bfloat16),
        ],
        in_specs=[pl.BlockSpec(memory_space=pltpu.HBM)] + [vmem] * 5,
        out_specs=[vmem] * 2,
        scratch_shapes=[pltpu.SemaphoreType.DMA(())],
        compiler_params=pltpu.CompilerParams(vmem_limit_bytes=30 * MIB),
        cost_estimate=pl.CostEstimate(flops=1 << 10, bytes_accessed=4*rows*rows, transcendentals=0),
        name="early_sums",
    )(queries, twin, own, early_counts, *near)

    middle = pl.pallas_call(
        middle_kernel,
        out_shape=jax.ShapeDtypeStruct((2 * rows, features), jnp.float32),
        in_specs=[vmem] * 6,
        out_specs=vmem,
        compiler_params=pltpu.CompilerParams(vmem_limit_bytes=30 * MIB),
        cost_estimate=pl.CostEstimate(flops=1 << 10, bytes_accessed=4*rows*rows, transcendentals=0),
        name="middle_sums",
    )(twin, own, early, middle_counts, beside[0], behind[0])

    def late(number, dest):
        return pl.pallas_call(
            functools.partial(late_kernel, number),
            out_shape=jax.ShapeDtypeStruct((rows, features), jnp.float32),
            in_specs=[vmem] * (5 + len(across)),
            out_specs=vmem,
            compiler_params=pltpu.CompilerParams(vmem_limit_bytes=30 * MIB),
            name="late_sums",
        )(dest, middle, late_counts, *across, beside[1], behind[1])

    twin_a = late(0, twin)
    own_b = swap(twin_a)
    own_a = late(1, own)
    twin_b = swap(own_a)

    half = count // 2
    augmented, best = pl.pallas_call(
        score_kernel,
        out_shape=[
            jax.ShapeDtypeStruct((rows, features), jnp.bfloat16),
            jax.ShapeDtypeStruct((planes, half // 128, 128), jnp.float32),
        ],
        in_specs=[vmem] * 6,
        out_specs=[vmem, vmem],
        scratch_shapes=[pltpu.VMEM((2 * rows, features), jnp.bfloat16)],
        compiler_params=pltpu.CompilerParams(vmem_limit_bytes=30 * MIB),
        cost_estimate=pl.CostEstimate(
            flops=2 * count * rows * features, bytes_accessed=count * features, transcendentals=0
        ),
        name="scores",
    )(own_a, own_b, twin_a, twin_b, first_queries, second_queries)

    best = jnp.max(among(best), axis=0)
    other_half = swap(best)
    first = jnp.where(core == 0, best, other_half)
    second = jnp.where(core == 0, other_half, best)
    return augmented, jnp.concatenate([first, second], axis=0).reshape(count)


def solution(mesh):
    return jax.shard_map(
        local,
        mesh=mesh,
        in_specs=(P("db", None), P("db", None), P("db"), P("pb", None)),
        out_specs=(P("db", None), P("pb")),
        check_vma=False,
    )
```

```python
import functools

import jax
import jax.numpy as jnp
from jax import lax
from jax.experimental import pallas as pl
from jax.experimental.pallas import tpu as pltpu
from jax.sharding import PartitionSpec as P

epsilon = 1e-06
MIB = 1 << 20


def column_inverse(values):
    squares = jnp.sum(values * values, axis=-1, keepdims=True)
    return lax.rsqrt(squares + epsilon)


def as_row(column):
    wide = jnp.broadcast_to(column, (column.shape[0], 128))
    return wide.T[0:1, :]


def position_of():
    owner = lax.axis_index("db")
    return lax.axis_index("pb"), owner // 2, owner % 2


def fetch_queries(queries_ref, held_ref, part, sem):
    rows = held_ref.shape[0]
    half = queries_ref.shape[0] // 2
    start = pl.multiple_of(position_of()[2] * half + part * rows, rows)
    return pltpu.make_async_copy(queries_ref.at[pl.ds(start, rows), :], held_ref, sem)


def count_kernel(
    planes, twin_ref, own_ref, database_ref, queries_ref, *rest
):
    count_refs = rest[:-6]
    copy_ref, held_ref, tiles_ref, lows_ref, sem, queries_sem = rest[-6:]
    rows = copy_ref.shape[0]
    fanout = own_ref.shape[0] * 128 // rows
    quarter = rows // 4
    span = (planes - 1) * quarter
    starts = [0]
    for count_ref in count_refs:
        starts.append(starts[-1] + count_ref.shape[1])
    cut = span // 2
    copy = pltpu.make_async_copy(database_ref, copy_ref, sem)
    copy.start()
    queries = fetch_queries(queries_ref, held_ref, 0, queries_sem)
    queries.start()
    me, plane, core = position_of()
    bits = rows.bit_length() - 1
    lines = own_ref.shape[0]
    for number, wanted_ref in enumerate((twin_ref, own_ref)):
        wanted = wanted_ref[...]
        owner = wanted >> bits
        side = owner & 1
        row = wanted & (rows - 1)
        cross = (row >> (bits - 2)) ^ me
        inner = row & (quarter - 1)
        away = (owner >> 1) ^ plane
        paired = (cross == 3) & (away > 1)
        held = jnp.where(paired, away & 1, side) == core
        straight = (away - 1) * quarter
        crossed = ((away >> 1) * 2 - 1 + (side ^ core)) * quarter
        straight = straight + inner
        crossed = crossed + inner
        second = jnp.where(cross == 1 + core, 0, cut)
        forwarded = straight + second + jnp.where(straight < cut, starts[2], starts[3] - cut)
        position = jnp.where(cross == 3, starts[4] + jnp.where(paired, crossed, straight), forwarded)
        position = jnp.where(cross == 0, starts[1] + straight, position)
        position = jnp.where(away == 0, row, position)
        position = jnp.where((wanted >= 0) & held, position, -1)
        tiles_ref[number * lines : (number + 1) * lines, :] = position >> 7
        lows_ref[number * lines : (number + 1) * lines, :] = position & 127

    group = 16
    height = starts[-1] // 128 * group
    width = group * fanout
    at_row = lax.broadcasted_iota(jnp.int32, (height, width), 0)
    at_lane = lax.broadcasted_iota(jnp.int32, (height, width), 1)
    target = jnp.where(at_lane // fanout == at_row % group, at_row // group, -2)
    low_of = lax.broadcasted_iota(jnp.int32, (128, width), 0)
    each = width // 128

    def flat(ref, at):
        return jnp.concatenate([ref[pl.ds(at * each + i, 1), :] for i in range(each)], axis=1)

    def body(at, carry):
        tile = jnp.broadcast_to(flat(tiles_ref, at), (height, width))
        low = jnp.broadcast_to(flat(lows_ref, at), (128, width))
        left = jnp.where(tile == target, 1.0, 0.0).astype(jnp.bfloat16)
        right = jnp.where(low == low_of, 1.0, 0.0).astype(jnp.bfloat16)
        counts = lax.dot_general(
            left, right, (((1,), (1,)), ((), ())), preferred_element_type=jnp.float32
        ).astype(jnp.bfloat16)
        start = pl.ds(pl.multiple_of(at * group, group), group)
        tile = 0
        for count_ref in count_refs:
            for t in range(count_ref.shape[1] // 128):
                count_ref[start, t * 128 : (t + 1) * 128] = counts[tile * group : (tile + 1) * group, :]
                tile += 1
        return carry

    lax.fori_loop(0, 2 * rows // group, body, 0, unroll=4)
    copy.wait()
    queries.wait()


def join_kernel(own_ref, twin_ref, total_ref, *rest):
    both_ref, alone_ref, first_ref, second_ref = rest[-4:]
    quarter = alone_ref.shape[0]
    me = position_of()[0]
    at = pl.multiple_of((me ^ 3) * quarter, quarter)
    both_ref[:quarter, :] = own_ref[pl.ds(at, quarter), :]
    both_ref[quarter:, :] = twin_ref[pl.ds(at, quarter), :]
    alone_ref[...] = own_ref[pl.ds(at, quarter), :]
    near = jnp.concatenate([ref[...] for ref in rest[:-4]], axis=0)
    cut = first_ref.shape[0]
    first_ref[...] = near[:cut]
    second_ref[...] = near[cut:]


def spread_terms(dest, dest_inverse, block, far, counts):
    products = lax.dot_general(
        dest, block, (((1,), (1,)), ((), ())), preferred_element_type=jnp.float32
    )
    cosine = products * dest_inverse * far
    halfway = (1.0 + cosine) * 0.5
    weight = halfway * halfway * halfway
    coefficient = (weight * far).astype(jnp.bfloat16).astype(jnp.float32)
    spread = coefficient * counts.astype(jnp.float32)
    high = spread.astype(jnp.bfloat16)
    low = (spread - high.astype(jnp.float32)).astype(jnp.bfloat16)
    return jnp.dot(high, block, preferred_element_type=jnp.float32) + jnp.dot(
        low, block, preferred_element_type=jnp.float32
    )


def sums_kernel(blocks, part, twin_ref, own_ref, counts_ref, *rest):
    block_refs, rest = rest[:blocks], rest[blocks:]
    if part is not None:
        queries_ref, *rest, held_ref, sem = rest
        queries = fetch_queries(queries_ref, held_ref, part, sem)
        queries.start()
    *before_ref, out_ref = rest
    rows = own_ref.shape[0]
    block = jnp.concatenate([ref[...] for ref in block_refs], axis=0) if blocks > 1 else block_refs[0][...]
    far = as_row(column_inverse(block.astype(jnp.float32)))
    for number, dest_ref in enumerate((twin_ref, own_ref)):
        lines = slice(number * rows, (number + 1) * rows)
        dest = dest_ref[...]
        values = dest.astype(jnp.float32)
        dest_inverse = column_inverse(values)
        terms = spread_terms(dest, dest_inverse, block, far, counts_ref[lines, : block.shape[0]])
        if before_ref:
            terms = before_ref[0][lines, :] + terms
        elif number == 1:
            terms = terms + values * dest_inverse
        out_ref[lines, :] = terms
    if part is not None:
        queries.wait()


def late_kernel(number, dest_ref, early_ref, counts_ref, *rest):
    out_ref = rest[-1]
    rows = dest_ref.shape[0]
    lines = slice(number * rows, (number + 1) * rows)
    block = jnp.concatenate([ref[...] for ref in rest[:-1]], axis=0)
    far = as_row(column_inverse(block.astype(jnp.float32)))
    dest = dest_ref[...]
    dest_inverse = column_inverse(dest.astype(jnp.float32))
    terms = spread_terms(dest, dest_inverse, block, far, counts_ref[lines, : block.shape[0]])
    out_ref[...] = early_ref[lines, :] + terms


def score_kernel(own_a_ref, own_b_ref, twin_a_ref, twin_b_ref, first_ref, second_ref, third_ref, augmented_ref, best_ref, rows_ref):
    rows = own_a_ref.shape[0]
    for number, (a_ref, b_ref) in enumerate(((own_a_ref, own_b_ref), (twin_a_ref, twin_b_ref))):
        summed = a_ref[...] + b_ref[...]
        augmented = (summed * column_inverse(summed)).astype(jnp.bfloat16)
        if number == 0:
            augmented_ref[...] = augmented
        rows_ref[number * rows : (number + 1) * rows, :] = augmented

    line_of = 0
    for held_ref in (first_ref, second_ref, third_ref):
        height = held_ref.shape[0]
        step = min(1024, height)
        tile = min(2048, height)
        before = line_of
        line_of += height // 128

        @pl.loop(0, height // tile)
        def _(i):
            at = pl.multiple_of(i * tile, tile)
            line = pl.multiple_of(before + i * (tile // 128), tile // 128)
            found = []
            for first in range(0, tile, step):
                scores = lax.dot_general(
                    rows_ref[...],
                    held_ref[pl.ds(at + first, step), :],
                    (((1,), (1,)), ((), ())),
                    preferred_element_type=jnp.float32,
                )
                best = jnp.max(scores, axis=0, keepdims=True)
                found += [best[:, part : part + 128] for part in range(0, step, 128)]
            best_ref[pl.ds(line, tile // 128), :] = jnp.concatenate(found, axis=0)


def local(database, neighbours, valid_count, queries):
    rows, features = database.shape
    fanout = neighbours.shape[1]
    count = queries.shape[0]
    owners = lax.axis_size("db")
    panels = lax.axis_size("pb")
    assert panels == 4 and owners % 4 == 0 and owners & (owners - 1) == 0
    planes = owners // 2
    quarter = rows // panels
    me = lax.axis_index("pb")
    core = lax.axis_index("db") % 2

    def along(value, even, odd):
        apart = (even, odd)
        pairs = [(i, ((i // 2) ^ apart[i % 2]) * 2 + i % 2) for i in range(owners)]
        return lax.ppermute(value, "db", pairs)

    def swap(value):
        return lax.ppermute(value, "db", [(i, i ^ 1) for i in range(owners)])

    def cross(value, bits):
        pairs = []
        for panel in range(panels):
            for i in range(owners):
                pairs.append((panel * owners + i, (panel ^ bits[i % 2]) * owners + i))
        return lax.ppermute(value, ("pb", "db"), pairs)

    mine = lax.dynamic_slice_in_dim(database, me * quarter, quarter, 0)
    pieces = [along(mine, apart, apart) for apart in range(1, planes)]
    twin = swap(database)
    vmem = pl.BlockSpec(memory_space=pltpu.VMEM)
    slots = jnp.arange(fanout, dtype=jnp.int32)[None, :]
    wanted = jnp.where(slots < valid_count[:, None], neighbours, -1).reshape(-1, 128)
    twin_wanted = swap(wanted)
    padded = lambda size: (size + 127) // 128 * 128
    span = (planes - 1) * quarter
    *counts, own, first_queries = pl.pallas_call(
        functools.partial(count_kernel, planes),
        out_shape=[
            jax.ShapeDtypeStruct((2 * rows, padded(width)), jnp.bfloat16) for width in (rows,) + (span,) * 4
        ]
        + [
            jax.ShapeDtypeStruct((rows, features), jnp.bfloat16),
            jax.ShapeDtypeStruct((count // 4, features), jnp.bfloat16),
        ],
        in_specs=[vmem, vmem] + [pl.BlockSpec(memory_space=pltpu.HBM)] * 2,
        out_specs=[vmem] * 7,
        scratch_shapes=[
            pltpu.VMEM((2 * wanted.shape[0], 128), jnp.int32),
            pltpu.VMEM((2 * wanted.shape[0], 128), jnp.int32),
            pltpu.SemaphoreType.DMA(()),
            pltpu.SemaphoreType.DMA(()),
        ],
        compiler_params=pltpu.CompilerParams(vmem_limit_bytes=30 * MIB),
        cost_estimate=pl.CostEstimate(flops=1 << 26, bytes_accessed=4 * rows * rows, transcendentals=0),
        name="counts",
    )(twin_wanted, wanted, database, queries)

    def sums(name, counts, blocks, before=None, part=None):
        out = [jax.ShapeDtypeStruct((2 * rows, features), jnp.float32)]
        operands = [twin, own, counts, *blocks]
        specs = [vmem] * len(operands)
        scratch = []
        if part is not None:
            operands.append(queries)
            specs.append(pl.BlockSpec(memory_space=pltpu.HBM))
            out.append(jax.ShapeDtypeStruct((count // 8, features), jnp.bfloat16))
            scratch.append(pltpu.SemaphoreType.DMA(()))
        if before is not None:
            operands.append(before)
            specs.append(vmem)
        return pl.pallas_call(
            functools.partial(sums_kernel, len(blocks), part),
            out_shape=out,
            in_specs=specs,
            out_specs=[vmem] * len(out),
            scratch_shapes=scratch,
            compiler_params=pltpu.CompilerParams(vmem_limit_bytes=30 * MIB),
            cost_estimate=pl.CostEstimate(flops=1 << 26, bytes_accessed=4 * rows * rows, transcendentals=0),
            name=name,
        )(*operands)

    total, second_queries = sums("own_sums", counts[0], [own], part=2)
    piece = lambda height: jax.ShapeDtypeStruct((height, features), jnp.bfloat16)
    both, alone, *near = pl.pallas_call(
        join_kernel,
        out_shape=[piece(2 * quarter), piece(quarter), piece(span // 2), piece(span // 2)],
        in_specs=[vmem] * (3 + len(pieces)),
        out_specs=[vmem] * 4,
        compiler_params=pltpu.CompilerParams(vmem_limit_bytes=8 * MIB),
        name="join",
    )(own, twin, total, *pieces)
    across = [along(alone, 1, 1)] + [along(both, apart, apart + 1) for apart in range(2, planes, 2)]
    beside = [cross(part, (1, 2)) for part in near]
    behind = [cross(part, (2, 1)) for part in near]

    total, third_queries = sums("near_sums", counts[1], near, total, part=3)
    (total,) = sums("first_sums", counts[2], [beside[0], behind[0]], total)
    (total,) = sums("second_sums", counts[3], [beside[1], behind[1]], total)

    def late(number, dest):
        return pl.pallas_call(
            functools.partial(late_kernel, number),
            out_shape=jax.ShapeDtypeStruct((rows, features), jnp.float32),
            in_specs=[vmem] * (3 + len(across)),
            out_specs=vmem,
            compiler_params=pltpu.CompilerParams(vmem_limit_bytes=30 * MIB),
            name="late_sums",
        )(dest, total, counts[4], *across)

    twin_a = late(0, twin)
    own_b = swap(twin_a)
    own_a = late(1, own)
    twin_b = swap(own_a)

    half = count // 2
    augmented, best = pl.pallas_call(
        score_kernel,
        out_shape=[
            jax.ShapeDtypeStruct((rows, features), jnp.bfloat16),
            jax.ShapeDtypeStruct((half // 128, 128), jnp.float32),
        ],
        in_specs=[vmem] * 7,
        out_specs=[vmem, vmem],
        scratch_shapes=[pltpu.VMEM((2 * rows, features), jnp.bfloat16)],
        compiler_params=pltpu.CompilerParams(vmem_limit_bytes=30 * MIB),
        cost_estimate=pl.CostEstimate(
            flops=2 * count * rows * features, bytes_accessed=count * features, transcendentals=0
        ),
        name="scores",
    )(own_a, own_b, twin_a, twin_b, first_queries, second_queries, third_queries)

    received = [along(best, apart, apart) for apart in range(planes - 1, 0, -1)]
    for value in received:
        best = jnp.maximum(best, value)
    other_half = swap(best)
    first = jnp.where(core == 0, best, other_half)
    second = jnp.where(core == 0, other_half, best)
    return augmented, jnp.concatenate([first, second], axis=0).reshape(count)


def solution(mesh):
    return jax.shard_map(
        local,
        mesh=mesh,
        in_specs=(P("db", None), P("db", None), P("db"), P("pb", None)),
        out_specs=(P("db", None), P("pb")),
        check_vma=False,
    )
```

```python
import functools

import jax
import jax.numpy as jnp
from jax import lax
from jax.experimental import pallas as pl
from jax.experimental.pallas import tpu as pltpu
from jax.sharding import PartitionSpec as P

epsilon = 1e-06
MIB = 1 << 20


def column_inverse(values):
    squares = jnp.sum(values * values, axis=-1, keepdims=True)
    return lax.rsqrt(squares + epsilon)


def as_row(column):
    wide = jnp.broadcast_to(column, (column.shape[0], 128))
    return wide.T[0:1, :]


def position_of():
    owner = lax.axis_index("db")
    return lax.axis_index("pb"), owner // 2, owner % 2


def fetch_queries(queries_ref, held_ref, part, sem):
    rows = held_ref.shape[0]
    half = queries_ref.shape[0] // 2
    start = pl.multiple_of(position_of()[2] * half + part * rows, rows)
    return pltpu.make_async_copy(queries_ref.at[pl.ds(start, rows), :], held_ref, sem)


def count_kernel(
    planes, twin_ref, own_ref, database_ref, queries_ref, *rest
):
    count_refs = rest[:-6]
    copy_ref, held_ref, tiles_ref, lows_ref, sem, queries_sem = rest[-6:]
    rows = copy_ref.shape[0]
    fanout = own_ref.shape[0] * 128 // rows
    quarter = rows // 4
    span = (planes - 1) * quarter
    starts = [0]
    for count_ref in count_refs:
        starts.append(starts[-1] + count_ref.shape[1])
    copy = pltpu.make_async_copy(database_ref, copy_ref, sem)
    copy.start()
    queries = fetch_queries(queries_ref, held_ref, 0, queries_sem)
    queries.start()
    me, plane, core = position_of()
    bits = rows.bit_length() - 1
    lines = own_ref.shape[0]
    for number, wanted_ref in enumerate((twin_ref, own_ref)):
        wanted = wanted_ref[...]
        owner = wanted >> bits
        side = owner & 1
        row = wanted & (rows - 1)
        cross = (row >> (bits - 2)) ^ me
        inner = row & (quarter - 1)
        away = (owner >> 1) ^ plane
        paired = (cross == 3) & (away > 1)
        held = jnp.where(paired, away & 1, side) == core
        straight = (away - 1) * quarter
        crossed = ((away >> 1) * 2 - 1 + (side ^ core)) * quarter
        straight = straight + inner
        crossed = crossed + inner
        second = jnp.where(cross == 1 + core, 0, 1)
        adjacent = starts[1] + span + second * quarter + inner
        farther = starts[2] + span + second * (span - quarter) + straight - quarter
        forwarded = jnp.where(away == 1, adjacent, farther)
        position = jnp.where(cross == 3, starts[2] + jnp.where(paired, crossed, straight), forwarded)
        position = jnp.where(cross == 0, starts[1] + straight, position)
        position = jnp.where(away == 0, row, position)
        position = jnp.where((wanted >= 0) & held, position, -1)
        tiles_ref[number * lines : (number + 1) * lines, :] = position >> 7
        lows_ref[number * lines : (number + 1) * lines, :] = position & 127

    group = 16
    height = starts[-1] // 128 * group
    width = group * fanout
    at_row = lax.broadcasted_iota(jnp.int32, (height, width), 0)
    at_lane = lax.broadcasted_iota(jnp.int32, (height, width), 1)
    target = jnp.where(at_lane // fanout == at_row % group, at_row // group, -2)
    low_of = lax.broadcasted_iota(jnp.int32, (128, width), 0)
    each = width // 128

    def flat(ref, at):
        return jnp.concatenate([ref[pl.ds(at * each + i, 1), :] for i in range(each)], axis=1)

    def body(at, carry):
        tile = jnp.broadcast_to(flat(tiles_ref, at), (height, width))
        low = jnp.broadcast_to(flat(lows_ref, at), (128, width))
        left = jnp.where(tile == target, 1.0, 0.0).astype(jnp.bfloat16)
        right = jnp.where(low == low_of, 1.0, 0.0).astype(jnp.bfloat16)
        counts = lax.dot_general(
            left, right, (((1,), (1,)), ((), ())), preferred_element_type=jnp.float32
        ).astype(jnp.bfloat16)
        start = pl.ds(pl.multiple_of(at * group, group), group)
        tile = 0
        for count_ref in count_refs:
            for t in range(count_ref.shape[1] // 128):
                count_ref[start, t * 128 : (t + 1) * 128] = counts[tile * group : (tile + 1) * group, :]
                tile += 1
        return carry

    lax.fori_loop(0, 2 * rows // group, body, 0, unroll=4)
    copy.wait()
    queries.wait()


def join_kernel(pieces, own_ref, twin_ref, *rest):
    both_ref, alone_ref, farther_ref = rest[-3:]
    quarter = alone_ref.shape[0]
    me = position_of()[0]
    at = pl.multiple_of((me ^ 3) * quarter, quarter)
    alone_ref[...] = own_ref[pl.ds(at, quarter), :]
    both_ref[:quarter, :] = own_ref[pl.ds(at, quarter), :]
    both_ref[quarter:, :] = twin_ref[pl.ds(at, quarter), :]
    for i in range(pieces):
        farther_ref[i * quarter : (i + 1) * quarter, :] = rest[i][...]


def spread_terms(dest, dest_inverse, block, far, counts):
    products = lax.dot_general(
        dest, block, (((1,), (1,)), ((), ())), preferred_element_type=jnp.float32
    )
    cosine = products * dest_inverse * far
    halfway = (1.0 + cosine) * 0.5
    weight = halfway * halfway * halfway
    coefficient = (weight * far).astype(jnp.bfloat16).astype(jnp.float32)
    spread = coefficient * counts.astype(jnp.float32)
    high = spread.astype(jnp.bfloat16)
    low = (spread - high.astype(jnp.float32)).astype(jnp.bfloat16)
    return jnp.dot(high, block, preferred_element_type=jnp.float32) + jnp.dot(
        low, block, preferred_element_type=jnp.float32
    )


def sums_kernel(blocks, twin_ref, own_ref, counts_ref, *rest):
    block_refs, rest = rest[:blocks], rest[blocks:]
    *before_ref, out_ref = rest
    rows = own_ref.shape[0]
    block = jnp.concatenate([ref[...] for ref in block_refs], axis=0) if blocks > 1 else block_refs[0][...]
    far = as_row(column_inverse(block.astype(jnp.float32)))
    for number, dest_ref in enumerate((twin_ref, own_ref)):
        lines = slice(number * rows, (number + 1) * rows)
        dest = dest_ref[...]
        values = dest.astype(jnp.float32)
        dest_inverse = column_inverse(values)
        terms = spread_terms(dest, dest_inverse, block, far, counts_ref[lines, : block.shape[0]])
        if before_ref:
            terms = before_ref[0][lines, :] + terms
        elif number == 1:
            terms = terms + values * dest_inverse
        out_ref[lines, :] = terms


def late_kernel(number, dest_ref, early_ref, counts_ref, *rest):
    out_ref = rest[-1]
    rows = dest_ref.shape[0]
    lines = slice(number * rows, (number + 1) * rows)
    block = jnp.concatenate([ref[...] for ref in rest[:-1]], axis=0)
    far = as_row(column_inverse(block.astype(jnp.float32)))
    dest = dest_ref[...]
    dest_inverse = column_inverse(dest.astype(jnp.float32))
    terms = spread_terms(dest, dest_inverse, block, far, counts_ref[lines, : block.shape[0]])
    out_ref[...] = early_ref[lines, :] + terms


def score_kernel(own_a_ref, own_b_ref, twin_a_ref, twin_b_ref, first_ref, queries_ref, augmented_ref, best_ref, rows_ref, held_ref, sems):
    rows = own_a_ref.shape[0]
    size = held_ref.shape[0] // sems.shape[0]
    fetched = lambda i: held_ref.at[pl.ds(i * size, size), :]
    ahead = first_ref.shape[0] // size
    fetches = [
        fetch_queries(queries_ref, fetched(i), ahead + i, sems.at[i]) for i in range(sems.shape[0])
    ]
    for fetch in fetches:
        fetch.start()
    for number, (a_ref, b_ref) in enumerate(((own_a_ref, own_b_ref), (twin_a_ref, twin_b_ref))):
        summed = a_ref[...] + b_ref[...]
        augmented = (summed * column_inverse(summed)).astype(jnp.bfloat16)
        if number == 0:
            augmented_ref[...] = augmented
        rows_ref[number * rows : (number + 1) * rows, :] = augmented

    line_of = 0
    for part in range(1 + sems.shape[0]):
        if part == 0:
            block_ref = first_ref
        else:
            fetches[part - 1].wait()
            block_ref = fetched(part - 1)
        height = block_ref.shape[0]
        step = min(1024, height)
        tile = min(2048, height)
        before = line_of
        line_of += height // 128

        @pl.loop(0, height // tile)
        def _(i):
            at = pl.multiple_of(i * tile, tile)
            line = pl.multiple_of(before + i * (tile // 128), tile // 128)
            found = []
            for first in range(0, tile, step):
                scores = lax.dot_general(
                    rows_ref[...],
                    block_ref[pl.ds(at + first, step), :],
                    (((1,), (1,)), ((), ())),
                    preferred_element_type=jnp.float32,
                )
                best = jnp.max(scores, axis=0, keepdims=True)
                found += [best[:, part : part + 128] for part in range(0, step, 128)]
            best_ref[pl.ds(line, tile // 128), :] = jnp.concatenate(found, axis=0)


def local(database, neighbours, valid_count, queries):
    rows, features = database.shape
    fanout = neighbours.shape[1]
    count = queries.shape[0]
    owners = lax.axis_size("db")
    panels = lax.axis_size("pb")
    assert panels == 4 and owners % 4 == 0 and owners & (owners - 1) == 0
    planes = owners // 2
    quarter = rows // panels
    me = lax.axis_index("pb")
    core = lax.axis_index("db") % 2

    def along(value, even, odd):
        apart = (even, odd)
        pairs = [(i, ((i // 2) ^ apart[i % 2]) * 2 + i % 2) for i in range(owners)]
        return lax.ppermute(value, "db", pairs)

    def swap(value):
        return lax.ppermute(value, "db", [(i, i ^ 1) for i in range(owners)])

    def cross(value, bits):
        pairs = []
        for panel in range(panels):
            for i in range(owners):
                pairs.append((panel * owners + i, (panel ^ bits[i % 2]) * owners + i))
        return lax.ppermute(value, ("pb", "db"), pairs)

    mine = lax.dynamic_slice_in_dim(database, me * quarter, quarter, 0)
    pieces = [along(mine, apart, apart) for apart in range(1, planes)]
    twin = swap(database)
    vmem = pl.BlockSpec(memory_space=pltpu.VMEM)
    slots = jnp.arange(fanout, dtype=jnp.int32)[None, :]
    wanted = jnp.where(slots < valid_count[:, None], neighbours, -1).reshape(-1, 128)
    twin_wanted = swap(wanted)
    padded = lambda size: (size + 127) // 128 * 128
    span = (planes - 1) * quarter
    widths = (rows, span + 2 * quarter, span + 2 * (span - quarter))
    *counts, own, first_queries = pl.pallas_call(
        functools.partial(count_kernel, planes),
        out_shape=[
            jax.ShapeDtypeStruct((2 * rows, padded(width)), jnp.bfloat16) for width in widths
        ]
        + [
            jax.ShapeDtypeStruct((rows, features), jnp.bfloat16),
            jax.ShapeDtypeStruct((count // 4, features), jnp.bfloat16),
        ],
        in_specs=[vmem, vmem] + [pl.BlockSpec(memory_space=pltpu.HBM)] * 2,
        out_specs=[vmem] * 5,
        scratch_shapes=[
            pltpu.VMEM((2 * wanted.shape[0], 128), jnp.int32),
            pltpu.VMEM((2 * wanted.shape[0], 128), jnp.int32),
            pltpu.SemaphoreType.DMA(()),
            pltpu.SemaphoreType.DMA(()),
        ],
        compiler_params=pltpu.CompilerParams(vmem_limit_bytes=30 * MIB),
        cost_estimate=pl.CostEstimate(flops=1 << 26, bytes_accessed=4 * rows * rows, transcendentals=0),
        name="counts",
    )(twin_wanted, wanted, database, queries)

    def sums(name, counts, blocks, before=None):
        out = [jax.ShapeDtypeStruct((2 * rows, features), jnp.float32)]
        operands = [twin, own, counts, *blocks]
        specs = [vmem] * len(operands)
        if before is not None:
            operands.append(before)
            specs.append(vmem)
        return pl.pallas_call(
            functools.partial(sums_kernel, len(blocks)),
            out_shape=out,
            in_specs=specs,
            out_specs=[vmem] * len(out),
            compiler_params=pltpu.CompilerParams(vmem_limit_bytes=30 * MIB),
            cost_estimate=pl.CostEstimate(flops=1 << 26, bytes_accessed=4 * rows * rows, transcendentals=0),
            name=name,
        )(*operands)

    (total,) = sums("own_sums", counts[0], [own])
    piece = lambda height: jax.ShapeDtypeStruct((height, features), jnp.bfloat16)
    beside = cross(pieces[0], (1, 2))
    behind = cross(pieces[0], (2, 1))
    both, alone, farther = pl.pallas_call(
        functools.partial(join_kernel, len(pieces) - 1),
        out_shape=[piece(2 * quarter), piece(quarter), piece(span - quarter)],
        in_specs=[vmem] * (4 + len(pieces)),
        out_specs=[vmem] * 3,
        compiler_params=pltpu.CompilerParams(vmem_limit_bytes=8 * MIB),
        name="join",
    )(own, twin, *pieces[1:], beside, behind, total)
    across = [along(alone, 1, 1)] + [along(both, apart, apart + 1) for apart in range(2, planes, 2)]
    beside_farther = cross(farther, (1, 2))
    behind_farther = cross(farther, (2, 1))
    (total,) = sums("near_sums", counts[1], [*pieces, beside, behind], total)

    def late(number, dest):
        return pl.pallas_call(
            functools.partial(late_kernel, number),
            out_shape=jax.ShapeDtypeStruct((rows, features), jnp.float32),
            in_specs=[vmem] * (5 + len(across)),
            out_specs=vmem,
            compiler_params=pltpu.CompilerParams(vmem_limit_bytes=30 * MIB),
            name="late_sums",
        )(dest, total, counts[2], *across, beside_farther, behind_farther)

    twin_a = late(0, twin)
    own_b = swap(twin_a)
    own_a = late(1, own)
    twin_b = swap(own_a)

    half = count // 2
    augmented, best = pl.pallas_call(
        score_kernel,
        out_shape=[
            jax.ShapeDtypeStruct((rows, features), jnp.bfloat16),
            jax.ShapeDtypeStruct((half // 128, 128), jnp.float32),
        ],
        in_specs=[vmem] * 5 + [pl.BlockSpec(memory_space=pltpu.HBM)],
        out_specs=[vmem, vmem],
        scratch_shapes=[
            pltpu.VMEM((2 * rows, features), jnp.bfloat16),
            pltpu.VMEM((count // 4, features), jnp.bfloat16),
            pltpu.SemaphoreType.DMA((2,)),
        ],
        compiler_params=pltpu.CompilerParams(vmem_limit_bytes=40 * MIB),
        cost_estimate=pl.CostEstimate(
            flops=2 * count * rows * features, bytes_accessed=count * features, transcendentals=0
        ),
        name="scores",
    )(own_a, own_b, twin_a, twin_b, first_queries, queries)

    received = [along(best, apart, apart) for apart in range(planes - 1, 0, -1)]
    for value in received:
        best = jnp.maximum(best, value)
    other_half = swap(best)
    first = jnp.where(core == 0, best, other_half)
    second = jnp.where(core == 0, other_half, best)
    return augmented, jnp.concatenate([first, second], axis=0).reshape(count)


def solution(mesh):
    return jax.shard_map(
        local,
        mesh=mesh,
        in_specs=(P("db", None), P("db", None), P("db"), P("pb", None)),
        out_specs=(P("db", None), P("pb")),
        check_vma=False,
    )
```

```python
import functools

import jax
import jax.numpy as jnp
from jax import lax
from jax.experimental import pallas as pl
from jax.experimental.pallas import tpu as pltpu
from jax.sharding import PartitionSpec as P

epsilon = 1e-06
MIB = 1 << 20


def column_inverse(values):
    squares = jnp.sum(values * values, axis=-1, keepdims=True)
    return lax.rsqrt(squares + epsilon)


def as_row(column):
    wide = jnp.broadcast_to(column, (column.shape[0], 128))
    return wide.T[0:1, :]


def position_of():
    owner = lax.axis_index("db")
    return lax.axis_index("pb"), owner // 2, owner % 2


def fetch_queries(queries_ref, held_ref, part, sem):
    rows = held_ref.shape[0]
    half = queries_ref.shape[0] // 2
    start = pl.multiple_of(position_of()[2] * half + part * rows, rows)
    return pltpu.make_async_copy(queries_ref.at[pl.ds(start, rows), :], held_ref, sem)


def count_kernel(
    planes, twin_ref, own_ref, database_ref, queries_ref, adjacent_ref, far_ref, *rest
):
    count_refs = rest[:-7]
    copy_ref, held_ref, near_ref, tiles_ref, lows_ref, sem, queries_sem = rest[-7:]
    rows = copy_ref.shape[0]
    fanout = own_ref.shape[0] * 128 // rows
    quarter = rows // 4
    span = (planes - 1) * quarter
    starts = [0]
    for count_ref in count_refs:
        starts.append(starts[-1] + count_ref.shape[1])
    copy = pltpu.make_async_copy(database_ref, copy_ref, sem)
    copy.start()
    queries = fetch_queries(queries_ref, held_ref, 0, queries_sem)
    queries.start()
    near_ref[...] = adjacent_ref[: near_ref.shape[0], :]
    me, plane, core = position_of()
    bits = rows.bit_length() - 1
    lines = own_ref.shape[0]
    for number, wanted_ref in enumerate((twin_ref, own_ref)):
        wanted = wanted_ref[...]
        owner = wanted >> bits
        side = owner & 1
        row = wanted & (rows - 1)
        cross = (row >> (bits - 2)) ^ me
        inner = row & (quarter - 1)
        away = (owner >> 1) ^ plane
        straight = (away - 1) * quarter + inner
        start = jnp.where(cross == 3, starts[3], starts[3] + span)
        start = jnp.where(cross == 1 + core, starts[2], start)
        position = jnp.where(cross == 0, starts[1], start) + straight
        position = jnp.where(away == 0, row, position)
        position = jnp.where((wanted >= 0) & (side == core), position, -1)
        tiles_ref[number * lines : (number + 1) * lines, :] = position >> 7
        lows_ref[number * lines : (number + 1) * lines, :] = position & 127

    group = 16
    height = starts[-1] // 128 * group
    width = group * fanout
    at_row = lax.broadcasted_iota(jnp.int32, (height, width), 0)
    at_lane = lax.broadcasted_iota(jnp.int32, (height, width), 1)
    target = jnp.where(at_lane // fanout == at_row % group, at_row // group, -2)
    low_of = lax.broadcasted_iota(jnp.int32, (128, width), 0)
    each = width // 128

    def flat(ref, at):
        return jnp.concatenate([ref[pl.ds(at * each + i, 1), :] for i in range(each)], axis=1)

    def body(at, carry):
        tile = jnp.broadcast_to(flat(tiles_ref, at), (height, width))
        low = jnp.broadcast_to(flat(lows_ref, at), (128, width))
        left = jnp.where(tile == target, 1.0, 0.0).astype(jnp.bfloat16)
        right = jnp.where(low == low_of, 1.0, 0.0).astype(jnp.bfloat16)
        counts = lax.dot_general(
            left, right, (((1,), (1,)), ((), ())), preferred_element_type=jnp.float32
        ).astype(jnp.bfloat16)
        start = pl.ds(pl.multiple_of(at * group, group), group)
        tile = 0
        for count_ref in count_refs:
            for t in range(count_ref.shape[1] // 128):
                count_ref[start, t * 128 : (t + 1) * 128] = counts[tile * group : (tile + 1) * group, :]
                tile += 1
        return carry

    lax.fori_loop(0, 2 * rows // group, body, 0, unroll=4)
    copy.wait()
    queries.wait()


def join_kernel(pieces, *rest):
    out_ref = rest[-1]
    quarter = out_ref.shape[0] // pieces
    for i in range(pieces):
        out_ref[i * quarter : (i + 1) * quarter, :] = rest[i][...]


def spread_terms(dest, dest_inverse, block, far, counts):
    products = lax.dot_general(
        dest, block, (((1,), (1,)), ((), ())), preferred_element_type=jnp.float32
    )
    cosine = products * dest_inverse * far
    halfway = (1.0 + cosine) * 0.5
    weight = halfway * halfway * halfway
    coefficient = (weight * far).astype(jnp.bfloat16).astype(jnp.float32)
    spread = coefficient * counts.astype(jnp.float32)
    high = spread.astype(jnp.bfloat16)
    low = (spread - high.astype(jnp.float32)).astype(jnp.bfloat16)
    return jnp.dot(high, block, preferred_element_type=jnp.float32) + jnp.dot(
        low, block, preferred_element_type=jnp.float32
    )


def sums_kernel(blocks, twin_ref, own_ref, counts_ref, *rest):
    block_refs, rest = rest[:blocks], rest[blocks:]
    *before_ref, out_ref = rest
    rows = own_ref.shape[0]
    block = jnp.concatenate([ref[...] for ref in block_refs], axis=0) if blocks > 1 else block_refs[0][...]
    far = as_row(column_inverse(block.astype(jnp.float32)))
    for number, dest_ref in enumerate((twin_ref, own_ref)):
        lines = slice(number * rows, (number + 1) * rows)
        dest = dest_ref[...]
        values = dest.astype(jnp.float32)
        dest_inverse = column_inverse(values)
        terms = spread_terms(dest, dest_inverse, block, far, counts_ref[lines, : block.shape[0]])
        if before_ref:
            terms = before_ref[0][lines, :] + terms
        elif number == 1:
            terms = terms + values * dest_inverse
        out_ref[lines, :] = terms


def late_kernel(number, dest_ref, early_ref, counts_ref, *rest):
    out_ref = rest[-1]
    rows = dest_ref.shape[0]
    lines = slice(number * rows, (number + 1) * rows)
    block = jnp.concatenate([ref[...] for ref in rest[:-1]], axis=0)
    far = as_row(column_inverse(block.astype(jnp.float32)))
    dest = dest_ref[...]
    dest_inverse = column_inverse(dest.astype(jnp.float32))
    terms = spread_terms(dest, dest_inverse, block, far, counts_ref[lines, : block.shape[0]])
    out_ref[...] = early_ref[lines, :] + terms


def score_kernel(own_a_ref, own_b_ref, twin_a_ref, twin_b_ref, first_ref, queries_ref, augmented_ref, best_ref, rows_ref, held_ref, sems):
    rows = own_a_ref.shape[0]
    size = held_ref.shape[0] // sems.shape[0]
    fetched = lambda i: held_ref.at[pl.ds(i * size, size), :]
    ahead = first_ref.shape[0] // size
    fetches = [
        fetch_queries(queries_ref, fetched(i), ahead + i, sems.at[i]) for i in range(sems.shape[0])
    ]
    for fetch in fetches:
        fetch.start()
    for number, (a_ref, b_ref) in enumerate(((own_a_ref, own_b_ref), (twin_a_ref, twin_b_ref))):
        summed = a_ref[...] + b_ref[...]
        augmented = (summed * column_inverse(summed)).astype(jnp.bfloat16)
        if number == 0:
            augmented_ref[...] = augmented
        rows_ref[number * rows : (number + 1) * rows, :] = augmented

    line_of = 0
    for part in range(1 + sems.shape[0]):
        if part == 0:
            block_ref = first_ref
        else:
            fetches[part - 1].wait()
            block_ref = fetched(part - 1)
        height = block_ref.shape[0]
        step = min(1024, height)
        tile = min(2048, height)
        before = line_of
        line_of += height // 128

        @pl.loop(0, height // tile)
        def _(i):
            at = pl.multiple_of(i * tile, tile)
            line = pl.multiple_of(before + i * (tile // 128), tile // 128)
            found = []
            for first in range(0, tile, step):
                scores = lax.dot_general(
                    rows_ref[...],
                    block_ref[pl.ds(at + first, step), :],
                    (((1,), (1,)), ((), ())),
                    preferred_element_type=jnp.float32,
                )
                best = jnp.max(scores, axis=0, keepdims=True)
                found += [best[:, part : part + 128] for part in range(0, step, 128)]
            best_ref[pl.ds(line, tile // 128), :] = jnp.concatenate(found, axis=0)


def local(database, neighbours, valid_count, queries):
    rows, features = database.shape
    fanout = neighbours.shape[1]
    count = queries.shape[0]
    owners = lax.axis_size("db")
    panels = lax.axis_size("pb")
    assert panels == 4 and owners % 4 == 0 and owners & (owners - 1) == 0
    planes = owners // 2
    quarter = rows // panels
    me = lax.axis_index("pb")
    core = lax.axis_index("db") % 2

    def along(value, apart):
        pairs = [(i, ((i // 2) ^ apart) * 2 + i % 2) for i in range(owners)]
        return lax.ppermute(value, "db", pairs)

    def along_all(value, adjacent):
        pieces = {0: value}
        apart = planes // 2
        while apart:
            for other in sorted(pieces):
                joined = apart == 1 and other == 0
                pieces[other ^ apart] = adjacent if joined else along(pieces[other], apart)
            apart //= 2
        return [pieces[apart] for apart in range(1, planes)]

    def swap(value):
        return lax.ppermute(value, "db", [(i, i ^ 1) for i in range(owners)])

    def cross(value, bits):
        pairs = []
        for panel in range(panels):
            for i in range(owners):
                pairs.append((panel * owners + i, (panel ^ bits[i % 2]) * owners + i))
        return lax.ppermute(value, ("pb", "db"), pairs)

    mine = lax.dynamic_slice_in_dim(database, me * quarter, quarter, 0)
    other = lax.dynamic_slice_in_dim(database, (me ^ 3) * quarter, quarter, 0)
    adjacent = along(jnp.concatenate([mine, other], axis=0), 1)
    near = along_all(mine, adjacent[:quarter])
    across = along_all(other, adjacent[quarter:])
    twin = swap(database)
    vmem = pl.BlockSpec(memory_space=pltpu.VMEM)
    slots = jnp.arange(fanout, dtype=jnp.int32)[None, :]
    wanted = jnp.where(slots < valid_count[:, None], neighbours, -1).reshape(-1, 128)
    twin_wanted = swap(wanted)
    padded = lambda size: (size + 127) // 128 * 128
    span = (planes - 1) * quarter
    widths = (rows, span, span, 2 * span)
    *counts, own, first_queries, near_first = pl.pallas_call(
        functools.partial(count_kernel, planes),
        out_shape=[
            jax.ShapeDtypeStruct((2 * rows, padded(width)), jnp.bfloat16) for width in widths
        ]
        + [
            jax.ShapeDtypeStruct((rows, features), jnp.bfloat16),
            jax.ShapeDtypeStruct((count // 8, features), jnp.bfloat16),
            jax.ShapeDtypeStruct((quarter, features), jnp.bfloat16),
        ],
        in_specs=[vmem, vmem] + [pl.BlockSpec(memory_space=pltpu.HBM)] * 2 + [vmem] * 2,
        out_specs=[vmem] * 7,
        scratch_shapes=[
            pltpu.VMEM((2 * wanted.shape[0], 128), jnp.int32),
            pltpu.VMEM((2 * wanted.shape[0], 128), jnp.int32),
            pltpu.SemaphoreType.DMA(()),
            pltpu.SemaphoreType.DMA(()),
        ],
        compiler_params=pltpu.CompilerParams(vmem_limit_bytes=30 * MIB),
        cost_estimate=pl.CostEstimate(flops=1<<30, bytes_accessed=4 * rows * rows, transcendentals=0),
        name="counts",
    )(twin_wanted, wanted, database, queries, adjacent, near[planes // 2 - 1])
    near = pl.pallas_call(
        functools.partial(join_kernel, planes - 1),
        out_shape=jax.ShapeDtypeStruct((span, features), jnp.bfloat16),
        in_specs=[vmem] * planes,
        out_specs=vmem,
        compiler_params=pltpu.CompilerParams(vmem_limit_bytes=8 * MIB),
        name="join",
    )(near_first, *near[1:], across[planes // 2 - 1])
    beside = cross(near, (1, 2))
    behind = cross(near, (2, 1))

    def sums(name, counts, blocks, before=None):
        out = [jax.ShapeDtypeStruct((2 * rows, features), jnp.float32)]
        operands = [twin, own, counts, *blocks]
        specs = [vmem] * len(operands)
        if before is not None:
            operands.append(before)
            specs.append(vmem)
        return pl.pallas_call(
            functools.partial(sums_kernel, len(blocks)),
            out_shape=out,
            in_specs=specs,
            out_specs=[vmem] * len(out),
            compiler_params=pltpu.CompilerParams(vmem_limit_bytes=30 * MIB),
            cost_estimate=pl.CostEstimate(flops=1<<26, bytes_accessed=4 * rows * rows, transcendentals=0),
            name=name,
        )(*operands)

    (total,) = sums("own_sums", counts[0], [own])
    (total,) = sums("near_sums", counts[1], [near], total)
    (total,) = sums("beside_sums", counts[2], [beside], total)

    def late(number, dest):
        return pl.pallas_call(
            functools.partial(late_kernel, number),
            out_shape=jax.ShapeDtypeStruct((rows, features), jnp.float32),
            in_specs=[vmem] * (4 + len(across)),
            out_specs=vmem,
            compiler_params=pltpu.CompilerParams(vmem_limit_bytes=30 * MIB),
            name="late_sums",
        )(dest, total, counts[3], *across, behind)

    twin_a = late(0, twin)
    own_b = swap(twin_a)
    own_a = late(1, own)
    twin_b = swap(own_a)

    half = count // 2
    augmented, best = pl.pallas_call(
        score_kernel,
        out_shape=[
            jax.ShapeDtypeStruct((rows, features), jnp.bfloat16),
            jax.ShapeDtypeStruct((half // 128, 128), jnp.float32),
        ],
        in_specs=[vmem] * 5 + [pl.BlockSpec(memory_space=pltpu.HBM)],
        out_specs=[vmem, vmem],
        scratch_shapes=[
            pltpu.VMEM((2 * rows, features), jnp.bfloat16),
            pltpu.VMEM((count // 8 * 3, features), jnp.bfloat16),
            pltpu.SemaphoreType.DMA((3,)),
        ],
        compiler_params=pltpu.CompilerParams(vmem_limit_bytes=40 * MIB),
        cost_estimate=pl.CostEstimate(
            flops=2 * count * rows * features, bytes_accessed=count * features, transcendentals=0
        ),
        name="scores",
    )(own_a, own_b, twin_a, twin_b, first_queries, queries)

    received = [along(best, apart) for apart in range(planes - 1, 0, -1)]
    for value in received:
        best = jnp.maximum(best, value)
    other_half = swap(best)
    first = jnp.where(core == 0, best, other_half)
    second = jnp.where(core == 0, other_half, best)
    return augmented, jnp.concatenate([first, second], axis=0).reshape(count)


def solution(mesh):
    return jax.shard_map(
        local,
        mesh=mesh,
        in_specs=(P("db", None), P("db", None), P("db"), P("pb", None)),
        out_specs=(P("db", None), P("pb")),
        check_vma=False,
    )
```

```python
import functools

import jax
import jax.numpy as jnp
from jax import lax
from jax.experimental import pallas as pl
from jax.experimental.pallas import tpu as pltpu
from jax.sharding import PartitionSpec as P

epsilon = 1e-06
MIB = 1 << 20


def column_inverse(values):
    squares = jnp.sum(values * values, axis=-1, keepdims=True)
    return lax.rsqrt(squares + epsilon)


def as_row(column):
    wide = jnp.broadcast_to(column, (column.shape[0], 128))
    return wide.T[0:1, :]


def position_of():
    owner = lax.axis_index("db")
    return lax.axis_index("pb"), owner // 2, owner % 2


def fetch_queries(queries_ref, held_ref, part, sem):
    rows = held_ref.shape[0]
    half = queries_ref.shape[0] // 2
    start = pl.multiple_of(position_of()[2] * half + part * rows, rows)
    return pltpu.make_async_copy(queries_ref.at[pl.ds(start, rows), :], held_ref, sem)


def count_kernel(
    planes, twin_ref, own_ref, database_ref, queries_ref, adjacent_ref, far_ref, *rest
):
    count_refs = rest[:-7]
    copy_ref, held_ref, near_ref, tiles_ref, lows_ref, sem, queries_sem = rest[-7:]
    rows = copy_ref.shape[0]
    fanout = own_ref.shape[0] * 128 // rows
    quarter = rows // 4
    span = (planes - 1) * quarter
    starts = [0]
    for count_ref in count_refs:
        starts.append(starts[-1] + count_ref.shape[1])
    copy = pltpu.make_async_copy(database_ref, copy_ref, sem)
    copy.start()
    queries = fetch_queries(queries_ref, held_ref, 0, queries_sem)
    queries.start()
    near_ref[...] = adjacent_ref[...]
    me, plane, core = position_of()
    bits = rows.bit_length() - 1
    lines = own_ref.shape[0]
    for number, wanted_ref in enumerate((twin_ref, own_ref)):
        wanted = wanted_ref[...]
        owner = wanted >> bits
        side = owner & 1
        row = wanted & (rows - 1)
        cross = (row >> (bits - 2)) ^ me
        inner = row & (quarter - 1)
        away = (owner >> 1) ^ plane
        straight = (away - 1) * quarter + inner
        half = away >> 1
        relayed = jnp.where(away & 1 == 1, planes // 2 - 1 + half, half - 1) * quarter + inner
        position = starts[3] + jnp.where(cross == 3, relayed, span + straight)
        position = jnp.where(cross == 1 + core, starts[2] + straight, position)
        position = jnp.where(cross == 0, starts[1] + straight, position)
        position = jnp.where(away == 0, row, position)
        position = jnp.where((wanted >= 0) & (side == core), position, -1)
        tiles_ref[number * lines : (number + 1) * lines, :] = position >> 7
        lows_ref[number * lines : (number + 1) * lines, :] = position & 127

    group = 16
    height = starts[-1] // 128 * group
    width = group * fanout
    at_row = lax.broadcasted_iota(jnp.int32, (height, width), 0)
    at_lane = lax.broadcasted_iota(jnp.int32, (height, width), 1)
    target = jnp.where(at_lane // fanout == at_row % group, at_row // group, -2)
    low_of = lax.broadcasted_iota(jnp.int32, (128, width), 0)
    each = width // 128

    def flat(ref, at):
        return jnp.concatenate([ref[pl.ds(at * each + i, 1), :] for i in range(each)], axis=1)

    def body(at, carry):
        tile = jnp.broadcast_to(flat(tiles_ref, at), (height, width))
        low = jnp.broadcast_to(flat(lows_ref, at), (128, width))
        left = jnp.where(tile == target, 1.0, 0.0).astype(jnp.bfloat16)
        right = jnp.where(low == low_of, 1.0, 0.0).astype(jnp.bfloat16)
        counts = lax.dot_general(
            left, right, (((1,), (1,)), ((), ())), preferred_element_type=jnp.float32
        ).astype(jnp.bfloat16)
        start = pl.ds(pl.multiple_of(at * group, group), group)
        tile = 0
        for count_ref in count_refs:
            for t in range(count_ref.shape[1] // 128):
                count_ref[start, t * 128 : (t + 1) * 128] = counts[tile * group : (tile + 1) * group, :]
                tile += 1
        return carry

    lax.fori_loop(0, 2 * rows // group, body, 0, unroll=4)
    copy.wait()
    queries.wait()


def join_kernel(pieces, *rest):
    *pieces_refs, near_ref, across_ref = rest
    quarter = near_ref.shape[0] // pieces
    for i, ref in enumerate(pieces_refs):
        out_ref, at = (near_ref, i) if i < pieces else (across_ref, i - pieces)
        out_ref[at * quarter : (at + 1) * quarter, :] = ref[...]


def spread_terms(dest, dest_inverse, block, far, counts):
    products = lax.dot_general(
        dest, block, (((1,), (1,)), ((), ())), preferred_element_type=jnp.float32
    )
    cosine = products * dest_inverse * far
    halfway = (1.0 + cosine) * 0.5
    weight = halfway * halfway * halfway
    coefficient = (weight * far).astype(jnp.bfloat16).astype(jnp.float32)
    spread = coefficient * counts.astype(jnp.float32)
    high = spread.astype(jnp.bfloat16)
    low = (spread - high.astype(jnp.float32)).astype(jnp.bfloat16)
    return jnp.dot(high, block, preferred_element_type=jnp.float32) + jnp.dot(
        low, block, preferred_element_type=jnp.float32
    )


def sums_kernel(blocks, twin_ref, own_ref, counts_ref, *rest):
    block_refs, rest = rest[:blocks], rest[blocks:]
    *before_ref, out_ref = rest
    rows = own_ref.shape[0]
    block = jnp.concatenate([ref[...] for ref in block_refs], axis=0) if blocks > 1 else block_refs[0][...]
    far = as_row(column_inverse(block.astype(jnp.float32)))
    for number, dest_ref in enumerate((twin_ref, own_ref)):
        lines = slice(number * rows, (number + 1) * rows)
        dest = dest_ref[...]
        values = dest.astype(jnp.float32)
        dest_inverse = column_inverse(values)
        terms = spread_terms(dest, dest_inverse, block, far, counts_ref[lines, : block.shape[0]])
        if before_ref:
            terms = before_ref[0][lines, :] + terms
        elif number == 1:
            terms = terms + values * dest_inverse
        out_ref[lines, :] = terms


def late_kernel(number, dest_ref, early_ref, counts_ref, *rest):
    out_ref = rest[-1]
    rows = dest_ref.shape[0]
    lines = slice(number * rows, (number + 1) * rows)
    block = jnp.concatenate([ref[...] for ref in rest[:-1]], axis=0)
    far = as_row(column_inverse(block.astype(jnp.float32)))
    dest = dest_ref[...]
    dest_inverse = column_inverse(dest.astype(jnp.float32))
    terms = spread_terms(dest, dest_inverse, block, far, counts_ref[lines, : block.shape[0]])
    out_ref[...] = early_ref[lines, :] + terms


def score_kernel(own_a_ref, own_b_ref, twin_a_ref, twin_b_ref, first_ref, queries_ref, augmented_ref, best_ref, rows_ref, held_ref, sems):
    rows = own_a_ref.shape[0]
    size = held_ref.shape[0] // sems.shape[0]
    fetched = lambda i: held_ref.at[pl.ds(i * size, size), :]
    ahead = first_ref.shape[0] // size
    fetches = [
        fetch_queries(queries_ref, fetched(i), ahead + i, sems.at[i]) for i in range(sems.shape[0])
    ]
    for fetch in fetches:
        fetch.start()
    for number, (a_ref, b_ref) in enumerate(((own_a_ref, own_b_ref), (twin_a_ref, twin_b_ref))):
        summed = a_ref[...] + b_ref[...]
        augmented = (summed * column_inverse(summed)).astype(jnp.bfloat16)
        if number == 0:
            augmented_ref[...] = augmented
        rows_ref[number * rows : (number + 1) * rows, :] = augmented

    line_of = 0
    for part in range(1 + sems.shape[0]):
        if part == 0:
            block_ref = first_ref
        else:
            fetches[part - 1].wait()
            block_ref = fetched(part - 1)
        height = block_ref.shape[0]
        step = min(1024, height)
        tile = min(2048, height)
        before = line_of
        line_of += height // 128

        @pl.loop(0, height // tile)
        def _(i):
            at = pl.multiple_of(i * tile, tile)
            line = pl.multiple_of(before + i * (tile // 128), tile // 128)
            found = []
            for first in range(0, tile, step):
                scores = lax.dot_general(
                    rows_ref[...],
                    block_ref[pl.ds(at + first, step), :],
                    (((1,), (1,)), ((), ())),
                    preferred_element_type=jnp.float32,
                )
                best = jnp.max(scores, axis=0, keepdims=True)
                found += [best[:, part : part + 128] for part in range(0, step, 128)]
            best_ref[pl.ds(line, tile // 128), :] = jnp.concatenate(found, axis=0)


def local(database, neighbours, valid_count, queries):
    rows, features = database.shape
    fanout = neighbours.shape[1]
    count = queries.shape[0]
    owners = lax.axis_size("db")
    panels = lax.axis_size("pb")
    assert panels == 4 and owners % 4 == 0 and owners & (owners - 1) == 0
    planes = owners // 2
    quarter = rows // panels
    me = lax.axis_index("pb")
    core = lax.axis_index("db") % 2

    def along(value, apart):
        pairs = [(i, ((i // 2) ^ apart) * 2 + i % 2) for i in range(owners)]
        return lax.ppermute(value, "db", pairs)

    def along_all(value, smallest):
        pieces = {0: value}
        apart = planes // 2
        while apart >= smallest:
            for other in sorted(pieces):
                pieces[other ^ apart] = along(pieces[other], apart)
            apart //= 2
        return [pieces[apart] for apart in sorted(pieces)]

    def swap(value):
        return lax.ppermute(value, "db", [(i, i ^ 1) for i in range(owners)])

    def cross(value, bits):
        pairs = []
        for panel in range(panels):
            for i in range(owners):
                pairs.append((panel * owners + i, (panel ^ bits[i % 2]) * owners + i))
        return lax.ppermute(value, ("pb", "db"), pairs)

    mine = lax.dynamic_slice_in_dim(database, me * quarter, quarter, 0)
    other = lax.dynamic_slice_in_dim(database, (me ^ 3) * quarter, quarter, 0)
    near = along_all(mine, 1)[1:]
    across = along_all(other, 2)
    twin = swap(database)
    vmem = pl.BlockSpec(memory_space=pltpu.VMEM)
    slots = jnp.arange(fanout, dtype=jnp.int32)[None, :]
    wanted = jnp.where(slots < valid_count[:, None], neighbours, -1).reshape(-1, 128)
    twin_wanted = swap(wanted)
    padded = lambda size: (size + 127) // 128 * 128
    span = (planes - 1) * quarter
    widths = (rows, span, span, 2 * span)
    *counts, own, first_queries, near_first = pl.pallas_call(
        functools.partial(count_kernel, planes),
        out_shape=[
            jax.ShapeDtypeStruct((2 * rows, padded(width)), jnp.bfloat16) for width in widths
        ]
        + [
            jax.ShapeDtypeStruct((rows, features), jnp.bfloat16),
            jax.ShapeDtypeStruct((count // 4, features), jnp.bfloat16),
            jax.ShapeDtypeStruct((quarter, features), jnp.bfloat16),
        ],
        in_specs=[vmem, vmem] + [pl.BlockSpec(memory_space=pltpu.HBM)] * 2 + [vmem] * 2,
        out_specs=[vmem] * 7,
        scratch_shapes=[
            pltpu.VMEM((2 * wanted.shape[0], 128), jnp.int32),
            pltpu.VMEM((2 * wanted.shape[0], 128), jnp.int32),
            pltpu.SemaphoreType.DMA(()),
            pltpu.SemaphoreType.DMA(()),
        ],
        compiler_params=pltpu.CompilerParams(vmem_limit_bytes=30 * MIB),
        cost_estimate=pl.CostEstimate(flops=1<<30, bytes_accessed=4 * rows * rows, transcendentals=0),
        name="counts",
    )(twin_wanted, wanted, database, queries, near[0], near[planes // 2 - 1])
    near, message = pl.pallas_call(
        functools.partial(join_kernel, planes - 1),
        out_shape=[
            jax.ShapeDtypeStruct((span, features), jnp.bfloat16),
            jax.ShapeDtypeStruct((planes // 2 * quarter, features), jnp.bfloat16),
        ],
        in_specs=[vmem] * (planes - 1 + planes // 2),
        out_specs=[vmem] * 2,
        compiler_params=pltpu.CompilerParams(vmem_limit_bytes=8 * MIB),
        name="join",
    )(near_first, *near[1:], *across)
    across = across[1:] + [along(message, 1)]
    beside = cross(near, (1, 2))
    behind = cross(near, (2, 1))

    def sums(name, counts, blocks, before=None):
        out = [jax.ShapeDtypeStruct((2 * rows, features), jnp.float32)]
        operands = [twin, own, counts, *blocks]
        specs = [vmem] * len(operands)
        if before is not None:
            operands.append(before)
            specs.append(vmem)
        return pl.pallas_call(
            functools.partial(sums_kernel, len(blocks)),
            out_shape=out,
            in_specs=specs,
            out_specs=[vmem] * len(out),
            compiler_params=pltpu.CompilerParams(vmem_limit_bytes=30 * MIB),
            cost_estimate=pl.CostEstimate(flops=1<<26, bytes_accessed=4 * rows * rows, transcendentals=0),
            name=name,
        )(*operands)

    (total,) = sums("own_sums", counts[0], [own])
    (total,) = sums("near_sums", counts[1], [near], total)
    (total,) = sums("beside_sums", counts[2], [beside], total)

    def late(number, dest):
        return pl.pallas_call(
            functools.partial(late_kernel, number),
            out_shape=jax.ShapeDtypeStruct((rows, features), jnp.float32),
            in_specs=[vmem] * (4 + len(across)),
            out_specs=vmem,
            compiler_params=pltpu.CompilerParams(vmem_limit_bytes=30 * MIB),
            name="late_sums",
        )(dest, total, counts[3], *across, behind)

    twin_a = late(0, twin)
    own_b = swap(twin_a)
    own_a = late(1, own)
    twin_b = swap(own_a)

    half = count // 2
    augmented, best = pl.pallas_call(
        score_kernel,
        out_shape=[
            jax.ShapeDtypeStruct((rows, features), jnp.bfloat16),
            jax.ShapeDtypeStruct((half // 128, 128), jnp.float32),
        ],
        in_specs=[vmem] * 5 + [pl.BlockSpec(memory_space=pltpu.HBM)],
        out_specs=[vmem, vmem],
        scratch_shapes=[
            pltpu.VMEM((2 * rows, features), jnp.bfloat16),
            pltpu.VMEM((count // 4, features), jnp.bfloat16),
            pltpu.SemaphoreType.DMA((2,)),
        ],
        compiler_params=pltpu.CompilerParams(vmem_limit_bytes=40 * MIB),
        cost_estimate=pl.CostEstimate(
            flops=2 * count * rows * features, bytes_accessed=count * features, transcendentals=0
        ),
        name="scores",
    )(own_a, own_b, twin_a, twin_b, first_queries, queries)

    received = [along(best, apart) for apart in range(planes - 1, 0, -1)]
    for value in received:
        best = jnp.maximum(best, value)
    other_half = swap(best)
    first = jnp.where(core == 0, best, other_half)
    second = jnp.where(core == 0, other_half, best)
    return augmented, jnp.concatenate([first, second], axis=0).reshape(count)


def solution(mesh):
    return jax.shard_map(
        local,
        mesh=mesh,
        in_specs=(P("db", None), P("db", None), P("db"), P("pb", None)),
        out_specs=(P("db", None), P("pb")),
        check_vma=False,
    )
```

```python
import functools

import jax
import jax.numpy as jnp
from jax import lax
from jax.experimental import pallas as pl
from jax.experimental.pallas import tpu as pltpu
from jax.sharding import PartitionSpec as P

epsilon = 1e-06
MIB = 1 << 20


def column_inverse(values):
    squares = jnp.sum(values * values, axis=-1, keepdims=True)
    return lax.rsqrt(squares + epsilon)


def as_row(column):
    wide = jnp.broadcast_to(column, (column.shape[0], 128))
    return wide.T[0:1, :]


def position_of():
    owner = lax.axis_index("db")
    return lax.axis_index("pb"), owner // 2, owner % 2


def fetch_queries(queries_ref, held_ref, part, sem):
    rows = held_ref.shape[0]
    half = queries_ref.shape[0] // 2
    start = pl.multiple_of(position_of()[2] * half + part * rows, rows)
    return pltpu.make_async_copy(queries_ref.at[pl.ds(start, rows), :], held_ref, sem)


def count_kernel(
    planes, twin_ref, own_ref, database_ref, queries_ref, adjacent_ref, far_ref, *rest
):
    count_refs = rest[:-7]
    copy_ref, held_ref, near_ref, tiles_ref, lows_ref, sem, queries_sem = rest[-7:]
    rows = copy_ref.shape[0]
    fanout = own_ref.shape[0] * 128 // rows
    quarter = rows // 4
    span = (planes - 1) * quarter
    starts = [0]
    for count_ref in count_refs:
        starts.append(starts[-1] + count_ref.shape[1])
    copy = pltpu.make_async_copy(database_ref, copy_ref, sem)
    copy.start()
    queries = fetch_queries(queries_ref, held_ref, 0, queries_sem)
    queries.start()
    near_ref[...] = adjacent_ref[...]
    me, plane, core = position_of()
    bits = rows.bit_length() - 1
    lines = own_ref.shape[0]
    for number, wanted_ref in enumerate((twin_ref, own_ref)):
        wanted = wanted_ref[...]
        owner = wanted >> bits
        side = owner & 1
        row = wanted & (rows - 1)
        cross = (row >> (bits - 2)) ^ me
        inner = row & (quarter - 1)
        away = (owner >> 1) ^ plane
        straight = (away - 1) * quarter + inner
        half = away >> 1
        relayed = jnp.where(away & 1 == 1, planes // 2 - 1 + half, half - 1) * quarter + inner
        second = jnp.where(cross == 1 + core, 0, 1)
        first = span - quarter
        early = starts[1] + span + second * first + straight
        late = starts[2] + span + second * quarter + straight - first
        position = jnp.where(straight < first, early, late)
        position = jnp.where(cross == 3, starts[2] + relayed, position)
        position = jnp.where(cross == 0, starts[1] + straight, position)
        position = jnp.where(away == 0, row, position)
        position = jnp.where((wanted >= 0) & (side == core), position, -1)
        tiles_ref[number * lines : (number + 1) * lines, :] = position >> 7
        lows_ref[number * lines : (number + 1) * lines, :] = position & 127

    group = 16
    height = starts[-1] // 128 * group
    width = group * fanout
    at_row = lax.broadcasted_iota(jnp.int32, (height, width), 0)
    at_lane = lax.broadcasted_iota(jnp.int32, (height, width), 1)
    target = jnp.where(at_lane // fanout == at_row % group, at_row // group, -2)
    low_of = lax.broadcasted_iota(jnp.int32, (128, width), 0)
    each = width // 128

    def flat(ref, at):
        return jnp.concatenate([ref[pl.ds(at * each + i, 1), :] for i in range(each)], axis=1)

    def body(at, carry):
        tile = jnp.broadcast_to(flat(tiles_ref, at), (height, width))
        low = jnp.broadcast_to(flat(lows_ref, at), (128, width))
        left = jnp.where(tile == target, 1.0, 0.0).astype(jnp.bfloat16)
        right = jnp.where(low == low_of, 1.0, 0.0).astype(jnp.bfloat16)
        counts = lax.dot_general(
            left, right, (((1,), (1,)), ((), ())), preferred_element_type=jnp.float32
        ).astype(jnp.bfloat16)
        start = pl.ds(pl.multiple_of(at * group, group), group)
        tile = 0
        for count_ref in count_refs:
            for t in range(count_ref.shape[1] // 128):
                count_ref[start, t * 128 : (t + 1) * 128] = counts[tile * group : (tile + 1) * group, :]
                tile += 1
        return carry

    lax.fori_loop(0, 2 * rows // group, body, 0, unroll=4)
    copy.wait()
    queries.wait()


def join_kernel(last_ref, *rest):
    *pieces, _, forward_ref, across_ref = rest
    quarter = last_ref.shape[0]
    forward_ref[...] = last_ref[...]
    for i, ref in enumerate(pieces):
        across_ref[i * quarter : (i + 1) * quarter, :] = ref[...]


def spread_terms(dest, dest_inverse, block, far, counts):
    products = lax.dot_general(
        dest, block, (((1,), (1,)), ((), ())), preferred_element_type=jnp.float32
    )
    cosine = products * dest_inverse * far
    halfway = (1.0 + cosine) * 0.5
    weight = halfway * halfway * halfway
    coefficient = (weight * far).astype(jnp.bfloat16).astype(jnp.float32)
    spread = coefficient * counts.astype(jnp.float32)
    high = spread.astype(jnp.bfloat16)
    low = (spread - high.astype(jnp.float32)).astype(jnp.bfloat16)
    return jnp.dot(high, block, preferred_element_type=jnp.float32) + jnp.dot(
        low, block, preferred_element_type=jnp.float32
    )


def sums_kernel(blocks, twin_ref, own_ref, counts_ref, *rest):
    block_refs, rest = rest[:blocks], rest[blocks:]
    *before_ref, out_ref = rest
    rows = own_ref.shape[0]
    block = jnp.concatenate([ref[...] for ref in block_refs], axis=0) if blocks > 1 else block_refs[0][...]
    far = as_row(column_inverse(block.astype(jnp.float32)))
    for number, dest_ref in enumerate((twin_ref, own_ref)):
        lines = slice(number * rows, (number + 1) * rows)
        dest = dest_ref[...]
        values = dest.astype(jnp.float32)
        dest_inverse = column_inverse(values)
        terms = spread_terms(dest, dest_inverse, block, far, counts_ref[lines, : block.shape[0]])
        if before_ref:
            terms = before_ref[0][lines, :] + terms
        elif number == 1:
            terms = terms + values * dest_inverse
        out_ref[lines, :] = terms


def late_kernel(number, dest_ref, early_ref, counts_ref, *rest):
    out_ref = rest[-1]
    rows = dest_ref.shape[0]
    lines = slice(number * rows, (number + 1) * rows)
    block = jnp.concatenate([ref[...] for ref in rest[:-1]], axis=0)
    far = as_row(column_inverse(block.astype(jnp.float32)))
    dest = dest_ref[...]
    dest_inverse = column_inverse(dest.astype(jnp.float32))
    terms = spread_terms(dest, dest_inverse, block, far, counts_ref[lines, : block.shape[0]])
    out_ref[...] = early_ref[lines, :] + terms


def score_kernel(own_a_ref, own_b_ref, twin_a_ref, twin_b_ref, first_ref, queries_ref, augmented_ref, best_ref, rows_ref, held_ref, sems):
    rows = own_a_ref.shape[0]
    size = held_ref.shape[0] // sems.shape[0]
    fetched = lambda i: held_ref.at[pl.ds(i * size, size), :]
    ahead = first_ref.shape[0] // size
    fetches = [
        fetch_queries(queries_ref, fetched(i), ahead + i, sems.at[i]) for i in range(sems.shape[0])
    ]
    for fetch in fetches:
        fetch.start()
    for number, (a_ref, b_ref) in enumerate(((own_a_ref, own_b_ref), (twin_a_ref, twin_b_ref))):
        summed = a_ref[...] + b_ref[...]
        augmented = (summed * column_inverse(summed)).astype(jnp.bfloat16)
        if number == 0:
            augmented_ref[...] = augmented
        rows_ref[number * rows : (number + 1) * rows, :] = augmented

    line_of = 0
    for part in range(1 + sems.shape[0]):
        if part == 0:
            block_ref = first_ref
        else:
            fetches[part - 1].wait()
            block_ref = fetched(part - 1)
        height = block_ref.shape[0]
        step = min(1024, height)
        tile = min(2048, height)
        before = line_of
        line_of += height // 128

        @pl.loop(0, height // tile)
        def _(i):
            at = pl.multiple_of(i * tile, tile)
            line = pl.multiple_of(before + i * (tile // 128), tile // 128)
            found = []
            for first in range(0, tile, step):
                scores = lax.dot_general(
                    rows_ref[...],
                    block_ref[pl.ds(at + first, step), :],
                    (((1,), (1,)), ((), ())),
                    preferred_element_type=jnp.float32,
                )
                best = jnp.max(scores, axis=0, keepdims=True)
                found += [best[:, part : part + 128] for part in range(0, step, 128)]
            best_ref[pl.ds(line, tile // 128), :] = jnp.concatenate(found, axis=0)


def local(database, neighbours, valid_count, queries):
    rows, features = database.shape
    fanout = neighbours.shape[1]
    count = queries.shape[0]
    owners = lax.axis_size("db")
    panels = lax.axis_size("pb")
    assert panels == 4 and owners % 4 == 0 and owners & (owners - 1) == 0
    planes = owners // 2
    quarter = rows // panels
    me = lax.axis_index("pb")
    core = lax.axis_index("db") % 2

    def along(value, apart):
        pairs = [(i, ((i // 2) ^ apart) * 2 + i % 2) for i in range(owners)]
        return lax.ppermute(value, "db", pairs)

    def along_all(value, smallest):
        pieces = {0: value}
        apart = planes // 2
        while apart >= smallest:
            for other in sorted(pieces):
                pieces[other ^ apart] = along(pieces[other], apart)
            apart //= 2
        return [pieces[apart] for apart in sorted(pieces)]

    def swap(value):
        return lax.ppermute(value, "db", [(i, i ^ 1) for i in range(owners)])

    def cross(value, bits):
        pairs = []
        for panel in range(panels):
            for i in range(owners):
                pairs.append((panel * owners + i, (panel ^ bits[i % 2]) * owners + i))
        return lax.ppermute(value, ("pb", "db"), pairs)

    mine = lax.dynamic_slice_in_dim(database, me * quarter, quarter, 0)
    other = lax.dynamic_slice_in_dim(database, (me ^ 3) * quarter, quarter, 0)
    near = along_all(mine, 1)[1:]
    across = along_all(other, 2)
    ahead = jnp.concatenate(near[:-1], axis=0)
    beside = cross(ahead, (1, 2))
    behind = cross(ahead, (2, 1))
    twin = swap(database)
    vmem = pl.BlockSpec(memory_space=pltpu.VMEM)
    slots = jnp.arange(fanout, dtype=jnp.int32)[None, :]
    wanted = jnp.where(slots < valid_count[:, None], neighbours, -1).reshape(-1, 128)
    twin_wanted = swap(wanted)
    padded = lambda size: (size + 127) // 128 * 128
    span = (planes - 1) * quarter
    widths = (rows, 3 * span - 2 * quarter, span + 2 * quarter)
    *counts, own, first_queries, near_first = pl.pallas_call(
        functools.partial(count_kernel, planes),
        out_shape=[
            jax.ShapeDtypeStruct((2 * rows, padded(width)), jnp.bfloat16) for width in widths
        ]
        + [
            jax.ShapeDtypeStruct((rows, features), jnp.bfloat16),
            jax.ShapeDtypeStruct((count // 4, features), jnp.bfloat16),
            jax.ShapeDtypeStruct((quarter, features), jnp.bfloat16),
        ],
        in_specs=[vmem, vmem] + [pl.BlockSpec(memory_space=pltpu.HBM)] * 2 + [vmem] * 2,
        out_specs=[vmem] * 6,
        scratch_shapes=[
            pltpu.VMEM((2 * wanted.shape[0], 128), jnp.int32),
            pltpu.VMEM((2 * wanted.shape[0], 128), jnp.int32),
            pltpu.SemaphoreType.DMA(()),
            pltpu.SemaphoreType.DMA(()),
        ],
        compiler_params=pltpu.CompilerParams(vmem_limit_bytes=30 * MIB),
        cost_estimate=pl.CostEstimate(flops=1<<26, bytes_accessed=4 * rows * rows, transcendentals=0),
        name="counts",
    )(twin_wanted, wanted, database, queries, near[0], near[planes // 2 - 1])
    forward, message = pl.pallas_call(
        join_kernel,
        out_shape=[
            jax.ShapeDtypeStruct((quarter, features), jnp.bfloat16),
            jax.ShapeDtypeStruct((planes // 2 * quarter, features), jnp.bfloat16),
        ],
        in_specs=[vmem] * (2 + planes // 2),
        out_specs=[vmem] * 2,
        compiler_params=pltpu.CompilerParams(vmem_limit_bytes=8 * MIB),
        name="join",
    )(near[-1], *across, near_first)
    across = across[1:] + [along(message, 1)]
    beside_last = cross(forward, (1, 2))
    behind_last = cross(forward, (2, 1))

    def sums(name, counts, blocks, before=None):
        out = [jax.ShapeDtypeStruct((2 * rows, features), jnp.float32)]
        operands = [twin, own, counts, *blocks]
        specs = [vmem] * len(operands)
        if before is not None:
            operands.append(before)
            specs.append(vmem)
        return pl.pallas_call(
            functools.partial(sums_kernel, len(blocks)),
            out_shape=out,
            in_specs=specs,
            out_specs=[vmem] * len(out),
            compiler_params=pltpu.CompilerParams(vmem_limit_bytes=30 * MIB),
            cost_estimate=pl.CostEstimate(flops=1<<26, bytes_accessed=4 * rows * rows, transcendentals=0),
            name=name,
        )(*operands)

    (total,) = sums("own_sums", counts[0], [own])
    (total,) = sums("near_sums", counts[1], [*near, beside, behind], total)

    def late(number, dest):
        return pl.pallas_call(
            functools.partial(late_kernel, number),
            out_shape=jax.ShapeDtypeStruct((rows, features), jnp.float32),
            in_specs=[vmem] * (5 + len(across)),
            out_specs=vmem,
            compiler_params=pltpu.CompilerParams(vmem_limit_bytes=30 * MIB),
            name="late_sums",
        )(dest, total, counts[2], *across, beside_last, behind_last)

    twin_a = late(0, twin)
    own_b = swap(twin_a)
    own_a = late(1, own)
    twin_b = swap(own_a)

    half = count // 2
    augmented, best = pl.pallas_call(
        score_kernel,
        out_shape=[
            jax.ShapeDtypeStruct((rows, features), jnp.bfloat16),
            jax.ShapeDtypeStruct((half // 128, 128), jnp.float32),
        ],
        in_specs=[vmem] * 5 + [pl.BlockSpec(memory_space=pltpu.HBM)],
        out_specs=[vmem, vmem],
        scratch_shapes=[
            pltpu.VMEM((2 * rows, features), jnp.bfloat16),
            pltpu.VMEM((count // 4, features), jnp.bfloat16),
            pltpu.SemaphoreType.DMA((2,)),
        ],
        compiler_params=pltpu.CompilerParams(vmem_limit_bytes=40 * MIB),
        cost_estimate=pl.CostEstimate(
            flops=2 * count * rows * features, bytes_accessed=count * features, transcendentals=0
        ),
        name="scores",
    )(own_a, own_b, twin_a, twin_b, first_queries, queries)

    received = [along(best, apart) for apart in range(planes - 1, 0, -1)]
    for value in received:
        best = jnp.maximum(best, value)
    other_half = swap(best)
    first = jnp.where(core == 0, best, other_half)
    second = jnp.where(core == 0, other_half, best)
    return augmented, jnp.concatenate([first, second], axis=0).reshape(count)


def solution(mesh):
    return jax.shard_map(
        local,
        mesh=mesh,
        in_specs=(P("db", None), P("db", None), P("db"), P("pb", None)),
        out_specs=(P("db", None), P("pb")),
        check_vma=False,
    )
```

```python
import functools

import jax
import jax.numpy as jnp
from jax import lax
from jax.experimental import pallas as pl
from jax.experimental.pallas import tpu as pltpu
from jax.sharding import PartitionSpec as P

epsilon = 1e-06
MIB = 1 << 20


def column_inverse(values):
    squares = jnp.sum(values * values, axis=-1, keepdims=True)
    return lax.rsqrt(squares + epsilon)


def as_row(column):
    wide = jnp.broadcast_to(column, (column.shape[0], 128))
    return wide.T[0:1, :]


def position_of():
    owner = lax.axis_index("db")
    return lax.axis_index("pb"), owner // 2, owner % 2


def fetch_queries(queries_ref, held_ref, part, sem):
    rows = held_ref.shape[0]
    half = queries_ref.shape[0] // 2
    start = pl.multiple_of(position_of()[2] * half + part * rows, rows)
    return pltpu.make_async_copy(queries_ref.at[pl.ds(start, rows), :], held_ref, sem)


def count_kernel(
    planes, twin_ref, own_ref, database_ref, queries_ref, *rest
):
    count_refs = rest[:-6]
    copy_ref, held_ref, tiles_ref, lows_ref, sem, queries_sem = rest[-6:]
    rows = copy_ref.shape[0]
    fanout = own_ref.shape[0] * 128 // rows
    quarter = rows // 4
    span = (planes - 1) * quarter
    starts = [0]
    for count_ref in count_refs:
        starts.append(starts[-1] + count_ref.shape[1])
    copy = pltpu.make_async_copy(database_ref, copy_ref, sem)
    copy.start()
    queries = fetch_queries(queries_ref, held_ref, 0, queries_sem)
    queries.start()
    me, plane, core = position_of()
    bits = rows.bit_length() - 1
    lines = own_ref.shape[0]
    for number, wanted_ref in enumerate((twin_ref, own_ref)):
        wanted = wanted_ref[...]
        owner = wanted >> bits
        side = owner & 1
        row = wanted & (rows - 1)
        cross = (row >> (bits - 2)) ^ me
        inner = row & (quarter - 1)
        away = (owner >> 1) ^ plane
        straight = (away - 1) * quarter + inner
        half = away >> 1
        relayed = jnp.where(away & 1 == 1, planes // 2 - 1 + half, half - 1) * quarter + inner
        second = jnp.where(cross == 1 + core, 0, 1)
        first = span - quarter
        early = starts[1] + span + second * first + straight
        late = starts[2] + span + second * quarter + straight - first
        position = jnp.where(straight < first, early, late)
        position = jnp.where(cross == 3, starts[2] + relayed, position)
        position = jnp.where(cross == 0, starts[1] + straight, position)
        position = jnp.where(away == 0, row, position)
        position = jnp.where((wanted >= 0) & (side == core), position, -1)
        tiles_ref[number * lines : (number + 1) * lines, :] = position >> 7
        lows_ref[number * lines : (number + 1) * lines, :] = position & 127

    group = 16
    height = starts[-1] // 128 * group
    width = group * fanout
    at_row = lax.broadcasted_iota(jnp.int32, (height, width), 0)
    at_lane = lax.broadcasted_iota(jnp.int32, (height, width), 1)
    target = jnp.where(at_lane // fanout == at_row % group, at_row // group, -2)
    low_of = lax.broadcasted_iota(jnp.int32, (128, width), 0)
    each = width // 128

    def flat(ref, at):
        return jnp.concatenate([ref[pl.ds(at * each + i, 1), :] for i in range(each)], axis=1)

    def body(at, carry):
        tile = jnp.broadcast_to(flat(tiles_ref, at), (height, width))
        low = jnp.broadcast_to(flat(lows_ref, at), (128, width))
        left = jnp.where(tile == target, 1.0, 0.0).astype(jnp.bfloat16)
        right = jnp.where(low == low_of, 1.0, 0.0).astype(jnp.bfloat16)
        counts = lax.dot_general(
            left, right, (((1,), (1,)), ((), ())), preferred_element_type=jnp.float32
        ).astype(jnp.bfloat16)
        start = pl.ds(pl.multiple_of(at * group, group), group)
        tile = 0
        for count_ref in count_refs:
            for t in range(count_ref.shape[1] // 128):
                count_ref[start, t * 128 : (t + 1) * 128] = counts[tile * group : (tile + 1) * group, :]
                tile += 1
        return carry

    lax.fori_loop(0, 2 * rows // group, body, 0, unroll=4)
    copy.wait()
    queries.wait()


def join_kernel(last_ref, *rest):
    *pieces, _, forward_ref, across_ref = rest
    quarter = last_ref.shape[0]
    forward_ref[...] = last_ref[...]
    for i, ref in enumerate(pieces):
        across_ref[i * quarter : (i + 1) * quarter, :] = ref[...]


def spread_terms(dest, dest_inverse, block, far, counts):
    products = lax.dot_general(
        dest, block, (((1,), (1,)), ((), ())), preferred_element_type=jnp.float32
    )
    cosine = products * dest_inverse * far
    halfway = (1.0 + cosine) * 0.5
    weight = halfway * halfway * halfway
    coefficient = (weight * far).astype(jnp.bfloat16).astype(jnp.float32)
    spread = coefficient * counts.astype(jnp.float32)
    high = spread.astype(jnp.bfloat16)
    low = (spread - high.astype(jnp.float32)).astype(jnp.bfloat16)
    return jnp.dot(high, block, preferred_element_type=jnp.float32) + jnp.dot(
        low, block, preferred_element_type=jnp.float32
    )


def sums_kernel(blocks, twin_ref, own_ref, counts_ref, *rest):
    block_refs, rest = rest[:blocks], rest[blocks:]
    *before_ref, out_ref = rest
    rows = own_ref.shape[0]
    block = jnp.concatenate([ref[...] for ref in block_refs], axis=0) if blocks > 1 else block_refs[0][...]
    far = as_row(column_inverse(block.astype(jnp.float32)))
    for number, dest_ref in enumerate((twin_ref, own_ref)):
        lines = slice(number * rows, (number + 1) * rows)
        dest = dest_ref[...]
        values = dest.astype(jnp.float32)
        dest_inverse = column_inverse(values)
        terms = spread_terms(dest, dest_inverse, block, far, counts_ref[lines, : block.shape[0]])
        if before_ref:
            terms = before_ref[0][lines, :] + terms
        elif number == 1:
            terms = terms + values * dest_inverse
        out_ref[lines, :] = terms


def late_kernel(number, dest_ref, early_ref, counts_ref, *rest):
    out_ref = rest[-1]
    rows = dest_ref.shape[0]
    lines = slice(number * rows, (number + 1) * rows)
    block = jnp.concatenate([ref[...] for ref in rest[:-1]], axis=0)
    far = as_row(column_inverse(block.astype(jnp.float32)))
    dest = dest_ref[...]
    dest_inverse = column_inverse(dest.astype(jnp.float32))
    terms = spread_terms(dest, dest_inverse, block, far, counts_ref[lines, : block.shape[0]])
    out_ref[...] = early_ref[lines, :] + terms


def score_kernel(own_a_ref, own_b_ref, twin_a_ref, twin_b_ref, first_ref, queries_ref, augmented_ref, best_ref, rows_ref, held_ref, sems):
    rows = own_a_ref.shape[0]
    size = held_ref.shape[0] // sems.shape[0]
    fetched = lambda i: held_ref.at[pl.ds(i * size, size), :]
    ahead = first_ref.shape[0] // size
    fetches = [
        fetch_queries(queries_ref, fetched(i), ahead + i, sems.at[i]) for i in range(sems.shape[0])
    ]
    for fetch in fetches:
        fetch.start()
    for number, (a_ref, b_ref) in enumerate(((own_a_ref, own_b_ref), (twin_a_ref, twin_b_ref))):
        summed = a_ref[...] + b_ref[...]
        augmented = (summed * column_inverse(summed)).astype(jnp.bfloat16)
        if number == 0:
            augmented_ref[...] = augmented
        rows_ref[number * rows : (number + 1) * rows, :] = augmented

    line_of = 0
    for part in range(1 + sems.shape[0]):
        if part == 0:
            block_ref = first_ref
        else:
            fetches[part - 1].wait()
            block_ref = fetched(part - 1)
        height = block_ref.shape[0]
        step = min(1024, height)
        tile = min(2048, height)
        before = line_of
        line_of += height // 128

        @pl.loop(0, height // tile)
        def _(i):
            at = pl.multiple_of(i * tile, tile)
            line = pl.multiple_of(before + i * (tile // 128), tile // 128)
            found = []
            for first in range(0, tile, step):
                scores = lax.dot_general(
                    rows_ref[...],
                    block_ref[pl.ds(at + first, step), :],
                    (((1,), (1,)), ((), ())),
                    preferred_element_type=jnp.float32,
                )
                best = jnp.max(scores, axis=0, keepdims=True)
                found += [best[:, part : part + 128] for part in range(0, step, 128)]
            best_ref[pl.ds(line, tile // 128), :] = jnp.concatenate(found, axis=0)


def local(database, neighbours, valid_count, queries):
    rows, features = database.shape
    fanout = neighbours.shape[1]
    count = queries.shape[0]
    owners = lax.axis_size("db")
    panels = lax.axis_size("pb")
    assert panels == 4 and owners % 4 == 0 and owners & (owners - 1) == 0
    planes = owners // 2
    quarter = rows // panels
    me = lax.axis_index("pb")
    core = lax.axis_index("db") % 2

    def along(value, apart):
        pairs = [(i, ((i // 2) ^ apart) * 2 + i % 2) for i in range(owners)]
        return lax.ppermute(value, "db", pairs)

    def along_all(value, smallest):
        pieces = {0: value}
        apart = planes // 2
        while apart >= smallest:
            for other in sorted(pieces):
                pieces[other ^ apart] = along(pieces[other], apart)
            apart //= 2
        return [pieces[apart] for apart in sorted(pieces)]

    def swap(value):
        return lax.ppermute(value, "db", [(i, i ^ 1) for i in range(owners)])

    def cross(value, bits):
        pairs = []
        for panel in range(panels):
            for i in range(owners):
                pairs.append((panel * owners + i, (panel ^ bits[i % 2]) * owners + i))
        return lax.ppermute(value, ("pb", "db"), pairs)

    mine = lax.dynamic_slice_in_dim(database, me * quarter, quarter, 0)
    other = lax.dynamic_slice_in_dim(database, (me ^ 3) * quarter, quarter, 0)
    near = along_all(mine, 1)[1:]
    across = along_all(other, 2)
    ahead = jnp.concatenate(near[:-1], axis=0)
    beside = cross(ahead, (1, 2))
    behind = cross(ahead, (2, 1))
    twin = swap(database)
    vmem = pl.BlockSpec(memory_space=pltpu.VMEM)
    slots = jnp.arange(fanout, dtype=jnp.int32)[None, :]
    wanted = jnp.where(slots < valid_count[:, None], neighbours, -1).reshape(-1, 128)
    twin_wanted = swap(wanted)
    padded = lambda size: (size + 127) // 128 * 128
    span = (planes - 1) * quarter
    widths = (rows, 3 * span - 2 * quarter, span + 2 * quarter)
    *counts, own, first_queries = pl.pallas_call(
        functools.partial(count_kernel, planes),
        out_shape=[
            jax.ShapeDtypeStruct((2 * rows, padded(width)), jnp.bfloat16) for width in widths
        ]
        + [
            jax.ShapeDtypeStruct((rows, features), jnp.bfloat16),
            jax.ShapeDtypeStruct((count // 4, features), jnp.bfloat16),
        ],
        in_specs=[vmem, vmem] + [pl.BlockSpec(memory_space=pltpu.HBM)] * 2,
        out_specs=[vmem] * 5,
        scratch_shapes=[
            pltpu.VMEM((2 * wanted.shape[0], 128), jnp.int32),
            pltpu.VMEM((2 * wanted.shape[0], 128), jnp.int32),
            pltpu.SemaphoreType.DMA(()),
            pltpu.SemaphoreType.DMA(()),
        ],
        compiler_params=pltpu.CompilerParams(vmem_limit_bytes=30 * MIB),
        cost_estimate=pl.CostEstimate(flops=1<<29, bytes_accessed=4 * rows * rows, transcendentals=0),
        name="counts",
    )(twin_wanted, wanted, database, queries)
    forward, message = pl.pallas_call(
        join_kernel,
        out_shape=[
            jax.ShapeDtypeStruct((quarter, features), jnp.bfloat16),
            jax.ShapeDtypeStruct((planes // 2 * quarter, features), jnp.bfloat16),
        ],
        in_specs=[vmem] * (2 + planes // 2),
        out_specs=[vmem] * 2,
        compiler_params=pltpu.CompilerParams(vmem_limit_bytes=8 * MIB),
        name="join",
    )(near[-1], *across, own)
    across = across[1:] + [along(message, 1)]
    beside_last = cross(forward, (1, 2))
    behind_last = cross(forward, (2, 1))

    def sums(name, counts, blocks, flops, before=None):
        out = [jax.ShapeDtypeStruct((2 * rows, features), jnp.float32)]
        operands = [twin, own, counts, *blocks]
        specs = [vmem] * len(operands)
        if before is not None:
            operands.append(before)
            specs.append(vmem)
        return pl.pallas_call(
            functools.partial(sums_kernel, len(blocks)),
            out_shape=out,
            in_specs=specs,
            out_specs=[vmem] * len(out),
            compiler_params=pltpu.CompilerParams(vmem_limit_bytes=30 * MIB),
            cost_estimate=pl.CostEstimate(flops=flops, bytes_accessed=4 * rows * rows, transcendentals=0),
            name=name,
        )(*operands)

    (total,) = sums("own_sums", counts[0], [own], 1<<31)
    (total,) = sums("near_sums", counts[1], [*near, beside, behind], 1<<26, total)

    def late(number, dest):
        return pl.pallas_call(
            functools.partial(late_kernel, number),
            out_shape=jax.ShapeDtypeStruct((rows, features), jnp.float32),
            in_specs=[vmem] * (5 + len(across)),
            out_specs=vmem,
            compiler_params=pltpu.CompilerParams(vmem_limit_bytes=30 * MIB),
            name="late_sums",
        )(dest, total, counts[2], *across, beside_last, behind_last)

    twin_a = late(0, twin)
    own_b = swap(twin_a)
    own_a = late(1, own)
    twin_b = swap(own_a)

    half = count // 2
    augmented, best = pl.pallas_call(
        score_kernel,
        out_shape=[
            jax.ShapeDtypeStruct((rows, features), jnp.bfloat16),
            jax.ShapeDtypeStruct((half // 128, 128), jnp.float32),
        ],
        in_specs=[vmem] * 5 + [pl.BlockSpec(memory_space=pltpu.HBM)],
        out_specs=[vmem, vmem],
        scratch_shapes=[
            pltpu.VMEM((2 * rows, features), jnp.bfloat16),
            pltpu.VMEM((count // 4, features), jnp.bfloat16),
            pltpu.SemaphoreType.DMA((2,)),
        ],
        compiler_params=pltpu.CompilerParams(vmem_limit_bytes=40 * MIB),
        cost_estimate=pl.CostEstimate(
            flops=2 * count * rows * features, bytes_accessed=count * features, transcendentals=0
        ),
        name="scores",
    )(own_a, own_b, twin_a, twin_b, first_queries, queries)

    received = [along(best, apart) for apart in range(planes - 1, 0, -1)]
    for value in received:
        best = jnp.maximum(best, value)
    other_half = swap(best)
    first = jnp.where(core == 0, best, other_half)
    second = jnp.where(core == 0, other_half, best)
    return augmented, jnp.concatenate([first, second], axis=0).reshape(count)


def solution(mesh):
    return jax.shard_map(
        local,
        mesh=mesh,
        in_specs=(P("db", None), P("db", None), P("db"), P("pb", None)),
        out_specs=(P("db", None), P("pb")),
        check_vma=False,
    )
```

```python
import functools

import jax
import jax.numpy as jnp
from jax import lax
from jax.experimental import pallas as pl
from jax.experimental.pallas import tpu as pltpu
from jax.sharding import PartitionSpec as P

epsilon = 1e-06
MIB = 1 << 20


def column_inverse(values):
    squares = jnp.sum(values * values, axis=-1, keepdims=True)
    return lax.rsqrt(squares + epsilon)


def as_row(column):
    wide = jnp.broadcast_to(column, (column.shape[0], 128))
    return wide.T[0:1, :]


def position_of():
    owner = lax.axis_index("db")
    return lax.axis_index("pb"), owner // 2, owner % 2


def fetch_queries(queries_ref, held_ref, part, sem):
    rows = held_ref.shape[0]
    half = queries_ref.shape[0] // 2
    start = pl.multiple_of(position_of()[2] * half + part * rows, rows)
    return pltpu.make_async_copy(queries_ref.at[pl.ds(start, rows), :], held_ref, sem)


def count_kernel(
    planes, twin_ref, own_ref, database_ref, queries_ref, *rest
):
    count_refs = rest[:-6]
    copy_ref, held_ref, tiles_ref, lows_ref, sem, queries_sem = rest[-6:]
    rows = copy_ref.shape[0]
    fanout = own_ref.shape[0] * 128 // rows
    quarter = rows // 4
    span = (planes - 1) * quarter
    starts = [0]
    for count_ref in count_refs:
        starts.append(starts[-1] + count_ref.shape[1])
    copy = pltpu.make_async_copy(database_ref, copy_ref, sem)
    copy.start()
    queries = fetch_queries(queries_ref, held_ref, 0, queries_sem)
    queries.start()
    me, plane, core = position_of()
    bits = rows.bit_length() - 1
    lines = own_ref.shape[0]
    for number, wanted_ref in enumerate((twin_ref, own_ref)):
        wanted = wanted_ref[...]
        owner = wanted >> bits
        side = owner & 1
        row = wanted & (rows - 1)
        cross = (row >> (bits - 2)) ^ me
        inner = row & (quarter - 1)
        away = (owner >> 1) ^ plane
        straight = (away - 1) * quarter + inner
        half = away >> 1
        relayed = jnp.where(away & 1 == 1, planes // 2 - 1 + half, half - 1) * quarter + inner
        second = jnp.where(cross == 1 + core, 0, 1)
        first = span - quarter
        early = starts[1] + span + second * first + straight
        late = starts[2] + span + second * quarter + straight - first
        position = jnp.where(straight < first, early, late)
        position = jnp.where(cross == 3, starts[2] + relayed, position)
        position = jnp.where(cross == 0, starts[1] + straight, position)
        position = jnp.where(away == 0, row, position)
        position = jnp.where((wanted >= 0) & (side == core), position, -1)
        tiles_ref[number * lines : (number + 1) * lines, :] = position >> 7
        lows_ref[number * lines : (number + 1) * lines, :] = position & 127

    group = 16
    height = starts[-1] // 128 * group
    width = group * fanout
    at_row = lax.broadcasted_iota(jnp.int32, (height, width), 0)
    at_lane = lax.broadcasted_iota(jnp.int32, (height, width), 1)
    target = jnp.where(at_lane // fanout == at_row % group, at_row // group, -2)
    low_of = lax.broadcasted_iota(jnp.int32, (128, width), 0)
    each = width // 128

    def flat(ref, at):
        return jnp.concatenate([ref[pl.ds(at * each + i, 1), :] for i in range(each)], axis=1)

    def body(at, carry):
        tile = jnp.broadcast_to(flat(tiles_ref, at), (height, width))
        low = jnp.broadcast_to(flat(lows_ref, at), (128, width))
        left = jnp.where(tile == target, 1.0, 0.0).astype(jnp.bfloat16)
        right = jnp.where(low == low_of, 1.0, 0.0).astype(jnp.bfloat16)
        counts = lax.dot_general(
            left, right, (((1,), (1,)), ((), ())), preferred_element_type=jnp.float32
        ).astype(jnp.bfloat16)
        start = pl.ds(pl.multiple_of(at * group, group), group)
        tile = 0
        for count_ref in count_refs:
            for t in range(count_ref.shape[1] // 128):
                count_ref[start, t * 128 : (t + 1) * 128] = counts[tile * group : (tile + 1) * group, :]
                tile += 1
        return carry

    lax.fori_loop(0, 2 * rows // group, body, 0, unroll=4)
    copy.wait()
    queries.wait()


def join_kernel(last_ref, *rest):
    *pieces, _, forward_ref, across_ref = rest
    quarter = last_ref.shape[0]
    forward_ref[...] = last_ref[...]
    for i, ref in enumerate(pieces):
        across_ref[i * quarter : (i + 1) * quarter, :] = ref[...]


def spread_terms(dest, dest_inverse, block, far, counts):
    products = lax.dot_general(
        dest, block, (((1,), (1,)), ((), ())), preferred_element_type=jnp.float32
    )
    cosine = products * dest_inverse * far
    halfway = (1.0 + cosine) * 0.5
    weight = halfway * halfway * halfway
    coefficient = (weight * far).astype(jnp.bfloat16).astype(jnp.float32)
    spread = coefficient * counts.astype(jnp.float32)
    high = spread.astype(jnp.bfloat16)
    low = (spread - high.astype(jnp.float32)).astype(jnp.bfloat16)
    return jnp.dot(high, block, preferred_element_type=jnp.float32) + jnp.dot(
        low, block, preferred_element_type=jnp.float32
    )


def sums_kernel(blocks, twin_ref, own_ref, counts_ref, *rest):
    block_refs, rest = rest[:blocks], rest[blocks:]
    *before_ref, out_ref = rest
    rows = own_ref.shape[0]
    block = jnp.concatenate([ref[...] for ref in block_refs], axis=0) if blocks > 1 else block_refs[0][...]
    far = as_row(column_inverse(block.astype(jnp.float32)))
    for number, dest_ref in enumerate((twin_ref, own_ref)):
        lines = slice(number * rows, (number + 1) * rows)
        dest = dest_ref[...]
        values = dest.astype(jnp.float32)
        dest_inverse = column_inverse(values)
        terms = spread_terms(dest, dest_inverse, block, far, counts_ref[lines, : block.shape[0]])
        if before_ref:
            terms = before_ref[0][lines, :] + terms
        elif number == 1:
            terms = terms + values * dest_inverse
        out_ref[lines, :] = terms


def late_kernel(number, dest_ref, early_ref, counts_ref, *rest):
    out_ref = rest[-1]
    rows = dest_ref.shape[0]
    lines = slice(number * rows, (number + 1) * rows)
    block = jnp.concatenate([ref[...] for ref in rest[:-1]], axis=0)
    far = as_row(column_inverse(block.astype(jnp.float32)))
    dest = dest_ref[...]
    dest_inverse = column_inverse(dest.astype(jnp.float32))
    terms = spread_terms(dest, dest_inverse, block, far, counts_ref[lines, : block.shape[0]])
    out_ref[...] = early_ref[lines, :] + terms


def score_kernel(own_a_ref, own_b_ref, twin_a_ref, twin_b_ref, first_ref, queries_ref, augmented_ref, best_ref, rows_ref, held_ref, sems):
    rows = own_a_ref.shape[0]
    size = held_ref.shape[0] // sems.shape[0]
    fetched = lambda i: held_ref.at[pl.ds(i * size, size), :]
    ahead = first_ref.shape[0] // size
    fetches = [
        fetch_queries(queries_ref, fetched(i), ahead + i, sems.at[i]) for i in range(sems.shape[0])
    ]
    for fetch in fetches:
        fetch.start()
    for number, (a_ref, b_ref) in enumerate(((own_a_ref, own_b_ref), (twin_a_ref, twin_b_ref))):
        summed = a_ref[...] + b_ref[...]
        augmented = (summed * column_inverse(summed)).astype(jnp.bfloat16)
        if number == 0:
            augmented_ref[...] = augmented
        rows_ref[number * rows : (number + 1) * rows, :] = augmented

    line_of = 0
    for part in range(1 + sems.shape[0]):
        if part == 0:
            block_ref = first_ref
        else:
            fetches[part - 1].wait()
            block_ref = fetched(part - 1)
        height = block_ref.shape[0]
        step = min(1024, height)
        tile = min(2048, height)
        before = line_of
        line_of += height // 128

        @pl.loop(0, height // tile)
        def _(i):
            at = pl.multiple_of(i * tile, tile)
            line = pl.multiple_of(before + i * (tile // 128), tile // 128)
            found = []
            for first in range(0, tile, step):
                scores = lax.dot_general(
                    rows_ref[...],
                    block_ref[pl.ds(at + first, step), :],
                    (((1,), (1,)), ((), ())),
                    preferred_element_type=jnp.float32,
                )
                best = jnp.max(scores, axis=0, keepdims=True)
                found += [best[:, part : part + 128] for part in range(0, step, 128)]
            best_ref[pl.ds(line, tile // 128), :] = jnp.concatenate(found, axis=0)


def local(database, neighbours, valid_count, queries):
    rows, features = database.shape
    fanout = neighbours.shape[1]
    count = queries.shape[0]
    owners = lax.axis_size("db")
    panels = lax.axis_size("pb")
    assert panels == 4 and owners % 4 == 0 and owners & (owners - 1) == 0
    planes = owners // 2
    quarter = rows // panels
    me = lax.axis_index("pb")
    core = lax.axis_index("db") % 2

    def along(value, apart):
        pairs = [(i, ((i // 2) ^ apart) * 2 + i % 2) for i in range(owners)]
        return lax.ppermute(value, "db", pairs)

    def along_all(value, smallest):
        pieces = {0: value}
        apart = planes // 2
        while apart >= smallest:
            for other in sorted(pieces):
                pieces[other ^ apart] = along(pieces[other], apart)
            apart //= 2
        return [pieces[apart] for apart in sorted(pieces)]

    def swap(value):
        return lax.ppermute(value, "db", [(i, i ^ 1) for i in range(owners)])

    def cross(value, bits):
        pairs = []
        for panel in range(panels):
            for i in range(owners):
                pairs.append((panel * owners + i, (panel ^ bits[i % 2]) * owners + i))
        return lax.ppermute(value, ("pb", "db"), pairs)

    mine = lax.dynamic_slice_in_dim(database, me * quarter, quarter, 0)
    other = lax.dynamic_slice_in_dim(database, (me ^ 3) * quarter, quarter, 0)
    near = along_all(mine, 1)[1:]
    across = along_all(other, 2)
    ahead = jnp.concatenate(near[:-1], axis=0)
    beside = cross(ahead, (1, 2))
    behind = cross(ahead, (2, 1))
    twin = swap(database)
    vmem = pl.BlockSpec(memory_space=pltpu.VMEM)
    slots = jnp.arange(fanout, dtype=jnp.int32)[None, :]
    wanted = jnp.where(slots < valid_count[:, None], neighbours, -1).reshape(-1, 128)
    twin_wanted = swap(wanted)
    padded = lambda size: (size + 127) // 128 * 128
    span = (planes - 1) * quarter
    widths = (rows, 3 * span - 2 * quarter, span + 2 * quarter)
    *counts, own, first_queries = pl.pallas_call(
        functools.partial(count_kernel, planes),
        out_shape=[
            jax.ShapeDtypeStruct((2 * rows, padded(width)), jnp.bfloat16) for width in widths
        ]
        + [
            jax.ShapeDtypeStruct((rows, features), jnp.bfloat16),
            jax.ShapeDtypeStruct((count // 4, features), jnp.bfloat16),
        ],
        in_specs=[vmem, vmem] + [pl.BlockSpec(memory_space=pltpu.HBM)] * 2,
        out_specs=[vmem] * 5,
        scratch_shapes=[
            pltpu.VMEM((2 * wanted.shape[0], 128), jnp.int32),
            pltpu.VMEM((2 * wanted.shape[0], 128), jnp.int32),
            pltpu.SemaphoreType.DMA(()),
            pltpu.SemaphoreType.DMA(()),
        ],
        compiler_params=pltpu.CompilerParams(vmem_limit_bytes=30 * MIB),
        cost_estimate=pl.CostEstimate(flops=1<<29, bytes_accessed=4 * rows * rows, transcendentals=0),
        name="counts",
    )(twin_wanted, wanted, database, queries)
    def sums(name, counts, blocks, flops, before=None):
        out = [jax.ShapeDtypeStruct((2 * rows, features), jnp.float32)]
        operands = [twin, own, counts, *blocks]
        specs = [vmem] * len(operands)
        if before is not None:
            operands.append(before)
            specs.append(vmem)
        return pl.pallas_call(
            functools.partial(sums_kernel, len(blocks)),
            out_shape=out,
            in_specs=specs,
            out_specs=[vmem] * len(out),
            compiler_params=pltpu.CompilerParams(vmem_limit_bytes=30 * MIB),
            cost_estimate=pl.CostEstimate(flops=flops, bytes_accessed=4 * rows * rows, transcendentals=0),
            name=name,
        )(*operands)

    (total,) = sums("own_sums", counts[0], [own], 1<<29)
    forward, message = pl.pallas_call(
        join_kernel,
        out_shape=[
            jax.ShapeDtypeStruct((quarter, features), jnp.bfloat16),
            jax.ShapeDtypeStruct((planes // 2 * quarter, features), jnp.bfloat16),
        ],
        in_specs=[vmem] * (2 + planes // 2),
        out_specs=[vmem] * 2,
        compiler_params=pltpu.CompilerParams(vmem_limit_bytes=8 * MIB),
        name="join",
    )(near[-1], *across, total)
    across = across[1:] + [along(message, 1)]
    beside_last = cross(forward, (1, 2))
    behind_last = cross(forward, (2, 1))

    (total,) = sums("near_sums", counts[1], [*near, beside, behind], 1<<26, total)

    def late(number, dest):
        return pl.pallas_call(
            functools.partial(late_kernel, number),
            out_shape=jax.ShapeDtypeStruct((rows, features), jnp.float32),
            in_specs=[vmem] * (5 + len(across)),
            out_specs=vmem,
            compiler_params=pltpu.CompilerParams(vmem_limit_bytes=30 * MIB),
            name="late_sums",
        )(dest, total, counts[2], *across, beside_last, behind_last)

    twin_a = late(0, twin)
    own_b = swap(twin_a)
    own_a = late(1, own)
    twin_b = swap(own_a)

    half = count // 2
    augmented, best = pl.pallas_call(
        score_kernel,
        out_shape=[
            jax.ShapeDtypeStruct((rows, features), jnp.bfloat16),
            jax.ShapeDtypeStruct((half // 128, 128), jnp.float32),
        ],
        in_specs=[vmem] * 5 + [pl.BlockSpec(memory_space=pltpu.HBM)],
        out_specs=[vmem, vmem],
        scratch_shapes=[
            pltpu.VMEM((2 * rows, features), jnp.bfloat16),
            pltpu.VMEM((count // 4, features), jnp.bfloat16),
            pltpu.SemaphoreType.DMA((2,)),
        ],
        compiler_params=pltpu.CompilerParams(vmem_limit_bytes=40 * MIB),
        cost_estimate=pl.CostEstimate(
            flops=2 * count * rows * features, bytes_accessed=count * features, transcendentals=0
        ),
        name="scores",
    )(own_a, own_b, twin_a, twin_b, first_queries, queries)

    received = [along(best, apart) for apart in range(planes - 1, 0, -1)]
    for value in received:
        best = jnp.maximum(best, value)
    other_half = swap(best)
    first = jnp.where(core == 0, best, other_half)
    second = jnp.where(core == 0, other_half, best)
    return augmented, jnp.concatenate([first, second], axis=0).reshape(count)


def solution(mesh):
    return jax.shard_map(
        local,
        mesh=mesh,
        in_specs=(P("db", None), P("db", None), P("db"), P("pb", None)),
        out_specs=(P("db", None), P("pb")),
        check_vma=False,
    )
```

```python
import functools

import jax
import jax.numpy as jnp
from jax import lax
from jax.experimental import pallas as pl
from jax.experimental.pallas import tpu as pltpu
from jax.sharding import PartitionSpec as P

epsilon = 1e-06
MIB = 1 << 20


def column_inverse(values):
    squares = jnp.sum(values * values, axis=-1, keepdims=True)
    return lax.rsqrt(squares + epsilon)


def as_row(column):
    wide = jnp.broadcast_to(column, (column.shape[0], 128))
    return wide.T[0:1, :]


def position_of():
    owner = lax.axis_index("db")
    return lax.axis_index("pb"), owner // 2, owner % 2


def fetch_queries(queries_ref, held_ref, part, sem):
    rows = held_ref.shape[0]
    half = queries_ref.shape[0] // 2
    start = pl.multiple_of(position_of()[2] * half + part * rows, rows)
    return pltpu.make_async_copy(queries_ref.at[pl.ds(start, rows), :], held_ref, sem)


def count_kernel(
    planes, twin_ref, own_ref, database_ref, queries_ref, *rest
):
    count_refs = rest[:-6]
    copy_ref, held_ref, tiles_ref, lows_ref, sem, queries_sem = rest[-6:]
    rows = copy_ref.shape[0]
    fanout = own_ref.shape[0] * 128 // rows
    quarter = rows // 4
    span = (planes - 1) * quarter
    starts = [0]
    for count_ref in count_refs:
        starts.append(starts[-1] + count_ref.shape[1])
    copy = pltpu.make_async_copy(database_ref, copy_ref, sem)
    copy.start()
    queries = fetch_queries(queries_ref, held_ref, 0, queries_sem)
    queries.start()
    me, plane, core = position_of()
    bits = rows.bit_length() - 1
    lines = own_ref.shape[0]
    for number, wanted_ref in enumerate((twin_ref, own_ref)):
        wanted = wanted_ref[...]
        owner = wanted >> bits
        side = owner & 1
        row = wanted & (rows - 1)
        cross = (row >> (bits - 2)) ^ me
        inner = row & (quarter - 1)
        away = (owner >> 1) ^ plane
        straight = (away - 1) * quarter + inner
        half = away >> 1
        relayed = jnp.where(away & 1 == 1, planes // 2 - 1 + half, half - 1) * quarter + inner
        second = jnp.where(cross == 1 + core, 0, 1)
        first = span - quarter
        early = starts[1] + span + second * first + straight
        late = starts[2] + span + second * quarter + straight - first
        position = jnp.where(straight < first, early, late)
        position = jnp.where(cross == 3, starts[2] + relayed, position)
        position = jnp.where(cross == 0, starts[1] + straight, position)
        position = jnp.where(away == 0, row, position)
        position = jnp.where((wanted >= 0) & (side == core), position, -1)
        tiles_ref[number * lines : (number + 1) * lines, :] = position >> 7
        lows_ref[number * lines : (number + 1) * lines, :] = position & 127

    group = 16
    height = starts[-1] // 128 * group
    width = group * fanout
    at_row = lax.broadcasted_iota(jnp.int32, (height, width), 0)
    at_lane = lax.broadcasted_iota(jnp.int32, (height, width), 1)
    target = jnp.where(at_lane // fanout == at_row % group, at_row // group, -2)
    low_of = lax.broadcasted_iota(jnp.int32, (128, width), 0)
    each = width // 128

    def flat(ref, at):
        return jnp.concatenate([ref[pl.ds(at * each + i, 1), :] for i in range(each)], axis=1)

    def body(at, carry):
        tile = jnp.broadcast_to(flat(tiles_ref, at), (height, width))
        low = jnp.broadcast_to(flat(lows_ref, at), (128, width))
        left = jnp.where(tile == target, 1.0, 0.0).astype(jnp.bfloat16)
        right = jnp.where(low == low_of, 1.0, 0.0).astype(jnp.bfloat16)
        counts = lax.dot_general(
            left, right, (((1,), (1,)), ((), ())), preferred_element_type=jnp.float32
        ).astype(jnp.bfloat16)
        start = pl.ds(pl.multiple_of(at * group, group), group)
        tile = 0
        for count_ref in count_refs:
            for t in range(count_ref.shape[1] // 128):
                count_ref[start, t * 128 : (t + 1) * 128] = counts[tile * group : (tile + 1) * group, :]
                tile += 1
        return carry

    lax.fori_loop(0, 2 * rows // group, body, 0, unroll=4)
    copy.wait()
    queries.wait()


def join_kernel(last_ref, *rest):
    *pieces, _, forward_ref, across_ref = rest
    quarter = last_ref.shape[0]
    forward_ref[...] = last_ref[...]
    for i, ref in enumerate(pieces):
        across_ref[i * quarter : (i + 1) * quarter, :] = ref[...]


def spread_terms(dest, dest_inverse, block, far, counts):
    products = lax.dot_general(
        dest, block, (((1,), (1,)), ((), ())), preferred_element_type=jnp.float32
    )
    cosine = products * dest_inverse * far
    halfway = (1.0 + cosine) * 0.5
    weight = halfway * halfway * halfway
    coefficient = (weight * far).astype(jnp.bfloat16).astype(jnp.float32)
    spread = coefficient * counts.astype(jnp.float32)
    high = spread.astype(jnp.bfloat16)
    low = (spread - high.astype(jnp.float32)).astype(jnp.bfloat16)
    return jnp.dot(high, block, preferred_element_type=jnp.float32) + jnp.dot(
        low, block, preferred_element_type=jnp.float32
    )


def sums_kernel(blocks, twin_ref, own_ref, counts_ref, *rest):
    block_refs, rest = rest[:blocks], rest[blocks:]
    *before_ref, out_ref = rest
    rows = own_ref.shape[0]
    block = jnp.concatenate([ref[...] for ref in block_refs], axis=0) if blocks > 1 else block_refs[0][...]
    far = as_row(column_inverse(block.astype(jnp.float32)))
    for number, dest_ref in enumerate((twin_ref, own_ref)):
        lines = slice(number * rows, (number + 1) * rows)
        dest = dest_ref[...]
        values = dest.astype(jnp.float32)
        dest_inverse = column_inverse(values)
        terms = spread_terms(dest, dest_inverse, block, far, counts_ref[lines, : block.shape[0]])
        if before_ref:
            terms = before_ref[0][lines, :] + terms
        elif number == 1:
            terms = terms + values * dest_inverse
        out_ref[lines, :] = terms


def late_kernel(number, dest_ref, early_ref, counts_ref, *rest):
    out_ref = rest[-1]
    rows = dest_ref.shape[0]
    lines = slice(number * rows, (number + 1) * rows)
    block = jnp.concatenate([ref[...] for ref in rest[:-1]], axis=0)
    far = as_row(column_inverse(block.astype(jnp.float32)))
    dest = dest_ref[...]
    dest_inverse = column_inverse(dest.astype(jnp.float32))
    terms = spread_terms(dest, dest_inverse, block, far, counts_ref[lines, : block.shape[0]])
    out_ref[...] = early_ref[lines, :] + terms


def score_kernel(own_a_ref, own_b_ref, twin_a_ref, twin_b_ref, first_ref, queries_ref, augmented_ref, best_ref, rows_ref, held_ref, sems):
    rows = own_a_ref.shape[0]
    size = held_ref.shape[0] // sems.shape[0]
    fetched = lambda i: held_ref.at[pl.ds(i * size, size), :]
    ahead = first_ref.shape[0] // size
    fetches = [
        fetch_queries(queries_ref, fetched(i), ahead + i, sems.at[i]) for i in range(sems.shape[0])
    ]
    for fetch in fetches:
        fetch.start()
    for number, (a_ref, b_ref) in enumerate(((own_a_ref, own_b_ref), (twin_a_ref, twin_b_ref))):
        summed = a_ref[...] + b_ref[...]
        augmented = (summed * column_inverse(summed)).astype(jnp.bfloat16)
        if number == 0:
            augmented_ref[...] = augmented
        rows_ref[number * rows : (number + 1) * rows, :] = augmented

    line_of = 0
    for part in range(1 + sems.shape[0]):
        if part == 0:
            block_ref = first_ref
        else:
            fetches[part - 1].wait()
            block_ref = fetched(part - 1)
        height = block_ref.shape[0]
        step = min(1024, height)
        tile = min(4096, height)
        before = line_of
        line_of += height // 128

        @pl.loop(0, height // tile)
        def _(i):
            at = pl.multiple_of(i * tile, tile)
            line = pl.multiple_of(before + i * (tile // 128), tile // 128)
            found = []
            for first in range(0, tile, step):
                scores = lax.dot_general(
                    rows_ref[...],
                    block_ref[pl.ds(at + first, step), :],
                    (((1,), (1,)), ((), ())),
                    preferred_element_type=jnp.float32,
                )
                best = jnp.max(scores, axis=0, keepdims=True)
                found += [best[:, part : part + 128] for part in range(0, step, 128)]
            best_ref[pl.ds(line, tile // 128), :] = jnp.concatenate(found, axis=0)


def local(database, neighbours, valid_count, queries):
    rows, features = database.shape
    fanout = neighbours.shape[1]
    count = queries.shape[0]
    owners = lax.axis_size("db")
    panels = lax.axis_size("pb")
    assert panels == 4 and owners % 4 == 0 and owners & (owners - 1) == 0
    planes = owners // 2
    quarter = rows // panels
    me = lax.axis_index("pb")
    core = lax.axis_index("db") % 2

    def along(value, apart):
        pairs = [(i, ((i // 2) ^ apart) * 2 + i % 2) for i in range(owners)]
        return lax.ppermute(value, "db", pairs)

    def along_all(value, smallest):
        pieces = {0: value}
        apart = planes // 2
        while apart >= smallest:
            for other in sorted(pieces):
                pieces[other ^ apart] = along(pieces[other], apart)
            apart //= 2
        return [pieces[apart] for apart in sorted(pieces)]

    def swap(value):
        return lax.ppermute(value, "db", [(i, i ^ 1) for i in range(owners)])

    def cross(value, bits):
        pairs = []
        for panel in range(panels):
            for i in range(owners):
                pairs.append((panel * owners + i, (panel ^ bits[i % 2]) * owners + i))
        return lax.ppermute(value, ("pb", "db"), pairs)

    mine = lax.dynamic_slice_in_dim(database, me * quarter, quarter, 0)
    other = lax.dynamic_slice_in_dim(database, (me ^ 3) * quarter, quarter, 0)
    near = along_all(mine, 1)[1:]
    across = along_all(other, 2)
    ahead = jnp.concatenate(near[:-1], axis=0)
    beside = cross(ahead, (1, 2))
    behind = cross(ahead, (2, 1))
    twin = swap(database)
    vmem = pl.BlockSpec(memory_space=pltpu.VMEM)
    slots = jnp.arange(fanout, dtype=jnp.int32)[None, :]
    wanted = jnp.where(slots < valid_count[:, None], neighbours, -1).reshape(-1, 128)
    twin_wanted = swap(wanted)
    padded = lambda size: (size + 127) // 128 * 128
    span = (planes - 1) * quarter
    widths = (rows, 3 * span - 2 * quarter, span + 2 * quarter)
    *counts, own, first_queries = pl.pallas_call(
        functools.partial(count_kernel, planes),
        out_shape=[
            jax.ShapeDtypeStruct((2 * rows, padded(width)), jnp.bfloat16) for width in widths
        ]
        + [
            jax.ShapeDtypeStruct((rows, features), jnp.bfloat16),
            jax.ShapeDtypeStruct((count // 4, features), jnp.bfloat16),
        ],
        in_specs=[vmem, vmem] + [pl.BlockSpec(memory_space=pltpu.HBM)] * 2,
        out_specs=[vmem] * 5,
        scratch_shapes=[
            pltpu.VMEM((2 * wanted.shape[0], 128), jnp.int32),
            pltpu.VMEM((2 * wanted.shape[0], 128), jnp.int32),
            pltpu.SemaphoreType.DMA(()),
            pltpu.SemaphoreType.DMA(()),
        ],
        compiler_params=pltpu.CompilerParams(vmem_limit_bytes=30 * MIB),
        cost_estimate=pl.CostEstimate(flops=1<<29, bytes_accessed=4 * rows * rows, transcendentals=0),
        name="counts",
    )(twin_wanted, wanted, database, queries)
    def sums(name, counts, blocks, flops, before=None):
        out = [jax.ShapeDtypeStruct((2 * rows, features), jnp.float32)]
        operands = [twin, own, counts, *blocks]
        specs = [vmem] * len(operands)
        if before is not None:
            operands.append(before)
            specs.append(vmem)
        return pl.pallas_call(
            functools.partial(sums_kernel, len(blocks)),
            out_shape=out,
            in_specs=specs,
            out_specs=[vmem] * len(out),
            compiler_params=pltpu.CompilerParams(vmem_limit_bytes=30 * MIB),
            cost_estimate=pl.CostEstimate(flops=flops, bytes_accessed=4 * rows * rows, transcendentals=0),
            name=name,
        )(*operands)

    (total,) = sums("own_sums", counts[0], [own], 1<<29)
    forward, message = pl.pallas_call(
        join_kernel,
        out_shape=[
            jax.ShapeDtypeStruct((quarter, features), jnp.bfloat16),
            jax.ShapeDtypeStruct((planes // 2 * quarter, features), jnp.bfloat16),
        ],
        in_specs=[vmem] * (2 + planes // 2),
        out_specs=[vmem] * 2,
        compiler_params=pltpu.CompilerParams(vmem_limit_bytes=8 * MIB),
        name="join",
    )(near[-1], *across, total)
    across = across[1:] + [along(message, 1)]
    beside_last = cross(forward, (1, 2))
    behind_last = cross(forward, (2, 1))

    (total,) = sums("near_sums", counts[1], [*near, beside, behind], 1<<26, total)

    def late(number, dest):
        return pl.pallas_call(
            functools.partial(late_kernel, number),
            out_shape=jax.ShapeDtypeStruct((rows, features), jnp.float32),
            in_specs=[vmem] * (5 + len(across)),
            out_specs=vmem,
            compiler_params=pltpu.CompilerParams(vmem_limit_bytes=30 * MIB),
            name="late_sums",
        )(dest, total, counts[2], *across, beside_last, behind_last)

    twin_a = late(0, twin)
    own_b = swap(twin_a)
    own_a = late(1, own)
    twin_b = swap(own_a)

    half = count // 2
    augmented, best = pl.pallas_call(
        score_kernel,
        out_shape=[
            jax.ShapeDtypeStruct((rows, features), jnp.bfloat16),
            jax.ShapeDtypeStruct((half // 128, 128), jnp.float32),
        ],
        in_specs=[vmem] * 5 + [pl.BlockSpec(memory_space=pltpu.HBM)],
        out_specs=[vmem, vmem],
        scratch_shapes=[
            pltpu.VMEM((2 * rows, features), jnp.bfloat16),
            pltpu.VMEM((count // 4, features), jnp.bfloat16),
            pltpu.SemaphoreType.DMA((2,)),
        ],
        compiler_params=pltpu.CompilerParams(vmem_limit_bytes=40 * MIB),
        cost_estimate=pl.CostEstimate(
            flops=2 * count * rows * features, bytes_accessed=count * features, transcendentals=0
        ),
        name="scores",
    )(own_a, own_b, twin_a, twin_b, first_queries, queries)

    received = [along(best, apart) for apart in range(planes - 1, 0, -1)]
    for value in received:
        best = jnp.maximum(best, value)
    other_half = swap(best)
    first = jnp.where(core == 0, best, other_half)
    second = jnp.where(core == 0, other_half, best)
    return augmented, jnp.concatenate([first, second], axis=0).reshape(count)


def solution(mesh):
    return jax.shard_map(
        local,
        mesh=mesh,
        in_specs=(P("db", None), P("db", None), P("db"), P("pb", None)),
        out_specs=(P("db", None), P("pb")),
        check_vma=False,
    )
```
